32 devices in a mesh: batch: 4 (over x, core), gene: 8 (over z, y).
Axes of the slice: x: 2, y: 2, z: 4, core: 2. Of those that a mesh axis runs over, the one named last changes fastest.
Arguments:
- counts_in: float32 [7168, 8192], P('gene', 'batch'), may hold values from 0 to 6
- umi_total: int32 [8192], P('batch'), may hold values from 2500 to 39999
- gene_mask: int32 [7168], P('gene'), may hold values 0 or 1
- noise: float32 [100, 8192], P(None, 'batch'), may hold values from -6 to 6
- w_enc: float32 [7168, 800], P('gene'), may hold values from -0.0625 to 0.0625
- gain_enc: float32 [800], P('gene'), may hold values from 0.25 to 1.75
- shift_enc: float32 [800], P('gene'), may hold values from -3 to 3
- w_lat: float32 [200, 800], replicated, may hold values from -0.21875 to 0.21875
- b_lat: float32 [200], replicated, may hold values from -2 to 2
- w_dec: float32 [100, 800], replicated, may hold values from -0.625 to 0.625
- gain_dec: float32 [800], replicated, may hold values from 0.25 to 1.75
- shift_dec: float32 [800], replicated, may hold values from -3 to 3
- w_out: float32 [7168, 800], P('gene'), may hold values from -0.21875 to 0.21875
- b_out: float32 [7168], P('gene'), may hold values from -3 to 3
- mean_enc: float32 [800], P('gene'), may hold values from -3 to 3
- var_enc: float32 [800], P('gene'), may hold values from 0.5 to 2
- mean_dec: float32 [800], replicated, may hold values from -3 to 3
- var_dec: float32 [800], replicated, may hold values from 0.5 to 2
Outputs:
- recon: float32 [7168, 8192], P('gene', 'batch')
- grad_counts: float32 [7168, 8192], P('gene', 'batch')
- grad_w_enc: float32 [7168, 800], P('gene')
- grad_gain_enc: float32 [800], P('gene')
- grad_shift_enc: float32 [800], P('gene')
- grad_w_lat: float32 [200, 800], P(None, 'gene')
- grad_b_lat: float32 [200], replicated
- grad_w_dec: float32 [100, 800], P(None, 'gene')
- grad_gain_dec: float32 [800], P('gene')
- grad_shift_dec: float32 [800], P('gene')
- grad_w_out: float32 [7168, 800], P('gene')
- grad_b_out: float32 [7168], P('gene')
- new_mean_enc: float32 [800], P('gene')
- new_var_enc: float32 [800], P('gene')
- new_mean_dec: float32 [800], replicated
- new_var_dec: float32 [800], replicated
The draws below stay inside these ranges and needn't reach their ends.
All inputs are finite; a program needn't handle non-finite values. No bound on the sum of `gene_mask` on one device may be relied on, other than what follows from the above.
Results may differ from the reference program's by a relative error of at most 0.00023.
Values sent between devices are 32-bit elements; how exact they have to be, the bound alone decides.
No kernel may reach another device: no remote copies, remote signals or barrier semaphores. Data moves between devices by JAX's collectives and lax.ppermute only.
A program may use at most 128 MiB of HBM per device.

```python
import math
import jax
import jax.numpy as jnp
from jax import lax

GENES = 7168
HIDDEN_SIZE = 800
LATENT = 100
CELLS = 8192


def draw_counts_in(key, part):
    key_level, key_value, key_keep = jax.random.split(key, 3)
    gene_level = jnp.exp(jax.random.uniform(key_level, (GENES, 1), jnp.float32, math.log(0.5), math.log(3.0)))
    kept_mask = jax.random.uniform(key_keep, (GENES, CELLS), jnp.float32) < 0.75
    spread = jnp.exp(0.6 * jax.random.normal(key_value, (GENES, CELLS), jnp.float32) - 0.18)
    values = jnp.clip(gene_level * spread / 0.75, 0.0, 6.0)
    return jnp.where(kept_mask, values, 0.0).astype(jnp.float32)


def with_ends(drawn, own_key, smallest, largest):
    longest = drawn.shape.index(max(drawn.shape))
    spots = []
    for shift in (0, 1):
        where = [jax.random.randint(jax.random.fold_in(own_key, axis), (), 0, length) for axis, length in enumerate(drawn.shape)]
        where[longest] = (where[longest] + shift) % drawn.shape[longest]
        spots.append(tuple(where))
    return drawn.at[spots[0]].set(smallest).at[spots[1]].set(largest)


def levels(key, dims, pieces, low, high):
    loudness = 1.0
    for axis_at, parts in pieces:
        draws = jax.random.uniform(jax.random.fold_in(jax.random.fold_in(key, 6), axis_at), (parts,), jnp.float32, low / len(pieces), high / len(pieces))
        loudness = loudness * jnp.repeat(jnp.exp(draws), dims[axis_at] // parts).reshape((-1,) + (1,) * (len(dims) - 1 - axis_at))
    return loudness


def scatter_about(key, shape, deviation, reach, cuts=(), dtype=jnp.bfloat16):
    level = levels(key, shape, cuts, -0.22, 0.18) if cuts else 1.0
    array = jax.random.normal(key, shape, jnp.float32) * deviation * level
    return jnp.minimum(jnp.maximum(array, -reach), reach).astype(dtype)


def setup_inputs(seed: int = 0) -> dict:
    key_list = jax.random.split(jax.random.key(seed), 19)
    return {
        "counts_in": draw_counts_in(jax.random.fold_in(key_list[18], 71), 0),
        "umi_total": with_ends(jax.random.randint(key_list[1], (CELLS,), 2500, 40000), jax.random.fold_in(key_list[1], 1), 2500, 39999).astype(jnp.int32),
        "gene_mask": with_ends((jax.random.randint(key_list[2], (GENES,), 0, 8) < 7).astype(jnp.int32), jax.random.fold_in(key_list[2], 1), 0, 1),
        "noise": scatter_about(key_list[3], (LATENT, CELLS), 1.0, 6.0, ((1, 4),), jnp.float32),
        "w_enc": scatter_about(key_list[4], (GENES, HIDDEN_SIZE), GENES ** -0.5, 0.0625, ((0, 8),), jnp.float32),
        "gain_enc": jnp.clip(1.0 + 0.15 * jax.random.normal(key_list[5], (HIDDEN_SIZE,), jnp.float32), 0.25, 1.75),
        "shift_enc": scatter_about(key_list[6], (HIDDEN_SIZE,), 0.5, 3.0, ((0, 8),), jnp.float32),
        "w_lat": scatter_about(key_list[7], (2 * LATENT, HIDDEN_SIZE), HIDDEN_SIZE ** -0.5, 0.21875, (), jnp.float32),
        "b_lat": scatter_about(key_list[8], (2 * LATENT,), 0.3, 2.0, (), jnp.float32),
        "w_dec": scatter_about(key_list[9], (LATENT, HIDDEN_SIZE), LATENT ** -0.5, 0.625, (), jnp.float32),
        "gain_dec": jnp.clip(1.0 + 0.15 * jax.random.normal(key_list[10], (HIDDEN_SIZE,), jnp.float32), 0.25, 1.75),
        "shift_dec": scatter_about(key_list[11], (HIDDEN_SIZE,), 0.5, 3.0, (), jnp.float32),
        "w_out": scatter_about(key_list[12], (GENES, HIDDEN_SIZE), HIDDEN_SIZE ** -0.5, 0.21875, ((0, 8),), jnp.float32),
        "b_out": scatter_about(key_list[13], (GENES,), 0.5, 3.0, ((0, 8),), jnp.float32),
        "mean_enc": scatter_about(key_list[14], (HIDDEN_SIZE,), 0.5, 3.0, ((0, 8),), jnp.float32),
        "var_enc": jnp.clip(jnp.exp(math.log(2.0) - 1.3862944 * jax.random.uniform(key_list[15], (HIDDEN_SIZE,), jnp.float32) ** levels(key_list[15], (HIDDEN_SIZE,), ((0, 8),), -0.2, 0.2)), 0.5, 2.0),
        "mean_dec": scatter_about(key_list[16], (HIDDEN_SIZE,), 0.5, 3.0, (), jnp.float32),
        "var_dec": jnp.clip(jnp.exp(jax.random.uniform(key_list[17], (HIDDEN_SIZE,), jnp.float32, math.log(0.5), math.log(2.0))), 0.5, 2.0),
    }


ALPHA = 0.002
BN_EPS = 1e-05
MOMENTUM = 0.1
UMI_SCALE = 10000.0

def matmul(left, right):
    return jnp.dot(left, right, precision=lax.Precision.HIGHEST, preferred_element_type=jnp.float32)

def batch_norm(values, gain, shift):
    mean = lax.optimization_barrier(jnp.mean(values, axis=0))
    centered = values - mean
    var = lax.optimization_barrier(jnp.mean(centered * centered, axis=0))
    return (centered * lax.rsqrt(var + BN_EPS) * gain + shift, mean, var)

def reference(counts_in, umi_total, gene_mask, noise, w_enc, gain_enc, shift_enc, w_lat, b_lat, w_dec, gain_dec, shift_dec, w_out, b_out, mean_enc, var_enc, mean_dec, var_dec):
    factor = UMI_SCALE / umi_total.astype(jnp.float32)
    maskf = gene_mask.astype(jnp.float32)
    cells = counts_in.shape[1]
    latent = noise.shape[0]
    noise_rows = noise.T

    def forward(counts, w_enc, gain_enc, shift_enc, w_lat, b_lat, w_dec, gain_dec, shift_dec, w_out, b_out):
        scaled = counts.T * factor[:, None] * maskf[None, :]
        in1, mean1, var1 = batch_norm(matmul(scaled, w_enc), gain_enc, shift_enc)
        act1 = jax.nn.silu(in1)
        lat = matmul(act1, w_lat.T) + b_lat
        mu = lat[:, :latent]
        logvar = lat[:, latent:]
        z = mu + jnp.exp(0.5 * logvar) * noise_rows
        in2, mean2, var2 = batch_norm(matmul(z, w_dec), gain_dec, shift_dec)
        act2 = jax.nn.silu(in2)
        recon = jax.nn.softplus(matmul(act2, w_out.T) + b_out)
        diff = recon - scaled
        kl = -0.5 * lax.optimization_barrier(jnp.sum(1.0 + logvar - mu * mu - jnp.exp(logvar), axis=1))
        loss = (0.5 * jnp.sum(maskf[None, :] * diff * diff) + ALPHA * jnp.sum(kl)) / cells
        return (loss, (recon.T, mean1, var1, mean2, var2))
    loss, pull, aux = jax.vjp(forward, counts_in, w_enc, gain_enc, shift_enc, w_lat, b_lat, w_dec, gain_dec, shift_dec, w_out, b_out, has_aux=True)
    grads = pull(jnp.ones_like(loss))
    recon, mean1, var1, mean2, var2 = aux
    correct = cells / (cells - 1.0)
    new_mean_enc = (1.0 - MOMENTUM) * mean_enc + MOMENTUM * mean1
    new_var_enc = (1.0 - MOMENTUM) * var_enc + MOMENTUM * var1 * correct
    new_mean_dec = (1.0 - MOMENTUM) * mean_dec + MOMENTUM * mean2
    new_var_dec = (1.0 - MOMENTUM) * var_dec + MOMENTUM * var2 * correct
    return (recon, grads[0], grads[1], grads[2], grads[3], grads[4], grads[5], grads[6], grads[7], grads[8], grads[9], grads[10], new_mean_enc, new_var_enc, new_mean_dec, new_var_dec)
```

```python
import jax
import jax.numpy as jnp
from jax import lax
from jax.experimental import pallas as pl
from jax.experimental.pallas import tpu as pltpu
from jax.sharding import PartitionSpec as P

ALPHA = 0.002
BN_EPS = 1e-05
MOMENTUM = 0.1
UMI_SCALE = 10000.0
BATCH = "batch"
GENE = "gene"
TILE = 256
VMEM_BYTES = 56 << 20
F32 = jnp.float32


BF16 = jnp.bfloat16
RATE = 1_100_000_000


def split(value):
    high = value.astype(BF16)
    return high, (value - high.astype(F32)).astype(BF16)


def whole(pair):
    return pair[0].astype(F32) + pair[1].astype(F32)


def dot(left, right, left_dim, right_dim):
    def one(a, b):
        return lax.dot_general(
            a,
            b,
            (((left_dim,), (right_dim,)), ((), ())),
            preferred_element_type=F32,
        )

    return one(left[0], right[0]) + (one(left[0], right[1]) + one(left[1], right[0]))


def kernel_call(
    body, grid, in_specs, out_specs, out_shape, micros, order=None, scratch=(), after=()
):
    leading = 0 if order is None else 1
    held = leading + len(in_specs)

    def run(*refs):
        body(*refs[:held], *refs[held + len(after) :])

    call = pl.pallas_call(
        run,
        grid_spec=pltpu.PrefetchScalarGridSpec(
            num_scalar_prefetch=leading,
            grid=grid,
            in_specs=list(in_specs) + [pl.BlockSpec(memory_space=pl.ANY)] * len(after),
            out_specs=out_specs,
            scratch_shapes=list(scratch),
        ),
        out_shape=out_shape,
        compiler_params=pltpu.CompilerParams(vmem_limit_bytes=VMEM_BYTES),
        cost_estimate=pl.CostEstimate(
            flops=int(micros * RATE), bytes_accessed=1024, transcendentals=0
        ),
    )
    prefetch = () if order is None else (order,)
    return lambda *args: call(*prefetch, *args, *after)


def shape(*dims, dtype=F32):
    return jax.ShapeDtypeStruct(dims, dtype)


def full(*dims):
    return pl.BlockSpec(dims, lambda *_: (0,) * len(dims))


def tile(rows):
    return pl.BlockSpec((rows, TILE), lambda j, *_: (0, j))


def pair_of(spec):
    return [spec, spec]


def sigmoid(value):
    return 0.5 * jnp.tanh(0.5 * value) + 0.5


def silu_pair(value):
    sig = sigmoid(value)
    act = value * sig
    return act, sig + act * (1.0 - sig)


def start_or_add(ref, value, first):
    @pl.when(first)
    def _():
        ref[...] = value

    @pl.when(jnp.logical_not(first))
    def _():
        ref[...] += value


def fold(value):
    width = value.shape[1]
    if width % 128:
        return jnp.broadcast_to(
            jnp.sum(value, axis=1, keepdims=True) / 128.0, (value.shape[0], 128)
        )
    return sum(
        value[:, at : at + 128] for at in range(128, width, 128)
    ) + value[:, :128] if width > 128 else value


def rows_of(*folded):
    return jnp.concatenate(
        [jnp.sum(value, axis=1, keepdims=True) for value in folded], axis=1
    ).T


def moments(pre):
    mean = jnp.mean(pre, axis=1, keepdims=True)
    cent = pre - mean
    return jnp.concatenate(
        [mean, jnp.sum(cent * cent, axis=1, keepdims=True)], axis=1
    ).T


def first_kernel(order, counts, factor, mask, w_enc_t, out, high, low):
    del order
    weight = split(w_enc_t[...])
    high[...], low[...] = weight
    scaled = counts[...] * factor[...] * mask[...].T
    out[...] = dot(weight, split(scaled), 1, 0)


def encode_kernel(order, counts, factor, mask, high, low, *outs):
    del order
    scaled = counts[...] * factor[...] * mask[...].T
    product = dot((high[...], low[...]), split(scaled), 1, 0)
    for place, out in enumerate(outs):

        @pl.when(pl.program_id(0) == place)
        def _():
            out[...] = product


def encode_products(order, counts, factor, mask, weight, after=()):
    genes = counts.shape[0]
    hidden = weight[0].shape[0]
    blocks = order.shape[0]
    begin = len(weight) == 1
    matrix = full(hidden, genes)
    return kernel_call(
        first_kernel if begin else encode_kernel,
        (blocks,),
        [
            pl.BlockSpec((genes, TILE), lambda j, order: (0, order[j])),
            pl.BlockSpec((1, TILE), lambda j, order: (0, order[j])),
            full(1, genes),
        ]
        + [matrix] * len(weight),
        [full(hidden, TILE)] * blocks + ([matrix] * 2 if begin else []),
        [shape(hidden, TILE)] * blocks
        + ([shape(hidden, genes, dtype=BF16)] * 2 if begin else []),
        2 * blocks,
        order=order,
        after=after,
    )(counts, factor, mask, *weight)


def prepare_kernel(w_out_t, w_enc_t, out_high, out_low, turn_high, turn_low,
                   enc_high, enc_low):
    out_high[...], out_low[...] = split(w_out_t[...])
    turn_high[...], turn_low[...] = split(w_out_t[...].T)
    enc_high[...], enc_low[...] = split(w_enc_t[...].T)


def prepare(w_out_t, w_enc_t, after):
    hidden, genes = w_out_t.shape
    specs = pair_of(full(hidden, genes)) + pair_of(full(genes, hidden)) * 2
    return kernel_call(
        prepare_kernel,
        (),
        pair_of(full(hidden, genes)),
        specs,
        [shape(hidden, genes, dtype=BF16)] * 2 + [shape(genes, hidden, dtype=BF16)] * 4,
        4,
        after=after,
    )(w_out_t, w_enc_t)


def own_kernel(*refs):
    *parts, pre_out, stats = refs
    pre = sum(part[...] for part in parts[1:]) + parts[0][...]
    pre_out[...] = pre
    stats[...] = moments(pre)


def own_moments(parts):
    rows, columns = parts[0].shape
    return kernel_call(
        own_kernel,
        (),
        [full(rows, columns)] * len(parts),
        [full(rows, columns), full(2, rows)],
        [shape(rows, columns), shape(2, rows)],
        3,
    )(*parts)


def normalize(pre, vector):
    columns = vector.T
    norm = (pre - columns[:, 0:1]) * lax.rsqrt(columns[:, 1:2] + BN_EPS)
    return norm, norm * columns[:, 2:3] + columns[:, 3:4]


def latent_kernel(pre, vector, w_lat, b_lat, noise, z_out):
    _, value = normalize(pre[...], vector[...])
    act, _ = silu_pair(value)
    lat = dot(split(w_lat[...]), split(act), 1, 0) + b_lat[...].T
    latent = noise.shape[0]
    z_out[...] = lat[:latent] + jnp.exp(0.5 * lat[latent:]) * noise[...]


def latent_own(pre, vector, w_lat, b_lat, noise):
    return kernel_call(
        latent_kernel,
        (),
        [full(*a.shape) for a in (pre, vector, w_lat, b_lat, noise)],
        full(*noise.shape),
        shape(*noise.shape),
        3,
    )(pre, vector, w_lat, b_lat, noise)


def spread_kernel(order, w_dec, mine, other, z_all, pre_out, stats):
    blocks = order.shape[1]
    width = mine.shape[2]
    for place in range(blocks):
        spot = order[0, place]
        block = jnp.where(order[1, place] == 0, mine[spot], other[spot])
        z_all[:, place * width : (place + 1) * width] = block
    pre = dot(split(w_dec[...]), split(z_all[...]), 0, 0)
    pre_out[...] = pre
    stats[...] = moments(pre)


def decoder_hidden(order, w_dec, mine, other):
    latent, hidden = w_dec.shape
    cells = order.shape[1] * mine.shape[2]
    return kernel_call(
        spread_kernel,
        (1,),
        [full(latent, hidden), full(*mine.shape), full(*other.shape)],
        [full(latent, cells), full(hidden, cells), full(2, hidden)],
        [shape(latent, cells), shape(hidden, cells), shape(2, hidden)],
        8,
        order=order,
    )(w_dec, mine, other)


def decoder_kernel(cells, order, pre, vector, out_high, out_low, turn_high, turn_low,
                   counts, factor, mask, b_out, w_dec,
                   recon_out, grad_high, grad_low, act_high, act_low, term_out, z_out,
                   sums, bias_out, sum_term, sum_gain, sum_grad):
    del order
    step = pl.program_id(0)
    first = step == 0
    norm, value = normalize(pre[...], vector[...])
    act, slope = silu_pair(value)
    act_pair = split(act)
    act_high[...], act_low[...] = act_pair
    out = dot((turn_high[...], turn_low[...]), act_pair, 1, 0) + b_out[...].T
    recon = jnp.maximum(out, 0.0) + jnp.log(1.0 + jnp.exp(-jnp.abs(out)))
    recon_out[...] = recon
    mask_column = mask[...].T * (1.0 / cells)
    grad = (recon - counts[...] * factor[...]) * (mask_column * sigmoid(out))
    grad_pair = split(grad)
    grad_high[...], grad_low[...] = grad_pair
    term = dot((out_high[...], out_low[...]), grad_pair, 1, 0) * slope
    term_out[...] = term
    scaled_dec = w_dec[...] * (vector[2:3, :] * lax.rsqrt(vector[1:2, :] + BN_EPS))
    z_out[...] = dot(split(scaled_dec), split(term), 1, 0)
    start_or_add(sum_term, fold(term), first)
    start_or_add(sum_gain, fold(term * norm), first)
    start_or_add(sum_grad, fold(grad), first)

    @pl.when(step == pl.num_programs(0) - 1)
    def _():
        sums[...] = rows_of(sum_term[...], sum_gain[...])
        bias_out[...] = rows_of(sum_grad[...])


def decoder(cells, order, pre, vector, out_pair, turn_pair, counts, factor, mask, b_out,
            w_dec):
    hidden, genes = out_pair[0].shape
    here = counts.shape[1]
    latent = w_dec.shape[0]
    return kernel_call(
        lambda *refs: decoder_kernel(cells, *refs),
        (here // TILE,),
        [tile(hidden), full(4, hidden)]
        + pair_of(full(hidden, genes))
        + pair_of(full(genes, hidden))
        + [
            tile(genes),
            tile(1),
            full(1, genes),
            full(1, genes),
            full(latent, hidden),
        ],
        [tile(genes)]
        + pair_of(tile(genes))
        + pair_of(tile(hidden))
        + [
            tile(hidden),
            pl.BlockSpec((latent, TILE), lambda j, order: (0, order[j])),
            full(2, hidden),
            full(1, genes),
        ],
        [shape(genes, here)]
        + [shape(genes, here, dtype=BF16)] * 2
        + [shape(hidden, here, dtype=BF16)] * 2
        + [
            shape(hidden, here),
            shape(latent, here),
            shape(2, hidden),
            shape(1, genes),
        ],
        40,
        order=order,
        scratch=[
            pltpu.VMEM((hidden, 128), F32),
            pltpu.VMEM((hidden, 128), F32),
            pltpu.VMEM((genes, 128), F32),
        ],
    )(pre, vector, *out_pair, *turn_pair, counts, factor, mask, b_out, w_dec)


def weight_kernel(order, left_high, left_low, right_high, right_low, out):
    del order
    product = dot(
        (left_high[...], left_low[...]), (right_high[...], right_low[...]), 1, 1
    )
    start_or_add(out, product, pl.program_id(0) == 0)


def weight_half(order, halves, left, right, width, after=()):
    rows, here = left[0].shape
    rows //= halves
    genes = right[0].shape[0]
    return kernel_call(
        weight_kernel,
        (here // width,),
        pair_of(pl.BlockSpec((rows, width), lambda j, order: (order[0], j)))
        + pair_of(pl.BlockSpec((genes, width), lambda j, order: (0, j))),
        full(rows, genes),
        shape(rows, genes),
        14 // halves,
        order=order,
        after=after,
    )(*left, *right)


def small_weight_kernel(z, pre, vector, term, term_out, pair_out, sum_out):
    first = pl.program_id(0) == 0
    norm, _ = normalize(pre[...], vector[...])
    z_pair = split(z[...])
    start_or_add(term_out, dot(z_pair, split(term[...]), 1, 1), first)
    start_or_add(pair_out, dot(z_pair, split(norm), 1, 1), first)
    start_or_add(sum_out, rows_of(z[...]), first)


def small_weights(z, pre, vector, term, after=()):
    hidden, here = pre.shape
    latent = z.shape[0]
    return kernel_call(
        small_weight_kernel,
        (here // TILE,),
        [tile(latent), tile(hidden), full(4, hidden), tile(hidden)],
        [full(latent, hidden)] * 2 + [full(1, latent)],
        [shape(latent, hidden)] * 2 + [shape(1, latent)],
        12,
        after=after,
    )(z, pre, vector, term)


def again_kernel(cells, pre_enc, vector1, w_lat, b_lat, pre_dec, vector2, sums2, w_dec,
                 lat_out, act_out, slope_out, fix_out):
    _, value = normalize(pre_enc[...], vector1[...])
    act, slope = silu_pair(value)
    act_out[...] = act
    slope_out[...] = slope
    lat_out[...] = dot(split(w_lat[...]), split(act), 1, 0) + b_lat[...].T
    norm2, _ = normalize(pre_dec[...], vector2[...])
    scaled_dec = w_dec[...] * (vector2[2:3, :] * lax.rsqrt(vector2[1:2, :] + BN_EPS))
    gain_term = scaled_dec * (sums2[1:2, :] * (1.0 / cells))
    shift_term = jnp.sum(
        scaled_dec * (sums2[0:1, :] * (1.0 / cells)), axis=1, keepdims=True
    )
    fix_out[...] = dot(split(gain_term), split(norm2), 1, 0) + shift_term


def encode_again(cells, pre_enc, vector1, w_lat, b_lat, pre_dec, vector2, sums2, w_dec,
                 after=()):
    hidden, here = pre_enc.shape
    latents = w_lat.shape[0]
    latent = w_dec.shape[0]
    return kernel_call(
        lambda *refs: again_kernel(cells, *refs),
        (here // TILE,),
        [
            tile(hidden),
            full(4, hidden),
            full(latents, hidden),
            full(1, latents),
            tile(hidden),
            full(4, hidden),
            full(2, hidden),
            full(latent, hidden),
        ],
        [tile(latents), tile(hidden), tile(hidden), tile(latent)],
        [
            shape(latents, here),
            shape(hidden, here),
            shape(hidden, here),
            shape(latent, here),
        ],
        16,
        after=after,
    )(pre_enc, vector1, w_lat, b_lat, pre_dec, vector2, sums2, w_dec)


def latent_back_kernel(cells, order, mine, other, fix, lat, noise, w_lat, slope, act, pre,
                       vector, grad_out, sums, weight_out, bias_out,
                       sum_grad, sum_gain, sum_lat):
    step = pl.program_id(0)
    first = step == 0
    latent = noise.shape[0]
    term_z = jnp.where(order[1, step] == 0, mine[...], other[...])
    grad_z = term_z - fix[...]
    mu = lat[:latent, :]
    spread = jnp.exp(0.5 * lat[latent:, :])
    grad_mu = grad_z + (ALPHA / cells) * mu
    grad_logvar = 0.5 * grad_z * noise[...] * spread + (0.5 * ALPHA / cells) * (
        spread * spread - 1.0
    )
    grad_lat = jnp.concatenate([grad_mu, grad_logvar], axis=0)
    lat_pair = split(grad_lat)
    grad_in = dot(split(w_lat[...]), lat_pair, 0, 0) * slope[...]
    grad_out[...] = grad_in
    norm, _ = normalize(pre[...], vector[...])
    start_or_add(sum_grad, fold(grad_in), first)
    start_or_add(sum_gain, fold(grad_in * norm), first)
    start_or_add(sum_lat, fold(grad_lat), first)
    start_or_add(weight_out, dot(lat_pair, split(act[...]), 1, 1), first)

    @pl.when(step == pl.num_programs(0) - 1)
    def _():
        sums[...] = rows_of(sum_grad[...], sum_gain[...])
        bias_out[...] = rows_of(sum_lat[...])


def latent_back(cells, order, mine, other, fix, lat, noise, w_lat, slope, act, pre, vector):
    hidden, here = pre.shape
    latents = lat.shape[0]
    latent = noise.shape[0]
    block = pl.BlockSpec((None, latent, TILE), lambda j, order: (order[0, j], 0, 0))
    return kernel_call(
        lambda *refs: latent_back_kernel(cells, *refs),
        (here // TILE,),
        [
            block,
            block,
            tile(latent),
            tile(latents),
            tile(latent),
            full(latents, hidden),
            tile(hidden),
            tile(hidden),
            tile(hidden),
            full(4, hidden),
        ],
        [tile(hidden), full(2, hidden), full(latents, hidden), full(1, latents)],
        [
            shape(hidden, here),
            shape(2, hidden),
            shape(latents, hidden),
            shape(1, latents),
        ],
        16,
        order=order,
        scratch=[
            pltpu.VMEM((hidden, 128), F32),
            pltpu.VMEM((hidden, 128), F32),
            pltpu.VMEM((latents, 128), F32),
        ],
    )(mine, other, fix, lat, noise, w_lat, slope, act, pre, vector)


def encoder_weight_kernel(cells, order, grad_in, pre, vector, counts, factor, mask,
                          high, low, out):
    del order
    columns = vector[...].T
    scale = lax.rsqrt(columns[:, 1:2] + BN_EPS)
    norm = (pre[...] - columns[:, 0:1]) * scale
    grad_pre = (columns[:, 2:3] * scale) * (
        grad_in[...]
        - columns[:, 4:5] * (1.0 / cells)
        - norm * (columns[:, 5:6] * (1.0 / cells))
    )
    pair = split(grad_pre)
    high[...], low[...] = pair
    scaled = counts[...] * factor[...] * mask[...].T
    product = dot(pair, split(scaled), 1, 1)
    start_or_add(out, product, pl.program_id(0) == 0)


def encoder_weight(cells, order, halves, grad_in, pre, vector, sums, counts, factor, mask,
                   width, after=()):
    hidden, here = pre.shape
    rows = hidden // halves
    genes = counts.shape[0]
    parts = pl.BlockSpec((rows, width), lambda j, order: (order[0], j))
    vectors = jnp.concatenate([vector, sums])
    vectors = vectors.reshape(6, halves, rows).swapaxes(0, 1)
    mine = pl.BlockSpec((rows, width), lambda j, order: (0, j))
    return kernel_call(
        lambda *refs: encoder_weight_kernel(cells, *refs),
        (here // width,),
        [
            parts,
            parts,
            pl.BlockSpec((None, 6, rows), lambda j, order: (order[0], 0, 0)),
            pl.BlockSpec((genes, width), lambda j, order: (0, j)),
            pl.BlockSpec((1, width), lambda j, order: (0, j)),
            full(1, genes),
        ],
        pair_of(mine) + [full(rows, genes)],
        [shape(rows, here, dtype=BF16)] * 2 + [shape(rows, genes)],
        18 // halves,
        order=order,
        after=after,
    )(grad_in, pre, vectors, counts, factor, mask)


def counts_kernel(cells, halves, order, *refs):
    enc_high, enc_low, *grads, recon, counts, factor, mask, out = refs
    mask_column = mask[...].T
    weight = factor[...] * mask_column
    diff = (recon[...] - counts[...] * factor[...]) * (mask_column * (1.0 / cells))
    pairs = [(grads[2 * k][...], grads[2 * k + 1][...]) for k in range(halves)]
    if halves == 2:
        swapped = order[0] != 0
        pairs = [
            tuple(jnp.where(swapped, b, a) for a, b in zip(*pairs)),
            tuple(jnp.where(swapped, a, b) for a, b in zip(*pairs)),
        ]
        pairs = [tuple(jnp.concatenate([a, b], axis=0) for a, b in zip(*pairs))]
    out[...] = (dot((enc_high[...], enc_low[...]), pairs[0], 1, 0) - diff) * weight


def counts_back(cells, order, enc_pair, grads, recon, counts, factor, mask, after=()):
    genes, hidden = enc_pair[0].shape
    here = counts.shape[1]
    halves = len(grads)
    return kernel_call(
        lambda *refs: counts_kernel(cells, halves, *refs),
        (here // TILE,),
        pair_of(full(genes, hidden))
        + pair_of(tile(hidden // halves)) * halves
        + [tile(genes), tile(genes), tile(1), full(1, genes)],
        tile(genes),
        shape(genes, here),
        18,
        order=order,
        after=after,
    )(*enc_pair, *[x for pair in grads for x in pair], recon, counts, factor, mask)


def add_kernel(left, right, out):
    out[...] = left[...] + right[...]


def add_arrays(left, right, after=()):
    rows, columns = left.shape
    return kernel_call(
        add_kernel,
        (2,),
        pair_of(pl.BlockSpec((rows // 2, columns), lambda j: (j, 0))),
        pl.BlockSpec((rows // 2, columns), lambda j: (j, 0)),
        shape(rows, columns),
        1,
        after=after,
    )(left, right)


def join_kernel(order, mine, other, out):
    own = order[0] == pl.program_id(0)

    @pl.when(own)
    def _():
        out[...] = other[...]

    @pl.when(jnp.logical_not(own))
    def _():
        out[...] = mine[...]


def join_halves(order, mine, other):
    rows, columns = mine.shape
    return kernel_call(
        join_kernel,
        (2,),
        pair_of(full(rows, columns)),
        pl.BlockSpec((rows, columns), lambda j, _: (j, 0)),
        shape(2 * rows, columns),
        2,
        order=order,
    )(mine, other)


def swap(value, axis, bit):
    size = lax.axis_size(axis)
    return lax.ppermute(value, axis, [(i, i ^ bit) for i in range(size)])


def bits(axis):
    size, bit, out = lax.axis_size(axis), 1, []
    while bit < size:
        out.append(bit)
        bit *= 2
    return out


def add_all(value, axes):
    for axis in axes:
        for bit in bits(axis):
            value = value + swap(value, axis, bit)
    return value


def moments_all(both, count, axes):
    for axis in axes:
        for bit in bits(axis):
            other = swap(both, axis, bit)
            gap = both[0] - other[0]
            both = jnp.stack(
                [
                    0.5 * (both[0] + other[0]),
                    both[1] + other[1] + gap * gap * (0.5 * count),
                ]
            )
            count = 2 * count
    return both[0], both[1] / count


def scatter_gene_blocks(value):
    me = lax.axis_index(GENE)
    for bit in reversed(bits(GENE)):
        half = value.shape[0] // 2
        upper = (me & bit) != 0
        sent = jnp.where(upper, value[:half], value[half:])
        kept = jnp.where(upper, value[half:], value[:half])
        value = kept + swap(sent, GENE, bit)
    return value[0]


def gene_pairs(links):
    return [(2 * a + y, 2 * b + y) for a, b in links for y in (0, 1)]


OUTER = gene_pairs([(0, 1), (3, 2)])
MIDDLE = gene_pairs([(1, 2), (2, 1)])
SIDES = gene_pairs([(0, 1), (1, 0), (2, 3), (3, 2)])


def line_order(z):
    low = z < 2
    return [
        jnp.where(low, z + 3, z + 1) % 4,
        (z + 2) % 4,
        jnp.where(low, z + 1, z + 3) % 4,
        z,
    ]


def scatter_encoded(counts, factor, mask, w_enc_t, w_out_t):
    size = lax.axis_size(GENE)
    here = counts.shape[1]
    me = lax.axis_index(GENE)
    if size != 8 or here != size * TILE:
        order = jnp.arange(here // TILE, dtype=jnp.int32)
        one, *pair = encode_products(order[:1], counts, factor, mask, [w_enc_t])
        blocks = [one] + list(encode_products(order[1:], counts, factor, mask, pair))
        return [
            lax.psum_scatter(
                jnp.concatenate(blocks, axis=1), GENE, scatter_dimension=1, tiled=True
            )
        ], prepare(w_out_t, w_enc_t, ())
    z, y = me // 2, me % 2
    order = jnp.stack(
        [2 * spot + side for spot in line_order(z) for side in (1 - y, y)]
    ).astype(jnp.int32)
    one, *pair = encode_products(order[:1], counts, factor, mask, [w_enc_t])
    blocks = [one]
    blocks += encode_products(order[1:3], counts, factor, mask, pair)
    blocks += encode_products(order[3:], counts, factor, mask, pair, after=blocks[1:2])
    weights = prepare(w_out_t, w_enc_t, blocks[3:4])
    part = [blocks[2 * k + 1] + swap(blocks[2 * k], GENE, 1) for k in range(4)]
    middle = (z == 1) | (z == 2)
    first = lax.ppermute(part[0], GENE, OUTER)
    second = lax.ppermute(part[1], GENE, OUTER)
    across = lax.ppermute(part[1] + first, GENE, MIDDLE)
    side = lax.ppermute(jnp.where(middle, part[0] + across, part[2]), GENE, SIDES)
    inner = lax.ppermute(part[2] + second, GENE, MIDDLE)
    return [part[3], side, inner], weights


def on_line(value):
    return lax.axis_size(GENE) == 8 and value.shape[1] == TILE


def gather_blocks(value):
    rows = value.shape[0]
    if not on_line(value):
        value = lax.all_gather(value, GENE, axis=1, tiled=True)
        blocks = value.shape[1] // TILE
        stack = jnp.moveaxis(value.reshape(rows, blocks, TILE), 1, 0)
        place = jnp.arange(blocks, dtype=jnp.int32)
        return stack, stack, jnp.stack([place, 0 * place])
    mine = jnp.stack([value] + [swap(value, GENE, bit) for bit in (2, 4, 6)])
    other = swap(mine, GENE, 1)
    rank = lax.axis_index(GENE) ^ jnp.arange(8, dtype=jnp.int32)
    return mine, other, jnp.stack([rank // 2, rank % 2]).astype(jnp.int32)


def send_order(here):
    if lax.axis_size(GENE) != 8 or here != 8 * TILE:
        return jnp.arange(here // TILE, dtype=jnp.int32)
    rank = lax.axis_index(GENE) ^ jnp.arange(8, dtype=jnp.int32)
    return (4 * (1 - rank % 2) + (rank // 2 + 3) % 4).astype(jnp.int32)


def scatter_terms(value):
    size = lax.axis_size(GENE)
    here = value.shape[1]
    if size != 8 or here != size * TILE:
        return lax.psum_scatter(value, GENE, scatter_dimension=1, tiled=True)
    half = here // 2
    part = value[:, half:] + swap(value[:, :half], GENE, 1)
    total = part[:, 3 * TILE :]
    for k in (1, 2, 3):
        total = total + swap(part[:, (k - 1) * TILE : k * TILE], GENE, 2 * k)
    return total


def add_batch_halves(order, halves, after=()):
    if len(halves) == 1:
        return lax.psum(halves[0], BATCH)
    other, mine = halves
    mine = add_arrays(mine, swap(other, BATCH, 1))
    mine = add_arrays(mine, swap(mine, BATCH, 2), after)
    other = swap(mine, BATCH, 1)
    return join_halves(order, mine, other)


def on_device(
    counts_in,
    umi_total,
    gene_mask,
    noise,
    w_enc,
    gain_enc,
    shift_enc,
    w_lat,
    b_lat,
    w_dec,
    gain_dec,
    shift_dec,
    w_out,
    b_out,
    mean_enc,
    var_enc,
    mean_dec,
    var_dec,
):
    here = counts_in.shape[1]
    cells = here * lax.axis_size(BATCH)
    hidden = w_enc.shape[1]
    ranks = lax.axis_size(GENE)
    share = hidden // ranks
    own = here // ranks
    latent = noise.shape[0]
    me = lax.axis_index(GENE)
    both = (BATCH, GENE)
    core = lax.axis_index(BATCH) % 2
    halves = 2 if lax.axis_size(BATCH) == 4 else 1
    order = [1 - core, core] if halves == 2 else [0 * core]
    order = [half.astype(jnp.int32)[None] for half in order]
    width = 1024

    def hidden_part(vector):
        return lax.dynamic_slice_in_dim(vector, me * share, share, vector.ndim - 1)

    def hidden_whole(part):
        empty = jnp.zeros((part.shape[0], hidden), F32)
        return add_all(
            lax.dynamic_update_slice_in_dim(empty, part, me * share, 1), (GENE,)
        )

    factor = (UMI_SCALE / umi_total.astype(F32))[None, :]
    mask = gene_mask.astype(F32)[None, :]
    w_enc_t = w_enc.T
    w_out_t = w_out.T
    b_lat_row = b_lat[None, :]
    noise_own = lax.dynamic_slice_in_dim(noise, me * own, own, 1)

    parts, weights = scatter_encoded(counts_in, factor, mask, w_enc_t, w_out_t)
    out_pair, turn_pair, enc_pair = weights[:2], weights[2:4], weights[4:]
    affine1 = hidden_whole(jnp.stack([gain_enc, shift_enc]))
    pre_own, stats1 = own_moments(parts)
    pre_enc = lax.all_gather(pre_own, GENE, axis=1, tiled=True)
    mean1, var1 = moments_all(stats1, own, both)
    vector1 = jnp.concatenate([mean1[None], var1[None], affine1])
    z_own = latent_own(pre_own, vector1, w_lat, b_lat_row, noise_own)

    z_mine, z_other, z_order = gather_blocks(z_own)
    z, pre_dec, stats2 = decoder_hidden(z_order, w_dec, z_mine, z_other)
    mean2, var2 = moments_all(stats2, here, (BATCH,))
    vector2 = jnp.stack([mean2, var2, gain_dec, shift_dec])
    recon, grad_high, grad_low, act_high, act_low, term, term_z, sums2, grad_b_out = decoder(
        cells, send_order(here), pre_dec, vector2, out_pair, turn_pair, counts_in, factor,
        mask, b_out[None, :], w_dec
    )

    term_mine, term_other, term_order = gather_blocks(scatter_terms(term_z))
    sums2 = add_all(sums2, both)
    grad_w_out = [
        weight_half(half, halves, (act_high, act_low), (grad_high, grad_low), width)
        for half in order
    ]
    grad_w_out = add_batch_halves(order[0], grad_w_out).T
    lat, act1, slope1, fix_z = encode_again(
        cells, pre_enc, vector1, w_lat, b_lat_row, pre_dec, vector2, sums2, w_dec
    )
    term_w_dec, pair_w_dec, sum_z = small_weights(z, pre_dec, vector2, term)

    grad_in1, sums1, grad_w_lat, grad_b_lat = latent_back(
        cells, term_order, term_mine, term_other, fix_z, lat, noise, w_lat, slope1, act1,
        pre_enc, vector1
    )
    sums1 = add_all(
        jnp.concatenate(
            [sums1.reshape(-1), grad_b_lat[0], grad_b_out[0], sum_z[0]]
        ),
        (BATCH,),
    )
    grad_b_lat = sums1[2 * hidden : 2 * hidden + 2 * latent]
    grad_b_out = sums1[2 * hidden + 2 * latent : -latent]
    sum_z = sums1[-latent:]
    sums1 = sums1[: 2 * hidden].reshape(2, hidden)
    grads, weight_parts, last = [], [], ()
    for half in order:
        high, low, part = encoder_weight(
            cells, half, halves, grad_in1, pre_enc, vector1, sums1, counts_in, factor, mask,
            width, after=last
        )
        grads.append((high, low))
        weight_parts.append(part)
        last = (part,)
    grad_counts = counts_back(
        cells, order[0], enc_pair, grads, recon, counts_in, factor, mask
    )
    grad_w_enc = add_batch_halves(order[0], weight_parts, (grad_counts,)).T

    term_w_dec = scatter_gene_blocks(
        jnp.moveaxis(term_w_dec.reshape(latent, ranks, share), 1, 0)
    )
    small = add_all(
        jnp.concatenate(
            [
                term_w_dec,
                hidden_part(pair_w_dec),
                hidden_part(grad_w_lat),
            ]
        ),
        (BATCH,),
    )
    term_w_dec = small[:latent]
    pair_w_dec = small[latent : 2 * latent]
    grad_w_lat = small[2 * latent :]
    scale2 = hidden_part(gain_dec * lax.rsqrt(var2 + BN_EPS))
    grad_shift2 = hidden_part(sums2[0])
    grad_gain2 = hidden_part(sums2[1])
    grad_w_dec = scale2[None, :] * (
        term_w_dec
        - sum_z[:, None] * (grad_shift2 / cells)[None, :]
        - pair_w_dec * (grad_gain2 / cells)[None, :]
    )

    correct = cells / (cells - 1.0)
    new_mean_enc = (1.0 - MOMENTUM) * mean_enc + MOMENTUM * hidden_part(mean1)
    new_var_enc = (1.0 - MOMENTUM) * var_enc + MOMENTUM * hidden_part(var1) * correct
    new_mean_dec = (1.0 - MOMENTUM) * mean_dec + MOMENTUM * mean2
    new_var_dec = (1.0 - MOMENTUM) * var_dec + MOMENTUM * var2 * correct
    return (
        recon,
        grad_counts,
        grad_w_enc,
        hidden_part(sums1[1]),
        hidden_part(sums1[0]),
        grad_w_lat,
        grad_b_lat,
        grad_w_dec,
        grad_gain2,
        grad_shift2,
        grad_w_out,
        grad_b_out,
        new_mean_enc,
        new_var_enc,
        new_mean_dec,
        new_var_dec,
    )


def solution(mesh):
    return jax.shard_map(
        on_device,
        mesh=mesh,
        in_specs=(
            P(GENE, BATCH),
            P(BATCH),
            P(GENE),
            P(None, BATCH),
            P(GENE, None),
            P(GENE),
            P(GENE),
            P(),
            P(),
            P(),
            P(),
            P(),
            P(GENE, None),
            P(GENE),
            P(GENE),
            P(GENE),
            P(),
            P(),
        ),
        out_specs=(
            P(GENE, BATCH),
            P(GENE, BATCH),
            P(GENE, None),
            P(GENE),
            P(GENE),
            P(None, GENE),
            P(),
            P(None, GENE),
            P(GENE),
            P(GENE),
            P(GENE, None),
            P(GENE),
            P(GENE),
            P(GENE),
            P(),
            P(),
        ),
        check_vma=False,
    )
```

```python
import jax
import jax.numpy as jnp
from jax import lax
from jax.experimental import pallas as pl
from jax.experimental.pallas import tpu as pltpu
from jax.sharding import PartitionSpec as P

ALPHA = 0.002
BN_EPS = 1e-05
MOMENTUM = 0.1
UMI_SCALE = 10000.0
BATCH = "batch"
GENE = "gene"
TILE = 512
HALF = 256
ROWS = 16
VMEM_BYTES = 56 << 20
F32 = jnp.float32


BF16 = jnp.bfloat16
RATE = 600_000_000


def split(value):
    high = value.astype(BF16)
    return high, (value - high.astype(F32)).astype(BF16)


def whole(pair):
    return pair[0].astype(F32) + pair[1].astype(F32)


def dot(left, right, left_dim, right_dim):
    def one(a, b):
        return lax.dot_general(
            a,
            b,
            (((left_dim,), (right_dim,)), ((), ())),
            preferred_element_type=F32,
        )

    return one(left[0], right[0]) + (one(left[0], right[1]) + one(left[1], right[0]))


def kernel_call(
    body, grid, in_specs, out_specs, out_shape, micros, order=None, scratch=(), after=(),
    onto=(),
):
    leading = 0 if order is None else 1
    held = leading + len(in_specs)

    def run(*refs):
        body(*refs[:held], *refs[held + len(after) :])

    call = pl.pallas_call(
        run,
        grid_spec=pltpu.PrefetchScalarGridSpec(
            num_scalar_prefetch=leading,
            grid=grid,
            in_specs=list(in_specs) + [pl.BlockSpec(memory_space=pl.ANY)] * len(after),
            out_specs=out_specs,
            scratch_shapes=list(scratch),
        ),
        out_shape=out_shape,
        input_output_aliases={held + k: out for k, out in enumerate(onto)},
        compiler_params=pltpu.CompilerParams(vmem_limit_bytes=VMEM_BYTES),
        cost_estimate=pl.CostEstimate(
            flops=int(micros * RATE), bytes_accessed=1024, transcendentals=0
        ),
    )
    prefetch = () if order is None else (order,)
    return lambda *args: call(*prefetch, *args, *after)


def shape(*dims, dtype=F32):
    return jax.ShapeDtypeStruct(dims, dtype)


def full(*dims):
    return pl.BlockSpec(dims, lambda *_: (0,) * len(dims))


def tile(rows):
    return pl.BlockSpec((rows, TILE), lambda j, *_: (0, j))


def pair_of(spec):
    return [spec, spec]


def sigmoid(value):
    return 0.5 * jnp.tanh(0.5 * value) + 0.5


def silu_pair(value):
    sig = sigmoid(value)
    act = value * sig
    return act, sig + act * (1.0 - sig)


def start_or_add(ref, value, first):
    @pl.when(first)
    def _():
        ref[...] = value

    @pl.when(jnp.logical_not(first))
    def _():
        ref[...] += value


def fold(value):
    width = value.shape[1]
    if width % 128:
        return jnp.broadcast_to(
            jnp.sum(value, axis=1, keepdims=True) / 128.0, (value.shape[0], 128)
        )
    return sum(
        value[:, at : at + 128] for at in range(128, width, 128)
    ) + value[:, :128] if width > 128 else value


def rows_of(*folded):
    return jnp.concatenate(
        [jnp.sum(value, axis=1, keepdims=True) for value in folded], axis=1
    ).T


def moments(pre):
    mean = jnp.mean(pre, axis=1, keepdims=True)
    cent = pre - mean
    return jnp.concatenate(
        [mean, jnp.sum(cent * cent, axis=1, keepdims=True)], axis=1
    ).T


def wide(column):
    return jnp.concatenate([column] * (TILE // 128), axis=1)


def spread(column):
    return jnp.broadcast_to(column, (column.shape[0], 128))


def split_scaled(counts, factor, mask, high, low):
    column = mask[...].T
    scale = factor[...]
    for at in range(0, counts.shape[0], ROWS):
        rows = pl.ds(at, ROWS)
        high[rows, :], low[rows, :] = split(
            counts[rows, :] * scale * column[at : at + ROWS]
        )


def encode_kernel(order, counts, factor, mask, w_enc_t, *refs):
    *outs, high, low, scaled_high, scaled_low = refs
    step = pl.program_id(0)

    @pl.when(step == 0)
    def _():
        for at in range(0, high.shape[0], ROWS):
            rows = pl.ds(at, ROWS)
            high[rows, :], low[rows, :] = split(w_enc_t[rows, :])

    split_scaled(counts, factor, mask, scaled_high, scaled_low)
    product = dot(
        (high[...], low[...]), (scaled_high[...], scaled_low[...]), 1, 0
    )
    side = order[0] == 0
    for place in range(len(outs) // 3):
        other, own, both = outs[3 * place : 3 * place + 3]
        rows = other.shape[0]

        @pl.when(step == place)
        def _():
            if rows < product.shape[0]:
                both[...] = product[rows:]

        @pl.when((step == place) & side)
        def _():
            other[...] = product[:rows, HALF:]
            own[...] = product[:rows, :HALF]

        @pl.when((step == place) & jnp.logical_not(side))
        def _():
            other[...] = product[:rows, :HALF]
            own[...] = product[:rows, HALF:]


def encode_products(side, order, counts, factor, mask, w_enc_t, rest, after=()):
    genes = counts.shape[0]
    hidden = w_enc_t.shape[0]
    blocks = order.shape[0]
    cells = lambda j, order: (0, order[j + 1])
    sizes = [(hidden - rest, HALF)] * 2 + [(max(rest, 8), TILE)]
    return kernel_call(
        encode_kernel,
        (blocks,),
        [
            pl.BlockSpec((genes, TILE), cells),
            pl.BlockSpec((1, TILE), cells),
            full(1, genes),
            full(hidden, genes),
        ],
        [full(*size) for size in sizes] * blocks,
        [shape(*size) for size in sizes] * blocks,
        4 * blocks,
        order=jnp.concatenate([side[None], order]).astype(jnp.int32),
        scratch=[pltpu.VMEM((hidden, genes), BF16)] * 2
        + [pltpu.VMEM((genes, TILE), BF16)] * 2,
        after=after,
    )(counts, factor, mask, w_enc_t)


def scale_counts(counts, factor, mask, after):
    genes, here = counts.shape
    return kernel_call(
        split_scaled,
        (here // TILE,),
        [tile(genes), tile(1), full(1, genes)],
        pair_of(tile(genes)),
        [shape(genes, here, dtype=BF16)] * 2,
        5,
        after=after,
    )(counts, factor, mask)


def prepare_kernel(w_out_t, w_enc_t, w_lat, w_dec, out_high, out_low, turn_high, turn_low,
                   enc_high, enc_low, lat_high, lat_low, tal_high, tal_low,
                   dec_high, dec_low):
    out_high[...], out_low[...] = split(w_out_t[...])
    turn_high[...], turn_low[...] = split(w_out_t[...].T)
    enc_high[...], enc_low[...] = split(w_enc_t[...].T)
    lat_high[...], lat_low[...] = split(w_lat[...])
    tal_high[...], tal_low[...] = split(w_lat[...].T)
    dec_high[...], dec_low[...] = split(w_dec[...].T)


def prepare(w_out_t, w_enc_t, w_lat, w_dec, after):
    hidden, genes = w_out_t.shape
    latents, latent = w_lat.shape[0], w_dec.shape[0]
    sizes = [
        (hidden, genes),
        (genes, hidden),
        (genes, hidden),
        (latents, hidden),
        (hidden, latents),
        (hidden, latent),
    ]
    out = kernel_call(
        prepare_kernel,
        (),
        pair_of(full(hidden, genes)) + [full(latents, hidden), full(latent, hidden)],
        [full(*size) for size in sizes for _ in range(2)],
        [shape(*size, dtype=BF16) for size in sizes for _ in range(2)],
        6,
        after=after,
    )(w_out_t, w_enc_t, w_lat, w_dec)
    return [tuple(out[2 * k : 2 * k + 2]) for k in range(len(sizes))]


def own_kernel(main, *refs):
    *parts, pre_out, stats = refs
    rows = parts[0].shape[0]
    pre_out[:rows] = sum(part[...] for part in parts[1:main]) + parts[0][...]
    if main < len(parts):
        pre_out[rows:] = sum(part[...] for part in parts[main:])
    stats[...] = moments(pre_out[...])


def own_moments(parts, rest, after=()):
    rows, columns = parts[0].shape
    rows += rest[0].shape[0] if rest else 0
    return kernel_call(
        lambda *refs: own_kernel(len(parts), *refs),
        (),
        [full(*part.shape) for part in (*parts, *rest)],
        [full(rows, columns), full(2, rows)],
        [shape(rows, columns), shape(2, rows)],
        3,
        after=after,
    )(*parts, *rest)


def normalize(pre, vector):
    columns = vector.T
    norm = (pre - columns[:, 0:1]) * lax.rsqrt(columns[:, 1:2] + BN_EPS)
    return norm, norm * columns[:, 2:3] + columns[:, 3:4]


def latent_kernel(pre, vector, lat_high, lat_low, b_lat, noise, z_out):
    _, value = normalize(pre[...], vector[...])
    act, _ = silu_pair(value)
    lat = dot((lat_high[...], lat_low[...]), split(act), 1, 0) + b_lat[...].T
    latent = noise.shape[0]
    z_out[...] = lat[:latent] + jnp.exp(0.5 * lat[latent:]) * noise[...]


def latent_own(pre, vector, lat_pair, b_lat, noise):
    return kernel_call(
        latent_kernel,
        (),
        [full(*a.shape) for a in (pre, vector, *lat_pair, b_lat, noise)],
        full(*noise.shape),
        shape(*noise.shape),
        3,
    )(pre, vector, *lat_pair, b_lat, noise)


def sides(order, mine, other):
    left = order[0] == 0
    return jnp.concatenate(
        [jnp.where(left, mine, other), jnp.where(left, other, mine)], axis=1
    )


def hidden_kernel(order, dec_high, dec_low, mine, other, z_all, pre_out, stats,
                  sums):
    for step in range(mine.shape[0]):
        spot = order[step + 1]
        z = sides(order, mine[spot], other[spot])
        columns = pl.ds(step * TILE, TILE)
        z_all[:, columns] = z
        pre = dot((dec_high[...], dec_low[...]), split(z), 1, 0)
        pre_out[:, columns] = pre
        if step == 0:
            sums[...] = fold(pre)
        else:
            sums[...] += fold(pre)
    hidden, here = pre_out.shape
    mean = jnp.sum(sums[...], axis=1, keepdims=True) * (1.0 / here)
    sums[...] = spread(mean)
    squares = []
    for at in range(0, hidden, ROWS):
        rows = pl.ds(at, ROWS)
        total = jnp.zeros((ROWS, 128), F32)
        for step in range(mine.shape[0]):
            cent = pre_out[rows, pl.ds(step * TILE, TILE)] - wide(sums[rows, :])
            total = total + fold(cent * cent)
        squares.append(total)
    square = jnp.sum(jnp.concatenate(squares, axis=0), axis=1, keepdims=True)
    stats[...] = jnp.concatenate([mean, square], axis=1).T


def decoder_hidden(order, dec_pair, mine, other):
    hidden, latent = dec_pair[0].shape
    cells = 2 * mine.shape[0] * HALF
    return kernel_call(
        hidden_kernel,
        (1,),
        pair_of(full(hidden, latent)) + [full(*mine.shape), full(*other.shape)],
        [full(latent, cells), full(hidden, cells), full(2, hidden)],
        [shape(latent, cells), shape(hidden, cells), shape(2, hidden)],
        8,
        order=order,
        scratch=[pltpu.VMEM((hidden, 128), F32)],
    )(*dec_pair, mine, other)


def decoder_kernel(cells, order, pre, vector, z, out_high, out_low, turn_high, turn_low,
                   counts, factor, mask, b_out, w_dec,
                   recon_out, grad_high, grad_low, act_high, act_low, z_other, z_own,
                   weight_out, sums, bias_out,
                   sum_term, sum_gain, sum_grad, mean_w, scale_w, shift_w, mask_w, bias_w,
                   dec_high, dec_low, slope, product, term_high, term_low):
    step = pl.program_id(0)
    hidden, genes = out_high.shape

    @pl.when(step == 0)
    def _():
        columns = vector[...].T
        rstd = lax.rsqrt(columns[:, 1:2] + BN_EPS)
        mean_w[...] = spread(columns[:, 0:1])
        scale_w[...] = spread(rstd * columns[:, 2:3])
        shift_w[...] = spread(columns[:, 3:4])
        mask_w[...] = spread(mask[...].T * (1.0 / cells))
        bias_w[...] = spread(b_out[...].T)
        dec_high[...], dec_low[...] = split(
            w_dec[...] * (vector[2:3, :] * lax.rsqrt(vector[1:2, :] + BN_EPS))
        )
        for ref in (sum_term, sum_gain, sum_grad, weight_out):
            ref[...] = jnp.zeros_like(ref)

    for at in range(0, hidden, ROWS):
        rows = pl.ds(at, ROWS)
        cent = pre[rows, :] - wide(mean_w[rows, :])
        act, slope[rows, :] = silu_pair(
            cent * wide(scale_w[rows, :]) + wide(shift_w[rows, :])
        )
        act_high[rows, :], act_low[rows, :] = split(act)
    product[:genes, :] = dot(
        (turn_high[...], turn_low[...]), (act_high[...], act_low[...]), 1, 0
    )
    scale = factor[...]
    for at in range(0, genes, ROWS):
        rows = pl.ds(at, ROWS)
        out = product[rows, :] + wide(bias_w[rows, :])
        recon = jnp.maximum(out, 0.0) + jnp.log(1.0 + jnp.exp(-jnp.abs(out)))
        recon_out[rows, :] = recon
        grad = (recon - counts[rows, :] * scale) * (wide(mask_w[rows, :]) * sigmoid(out))
        sum_grad[rows, :] += fold(grad)
        grad_high[rows, :], grad_low[rows, :] = split(grad)
    product[:hidden, :] = dot(
        (out_high[...], out_low[...]), (grad_high[...], grad_low[...]), 1, 0
    )
    for at in range(0, hidden, ROWS):
        rows = pl.ds(at, ROWS)
        term = product[rows, :] * slope[rows, :]
        cent = pre[rows, :] - wide(mean_w[rows, :])
        sum_term[rows, :] += fold(term)
        sum_gain[rows, :] += fold(term * cent)
        term_high[rows, :], term_low[rows, :] = split(term)
    terms = term_high[...], term_low[...]
    back = dot((dec_high[...], dec_low[...]), terms, 1, 0)
    left = order[0] == 0
    z_other[...] = jnp.where(left, back[:, HALF:], back[:, :HALF])
    z_own[...] = jnp.where(left, back[:, :HALF], back[:, HALF:])
    weight_out[...] += dot(terms, split(z[...]), 1, 1)

    @pl.when(step == pl.num_programs(0) - 1)
    def _():
        rstd = lax.rsqrt(vector[1:2, :] + BN_EPS)
        both = rows_of(sum_term[...], sum_gain[...])
        sums[...] = jnp.concatenate([both[0:1], both[1:2] * rstd], axis=0)
        bias_out[...] = rows_of(sum_grad[...])


def decoder(cells, order, pre, vector, z, out_pair, turn_pair, counts, factor, mask, b_out,
            w_dec):
    hidden, genes = out_pair[0].shape
    here = counts.shape[1]
    latent = w_dec.shape[0]
    most = max(hidden, genes)
    placed = pl.BlockSpec((latent, HALF), lambda j, order: (0, order[j + 1]))
    return kernel_call(
        lambda *refs: decoder_kernel(cells, *refs),
        (here // TILE,),
        [tile(hidden), full(4, hidden), tile(latent)]
        + pair_of(full(hidden, genes))
        + pair_of(full(genes, hidden))
        + [
            tile(genes),
            tile(1),
            full(1, genes),
            full(1, genes),
            full(latent, hidden),
        ],
        [tile(genes)]
        + pair_of(tile(genes))
        + pair_of(tile(hidden))
        + pair_of(placed)
        + [full(hidden, latent), full(2, hidden), full(1, genes)],
        [shape(genes, here)]
        + [shape(genes, here, dtype=BF16)] * 2
        + [shape(hidden, here, dtype=BF16)] * 2
        + [shape(latent, here // 2)] * 2
        + [shape(hidden, latent), shape(2, hidden), shape(1, genes)],
        42,
        order=order,
        scratch=[pltpu.VMEM((hidden, 128), F32)] * 2
        + [pltpu.VMEM((genes, 128), F32)]
        + [pltpu.VMEM((hidden, 128), F32)] * 3
        + [pltpu.VMEM((genes, 128), F32)] * 2
        + [pltpu.VMEM((latent, hidden), BF16)] * 2
        + [pltpu.VMEM((hidden, TILE), F32), pltpu.VMEM((most, TILE), F32)]
        + [pltpu.VMEM((hidden, TILE), BF16)] * 2,
    )(pre, vector, z, *out_pair, *turn_pair, counts, factor, mask, b_out, w_dec)


def start_halves(order, product, outs, first):
    if len(outs) == 1:
        start_or_add(outs[0], product, first)
        return
    rows = product.shape[0] // 2
    upper = order[0] != 0

    @pl.when(upper)
    def _():
        start_or_add(outs[0], product[rows:], first)
        start_or_add(outs[1], product[:rows], first)

    @pl.when(jnp.logical_not(upper))
    def _():
        start_or_add(outs[0], product[:rows], first)
        start_or_add(outs[1], product[rows:], first)


def weight_kernel(order, left_high, left_low, right_high, right_low, *outs):
    product = dot(
        (left_high[...], left_low[...]), (right_high[...], right_low[...]), 1, 1
    )
    start_halves(order, product, outs, pl.program_id(0) == 0)


def weight_halves(order, halves, left, right, width, chunk=(0, 1), after=()):
    hidden, here = left[0].shape
    rows = hidden // halves
    place, chunks = chunk
    genes = right[0].shape[0] // chunks
    return kernel_call(
        weight_kernel,
        (here // width,),
        pair_of(pl.BlockSpec((hidden, width), lambda j, order: (0, j)))
        + pair_of(pl.BlockSpec((genes, width), lambda j, order: (place, j))),
        [full(rows, genes)] * halves,
        [shape(rows, genes)] * halves,
        14 // chunks,
        order=order,
        after=after,
    )(*left, *right)


def latent_weight_kernel(lat, part, vector, z, b_lat, out, gram, sum_out):
    first = pl.program_id(0) == 0
    _, value = normalize(part[...], vector[...])
    act, _ = silu_pair(value)
    start_or_add(out, dot(split(lat[...]), split(act), 1, 1), first)
    latent = z.shape[0]
    moved = z[...] - b_lat[:, :latent].T
    pair = split(moved)
    start_or_add(gram, dot(pair, pair, 1, 1), first)
    start_or_add(sum_out, rows_of(moved), first)


def latent_weight(lat, part, vector, z, b_lat, after=()):
    latents, here = lat.shape
    share = part.shape[0]
    latent = z.shape[0]
    return kernel_call(
        latent_weight_kernel,
        (here // TILE,),
        [tile(latents), tile(share), full(4, share), tile(latent), full(1, latents)],
        [full(latents, share), full(latent, latent), full(1, latent)],
        [shape(latents, share), shape(latent, latent), shape(1, latent)],
        4,
        after=after,
    )(lat, part, vector, z, b_lat)


def again_kernel(pre_enc, vector, lat_high, lat_low, b_lat, later,
                 lat_out, slope_out, later_out, act_high, act_low):
    later_out[...] = later[...]
    columns = vector[...].T
    scale = lax.rsqrt(columns[:, 1:2] + BN_EPS) * columns[:, 2:3]
    for at in range(0, pre_enc.shape[0], ROWS):
        rows = pl.ds(at, ROWS)
        part = slice(at, at + ROWS)
        act, slope_out[rows, :] = silu_pair(
            (pre_enc[rows, :] - columns[part, 0:1]) * scale[part] + columns[part, 3:4]
        )
        act_high[rows, :], act_low[rows, :] = split(act)
    lat_out[...] = (
        dot((lat_high[...], lat_low[...]), (act_high[...], act_low[...]), 1, 0)
        + b_lat[...].T
    )


def encode_again(pre_enc, vector, lat_pair, b_lat, later, after=()):
    hidden, here = pre_enc.shape
    latents = lat_pair[0].shape[0]
    return kernel_call(
        again_kernel,
        (here // TILE,),
        [tile(hidden), full(4, hidden)]
        + pair_of(full(latents, hidden))
        + [full(1, latents), full(*later.shape)],
        [tile(latents), tile(hidden), full(*later.shape)],
        [shape(latents, here), shape(hidden, here), shape(*later.shape)],
        10,
        scratch=[pltpu.VMEM((hidden, TILE), BF16)] * 2,
        after=after,
    )(pre_enc, vector, *lat_pair, b_lat, later)


def fix_kernel(cells, w_dec, vector, sums, b_lat, matrix_out, column_out):
    weight = w_dec[...]
    rstd = lax.rsqrt(vector[1:2, :] + BN_EPS)
    scaled = weight * (vector[2:3, :] * rstd * (1.0 / cells))
    gained = scaled * (sums[1:2, :] * rstd)
    matrix_out[...] = dot(split(gained), split(weight), 1, 1)
    bias = b_lat[:, : weight.shape[0]].T
    mean = vector[0:1, :] - jnp.sum(weight * bias, axis=0, keepdims=True)
    column_out[...] = spread(
        jnp.sum(scaled * sums[0:1, :] - gained * mean, axis=1, keepdims=True)
    )


def fix_terms(cells, w_dec, vector, sums, b_lat):
    latent, hidden = w_dec.shape
    return kernel_call(
        lambda *refs: fix_kernel(cells, *refs),
        (),
        [full(latent, hidden), full(4, hidden), full(2, hidden), full(*b_lat.shape)],
        [full(latent, latent), full(latent, 128)],
        [shape(latent, latent), shape(latent, 128)],
        2,
    )(w_dec, vector, sums, b_lat)


def latent_back_kernel(cells, order, mine, other, z, matrix, column, b_lat, lat, noise,
                       tal_high, tal_low, slope, pre, vector, grad_out, sums, lat_out, bias_out,
                       sum_grad, sum_gain, sum_lat, product):
    step = pl.program_id(0)

    @pl.when(step == 0)
    def _():
        for ref in (sum_grad, sum_gain, sum_lat):
            ref[...] = jnp.zeros_like(ref)

    latent = noise.shape[0]
    moved = z[...] - b_lat[:, :latent].T
    fix = dot(split(matrix[...]), split(moved), 1, 0) + wide(column[...])
    grad_z = sides(order, mine[:latent, :], other[:latent, :]) - fix
    mu = lat[:latent, :]
    spread_z = jnp.exp(0.5 * lat[latent:, :])
    grad_mu = grad_z + (ALPHA / cells) * mu
    grad_logvar = 0.5 * grad_z * noise[...] * spread_z + (0.5 * ALPHA / cells) * (
        spread_z * spread_z - 1.0
    )
    grad_lat = jnp.concatenate([grad_mu, grad_logvar], axis=0)
    lat_out[...] = grad_lat
    sum_lat[...] += fold(grad_lat)
    product[...] = dot((tal_high[...], tal_low[...]), split(grad_lat), 1, 0)
    mean = vector[0:1, :].T
    for at in range(0, product.shape[0], ROWS):
        rows = pl.ds(at, ROWS)
        grad = product[rows, :] * slope[rows, :]
        grad_out[rows, :] = grad
        sum_grad[rows, :] += fold(grad)
        sum_gain[rows, :] += fold(grad * (pre[rows, :] - mean[at : at + ROWS]))

    @pl.when(step == pl.num_programs(0) - 1)
    def _():
        both = rows_of(sum_grad[...], sum_gain[...])
        sums[...] = jnp.concatenate(
            [both[0:1], both[1:2] * lax.rsqrt(vector[1:2, :] + BN_EPS)], axis=0
        )
        bias_out[...] = rows_of(sum_lat[...])


def latent_back(cells, order, mine, other, z, fix, b_lat, lat, noise, tal_pair, slope, pre,
                vector, after=()):
    hidden, here = pre.shape
    latents = lat.shape[0]
    latent = noise.shape[0]
    block = pl.BlockSpec(
        (None, mine.shape[1], HALF), lambda j, order: (order[j + 1], 0, 0)
    )
    return kernel_call(
        lambda *refs: latent_back_kernel(cells, *refs),
        (here // TILE,),
        [block, block, tile(latent), full(latent, latent), full(latent, 128)]
        + [full(1, latents), tile(latents), tile(latent)]
        + pair_of(full(hidden, latents))
        + [tile(hidden), tile(hidden), full(4, hidden)],
        [tile(hidden), full(2, hidden), tile(latents), full(1, latents)],
        [
            shape(hidden, here),
            shape(2, hidden),
            shape(latents, here),
            shape(1, latents),
        ],
        12,
        order=order,
        scratch=[
            pltpu.VMEM((hidden, 128), F32),
            pltpu.VMEM((hidden, 128), F32),
            pltpu.VMEM((latents, 128), F32),
            pltpu.VMEM((hidden, TILE), F32),
        ],
        after=after,
    )(mine, other, z, *fix, b_lat, lat, noise, *tal_pair, slope, pre, vector)


def encoder_weight_kernel(cells, order, grad_in, pre, vector, scaled_high, scaled_low,
                          high, low, *outs):
    columns = vector[...].T
    scale = lax.rsqrt(columns[:, 1:2] + BN_EPS)
    outer = columns[:, 2:3] * scale
    shift = columns[:, 4:5] * (1.0 / cells)
    gain = columns[:, 5:6] * (1.0 / cells) * scale
    for at in range(0, grad_in.shape[0], ROWS):
        rows = pl.ds(at, ROWS)
        part = slice(at, at + ROWS)
        grad = outer[part] * (
            grad_in[rows, :]
            - shift[part]
            - (pre[rows, :] - columns[part, 0:1]) * gain[part]
        )
        high[rows, :], low[rows, :] = split(grad)
    product = dot((high[...], low[...]), (scaled_high[...], scaled_low[...]), 1, 1)
    start_halves(order, product, outs, pl.program_id(0) == 0)


def encoder_weight(cells, order, halves, chunks, grad_in, pre, vector, scaled):
    hidden, here = pre.shape
    genes = scaled[0].shape[0] // chunks
    rows = hidden // halves
    return kernel_call(
        lambda *refs: encoder_weight_kernel(cells, *refs),
        (here // TILE,),
        [tile(hidden), tile(hidden), full(6, hidden)] + pair_of(tile(genes)),
        pair_of(tile(hidden)) + [full(rows, genes)] * halves,
        [shape(hidden, here, dtype=BF16)] * 2 + [shape(rows, genes)] * halves,
        12,
        order=order,
    )(grad_in, pre, vector, *scaled)


def counts_kernel(cells, enc_high, enc_low, high, low, recon, counts, factor, mask, out,
                  product):
    product[...] = dot((enc_high[...], enc_low[...]), (high[...], low[...]), 1, 0)
    mask_column = mask[...].T
    scale = factor[...]
    for at in range(0, out.shape[0], ROWS):
        rows = pl.ds(at, ROWS)
        column = mask_column[at : at + ROWS]
        diff = (recon[rows, :] - counts[rows, :] * scale) * (column * (1.0 / cells))
        out[rows, :] = (product[rows, :] - diff) * (scale * column)


def counts_back(cells, enc_pair, grads, recon, counts, factor, mask, after=()):
    genes, hidden = enc_pair[0].shape
    here = counts.shape[1]
    return kernel_call(
        lambda *refs: counts_kernel(cells, *refs),
        (here // TILE,),
        pair_of(full(genes, hidden))
        + pair_of(tile(hidden))
        + [tile(genes), tile(genes), tile(1), full(1, genes)],
        tile(genes),
        shape(genes, here),
        16,
        scratch=[pltpu.VMEM((genes, TILE), F32)],
        after=after,
    )(*enc_pair, *grads, recon, counts, factor, mask)


def token_kernel(out):
    out[...] = jnp.zeros_like(out)


def token(after):
    return kernel_call(
        token_kernel, (), [], full(1, 1), shape(1, 1), 0, after=after
    )()[0, 0]


def swap(value, axis, bit):
    size = lax.axis_size(axis)
    return lax.ppermute(value, axis, [(i, i ^ bit) for i in range(size)])


def bits(axis):
    size, bit, out = lax.axis_size(axis), 1, []
    while bit < size:
        out.append(bit)
        bit *= 2
    return out


def add_all(value, axes):
    for axis in axes:
        for bit in bits(axis):
            value = value + swap(value, axis, bit)
    return value


def moments_all(both, count, axes, others=None):
    for axis in axes:
        if axis == GENE and others is not None:
            both = jnp.concatenate([both, others])
        for bit in bits(axis):
            other = swap(both, axis, bit)
            gap = both[0] - other[0]
            rows = [
                0.5 * (both[0] + other[0]),
                both[1] + other[1] + gap * gap * (0.5 * count),
            ]
            both = jnp.concatenate([jnp.stack(rows), both[2:] + other[2:]])
            count = 2 * count
    return both[0], both[1] / count, both[2:]


def rows_wide(vector, share):
    size = vector.shape[0]
    lines = -(-size // share)
    return jnp.pad(vector, (0, lines * share - size)).reshape(lines, share)


def scatter_gene_blocks(value, times):
    me = lax.axis_index(GENE)
    for place, bit in enumerate(reversed(bits(GENE))):
        half = value.shape[0] // 2
        upper = (me & bit) != 0
        sent = jnp.where(upper, value[:half], value[half:])
        kept = jnp.where(upper, value[half:], value[:half])
        value = kept + swap(sent, GENE, bit)
        if place < len(times):
            value = value + token(times[place : place + 1])
    return value[0]


def gene_pairs(links):
    return [(2 * a + y, 2 * b + y) for a, b in links for y in (0, 1)]


OUTER = gene_pairs([(0, 1), (3, 2)])
MIDDLE = gene_pairs([(1, 2), (2, 1)])
SIDES = gene_pairs([(0, 1), (1, 0), (2, 3), (3, 2)])


def line_order(z):
    low = z < 2
    return [
        jnp.where(low, z + 3, z + 1) % 4,
        (z + 2) % 4,
        jnp.where(low, z + 1, z + 3) % 4,
        z,
    ]


def by_line(here):
    return lax.axis_size(GENE) == 8 and here == 8 * HALF


def scatter_encoded(counts, factor, mask, w_enc_t, others):
    here = counts.shape[1]
    hidden = w_enc_t.shape[0]
    me = lax.axis_index(GENE)
    if not by_line(here):
        side = 0 * me
        order = jnp.arange(here // TILE, dtype=jnp.int32)
        blocks = encode_products(side, order, counts, factor, mask, w_enc_t, 0)
        pre = [blocks[3 * k + i] for k in range(len(blocks) // 3) for i in (1, 0)]
        pre = lax.psum_scatter(
            jnp.concatenate(pre, axis=1), GENE, scatter_dimension=1, tiled=True
        )
        scaled = scale_counts(counts, factor, mask, (blocks[0],))
        return [pre], [], scaled, prepare(*others, (scaled[0],))
    z, y = me // 2, me % 2
    rest = hidden // 6 // 16 * 16
    order = jnp.stack(line_order(z)).astype(jnp.int32)

    def products(first, last, after=()):
        return encode_products(
            y, order[first:last], counts, factor, mask, w_enc_t, rest, after
        )

    middle = (z == 1) | (z == 2)
    blocks = products(0, 1)
    step1 = lax.ppermute(blocks[2], GENE, OUTER)
    blocks += products(1, 2, blocks[:1])
    blocks += products(2, 4, (step1, blocks[3]))
    part = [blocks[3 * k + 1] + swap(blocks[3 * k], GENE, 1) for k in range(4)]
    tail = blocks[2::3]
    step2 = lax.ppermute(tail[1], GENE, OUTER)
    across = lax.ppermute(tail[1] + step1, GENE, MIDDLE)
    scaled = scale_counts(counts, factor, mask, (step2, across, blocks[6]))
    side = lax.ppermute(jnp.where(middle, tail[0] + across, tail[2]), GENE, SIDES)
    inner = lax.ppermute(tail[2] + step2, GENE, MIDDLE)
    weights = prepare(*others, (side, inner, scaled[0]))
    tail = tail[3] + side + inner
    left, right = tail[:, :HALF], tail[:, HALF:]
    mine = jnp.where(y == 0, left, right)
    step1 = lax.ppermute(part[0], GENE, OUTER)
    step2 = lax.ppermute(part[1], GENE, OUTER)
    across = lax.ppermute(part[1] + step1, GENE, MIDDLE)
    side = lax.ppermute(jnp.where(middle, part[0] + across, part[2]), GENE, SIDES)
    inner = lax.ppermute(part[2] + step2, GENE, MIDDLE)
    back = swap(jnp.where(y == 0, right, left), GENE, 1)
    return [part[3], side, inner], [mine, back], scaled, weights


def gather_blocks(value, before=None):
    rows, own = value.shape
    if not by_line(own * lax.axis_size(GENE)):
        value = lax.all_gather(value, GENE, axis=1, tiled=True)
        blocks = value.shape[1] // TILE
        stack = jnp.moveaxis(value.reshape(rows, blocks, 2, HALF), 0, 2)
        order = jnp.concatenate([jnp.zeros(1), jnp.arange(blocks)])
        return stack[:, 0], stack[:, 1], order.astype(jnp.int32)
    me = lax.axis_index(GENE)
    mine = jnp.stack([value] + [swap(value, GENE, bit) for bit in (2, 4, 6)])
    if before is not None:
        mine = mine + token(before)
    other = swap(mine, GENE, 1)
    order = jnp.concatenate([(me % 2)[None], (me // 2) ^ jnp.arange(4)])
    return mine, other, order.astype(jnp.int32)


def term_order(here):
    blocks = jnp.arange(here // TILE)
    if not by_line(here):
        return jnp.concatenate([jnp.zeros(1), blocks]).astype(jnp.int32)
    me = lax.axis_index(GENE)
    return jnp.concatenate([(me % 2)[None], ((me // 2 ^ blocks) + 3) % 4]).astype(
        jnp.int32
    )


def scatter_sides(other, own, sums):
    rows, half = own.shape
    if not by_line(2 * half):
        value = jnp.stack(
            [own.reshape(rows, -1, HALF), other.reshape(rows, -1, HALF)], axis=2
        ).reshape(rows, 2 * half)
        return value, add_all(sums, (BATCH, GENE))
    z = lax.axis_index(GENE) // 2
    sums = add_all(sums, (BATCH,))
    sums = sums + swap(sums, GENE, 1)
    quarter = sums.shape[1] // 4
    quarters = [
        jnp.pad(
            lax.dynamic_slice_in_dim(sums, (z ^ k) * quarter, quarter, 1),
            ((0, 0), (0, HALF - quarter)),
        )
        for k in (1, 2, 3, 0)
    ]
    return jnp.concatenate(
        [own + swap(other, GENE, 1), jnp.concatenate(quarters, axis=1)], axis=0
    ), sums


def scatter_terms(part, before):
    if not by_line(2 * part.shape[1]):
        return lax.psum_scatter(part, GENE, scatter_dimension=1, tiled=True)
    total = part[:, 3 * HALF :] + token(before)
    for k in (1, 2, 3):
        total = total + swap(part[:, (k - 1) * HALF : k * HALF], GENE, 2 * k)
    return total


def gather_sums(stack, sums):
    if stack.shape[0] != 4 or not by_line(8 * stack.shape[2]):
        return sums
    z = lax.axis_index(GENE) // 2
    quarter = sums.shape[1] // 4
    quarters = stack[:, -sums.shape[0] :, :quarter]
    return jnp.concatenate(
        [
            lax.dynamic_index_in_dim(quarters, z ^ place, 0, keepdims=False)
            for place in range(4)
        ],
        axis=1,
    )


def add_cores(chunks, zero):
    if len(chunks[0]) == 1:
        return chunks
    return [own + swap(other, BATCH, 1) + zero for other, own in chunks]


def swap_chips(part, zero=0.0):
    if lax.axis_size(BATCH) != 4:
        return part
    return part + swap(part, BATCH, 2) + zero


def join_cores(order, chunks):
    if lax.axis_size(BATCH) != 4:
        return lax.psum(jnp.concatenate([chunk[0] for chunk in chunks], axis=1), BATCH)
    low = order[0] != 0
    other = [swap(part, BATCH, 1) for part in chunks]
    return jnp.concatenate(
        [
            jnp.concatenate([jnp.where(low, a, b), jnp.where(low, b, a)], axis=0)
            for a, b in zip(chunks, other)
        ],
        axis=1,
    )


def on_device(
    counts_in,
    umi_total,
    gene_mask,
    noise,
    w_enc,
    gain_enc,
    shift_enc,
    w_lat,
    b_lat,
    w_dec,
    gain_dec,
    shift_dec,
    w_out,
    b_out,
    mean_enc,
    var_enc,
    mean_dec,
    var_dec,
):
    here = counts_in.shape[1]
    cells = here * lax.axis_size(BATCH)
    hidden = w_enc.shape[1]
    ranks = lax.axis_size(GENE)
    share = hidden // ranks
    own = here // ranks
    latent = noise.shape[0]
    me = lax.axis_index(GENE)
    both = (BATCH, GENE)
    core = lax.axis_index(BATCH) % 2
    halves = 2 if lax.axis_size(BATCH) == 4 else 1
    order = (1 - core).astype(jnp.int32)[None]

    def hidden_part(vector):
        return lax.dynamic_slice_in_dim(vector, me * share, share, vector.ndim - 1)

    def hidden_placed(part):
        empty = jnp.zeros((part.shape[0], hidden), F32)
        return lax.dynamic_update_slice_in_dim(empty, part, me * share, 1)

    factor = (UMI_SCALE / umi_total.astype(F32))[None, :]
    mask = gene_mask.astype(F32)[None, :]
    w_enc_t = w_enc.T
    w_out_t = w_out.T
    b_lat_row = b_lat[None, :]
    noise_own = lax.dynamic_slice_in_dim(noise, me * own, own, 1)

    parts, rest, scaled, weights = scatter_encoded(
        counts_in, factor, mask, w_enc_t, (w_out_t, w_enc_t, w_lat, w_dec)
    )
    out_pair, turn_pair, enc_pair, lat_pair, tal_pair, dec_pair = weights
    affine1 = hidden_placed(jnp.stack([gain_enc, shift_enc]))
    pre_own, stats1 = own_moments(
        parts, rest, after=(affine1, noise_own, out_pair[0])
    )
    pre_enc = lax.all_gather(pre_own, GENE, axis=1, tiled=True)
    mean1, var1, affine1 = moments_all(stats1, own, both, affine1)
    vector1 = jnp.concatenate([mean1[None], var1[None], affine1])
    z_own = latent_own(pre_own, vector1, lat_pair, b_lat_row, noise_own)

    z_mine, z_other, z_order = gather_blocks(z_own)
    z, pre_dec, stats2 = decoder_hidden(z_order, dec_pair, z_mine, z_other)
    mean2, var2, _ = moments_all(stats2, here, (BATCH,))
    vector2 = jnp.stack([mean2, var2, gain_dec, shift_dec])
    recon, grad_high, grad_low, act_high, act_low, *terms, term_w_dec, sums2, grad_b_out = (
        decoder(
            cells, term_order(here), pre_dec, vector2, z, out_pair, turn_pair, counts_in,
            factor, mask, b_out[None, :], w_dec
        )
    )

    part, sums2 = scatter_sides(*terms, sums2)
    grad_w_out = weight_halves(
        order, halves, (act_high, act_low), (grad_high, grad_low), 1024, after=(part,)
    )
    total = scatter_terms(part, (grad_w_out[0],))
    zero = token((total,))
    grad_w_out = add_cores([[grad_w_out[0] + zero, *grad_w_out[1:]]], 0.0)
    lat, slope1, term_w_dec = encode_again(
        pre_enc, vector1, lat_pair, b_lat_row, term_w_dec
    )
    term_mine, term_other, z_order = gather_blocks(total, (lat,))
    sums2 = gather_sums(term_mine, sums2)
    fix_z = fix_terms(cells, w_dec, vector2, sums2, b_lat_row)

    grad_in1, sums1, grad_lat, grad_b_lat = latent_back(
        cells, z_order, term_mine, term_other, z, fix_z, b_lat_row, lat, noise, tal_pair,
        slope1, pre_enc, vector1
    )
    if halves == 2:
        cuts = [0, 256, 512, counts_in.shape[0]]
        times = [lat, term_mine, grad_lat]
        grad_w_out = [
            swap_chips(grad_w_out[0][:, a:b], token((time,)))
            for a, b, time in zip(cuts, cuts[1:], times)
        ]
    sums1 = add_all(
        jnp.concatenate([sums1.reshape(-1), grad_b_lat[0], grad_b_out[0]]),
        (BATCH,),
    )
    grad_b_lat = sums1[2 * hidden : 2 * hidden + 2 * latent]
    grad_b_out = sums1[2 * hidden + 2 * latent :]
    sums1 = sums1[: 2 * hidden].reshape(2, hidden)
    grad_w_lat, gram_z, sum_z = latent_weight(
        grad_lat, lax.dynamic_slice_in_dim(pre_enc, me * share, share, 0),
        hidden_part(vector1), z, b_lat_row
    )
    vector6 = jnp.concatenate([vector1, sums1])
    chunks = 2 if counts_in.shape[0] % 32 == 0 and halves == 2 else 1
    high, low, *weight_part = encoder_weight(
        cells, order, halves, chunks, grad_in1, pre_enc, vector6, scaled
    )
    term_w_dec = scatter_gene_blocks(
        term_w_dec.reshape(ranks, share, latent), (grad_lat, grad_w_lat, high)
    ).T
    small = jnp.concatenate(
        [
            term_w_dec,
            grad_w_lat,
            rows_wide(gram_z.reshape(-1), share),
            rows_wide(sum_z[0], share),
        ]
    )
    small = small + swap(small, BATCH, 1)

    weight_parts = [weight_part]
    for chunk in range(1, chunks):
        weight_parts.append(
            weight_halves(
                order, halves, (high, low), scaled, 1024, (chunk, chunks), (small,)
            )
        )
    for bit in bits(BATCH)[1:]:
        small = small + swap(small, BATCH, bit)

    weight_parts = add_cores(weight_parts, token((small,)))
    grad_counts = counts_back(
        cells, enc_pair, (high, low), recon, counts_in, factor, mask,
        after=[x for x in weight_parts if halves == 2]
    )
    grad_w_out = join_cores(order, grad_w_out).T
    zero = token((grad_counts,))
    weight_parts = [swap_chips(part, zero) for part in weight_parts]
    grad_w_enc = join_cores(order, weight_parts).T
    term_w_dec = small[:latent]
    grad_w_lat = small[latent : 3 * latent]
    lines = -(-latent // share)
    gram_z = small[3 * latent : -lines].reshape(-1)[: latent * latent]
    gram_z = gram_z.reshape(latent, latent)
    sum_z = small[-lines:].reshape(-1)[:latent]
    grad_shift2 = hidden_part(sums2[0])
    grad_gain2 = hidden_part(sums2[1])
    rstd2 = hidden_part(lax.rsqrt(var2 + BN_EPS))
    cov_z = gram_z - sum_z[:, None] * (sum_z / cells)[None, :]
    pair_w_dec = rstd2[None, :] * jnp.dot(
        cov_z, hidden_part(w_dec), precision=lax.Precision.HIGHEST
    )
    sum_z = sum_z + cells * b_lat[:latent]
    grad_w_dec = (hidden_part(gain_dec) * rstd2)[None, :] * (
        term_w_dec
        - sum_z[:, None] * (grad_shift2 / cells)[None, :]
        - pair_w_dec * (grad_gain2 / cells)[None, :]
    )

    correct = cells / (cells - 1.0)
    new_mean_enc = (1.0 - MOMENTUM) * mean_enc + MOMENTUM * hidden_part(mean1)
    new_var_enc = (1.0 - MOMENTUM) * var_enc + MOMENTUM * hidden_part(var1) * correct
    new_mean_dec = (1.0 - MOMENTUM) * mean_dec + MOMENTUM * mean2
    new_var_dec = (1.0 - MOMENTUM) * var_dec + MOMENTUM * var2 * correct
    return (
        recon,
        grad_counts,
        grad_w_enc,
        hidden_part(sums1[1]),
        hidden_part(sums1[0]),
        grad_w_lat,
        grad_b_lat,
        grad_w_dec,
        grad_gain2,
        grad_shift2,
        grad_w_out,
        grad_b_out,
        new_mean_enc,
        new_var_enc,
        new_mean_dec,
        new_var_dec,
    )


def solution(mesh):
    return jax.shard_map(
        on_device,
        mesh=mesh,
        in_specs=(
            P(GENE, BATCH),
            P(BATCH),
            P(GENE),
            P(None, BATCH),
            P(GENE, None),
            P(GENE),
            P(GENE),
            P(),
            P(),
            P(),
            P(),
            P(),
            P(GENE, None),
            P(GENE),
            P(GENE),
            P(GENE),
            P(),
            P(),
        ),
        out_specs=(
            P(GENE, BATCH),
            P(GENE, BATCH),
            P(GENE, None),
            P(GENE),
            P(GENE),
            P(None, GENE),
            P(),
            P(None, GENE),
            P(GENE),
            P(GENE),
            P(GENE, None),
            P(GENE),
            P(GENE),
            P(GENE),
            P(),
            P(),
        ),
        check_vma=False,
    )
```

```python
import jax
import jax.numpy as jnp
from jax import lax
from jax.experimental import pallas as pl
from jax.experimental.pallas import tpu as pltpu
from jax.sharding import PartitionSpec as P

ALPHA = 0.002
BN_EPS = 1e-05
MOMENTUM = 0.1
UMI_SCALE = 10000.0
BATCH = "batch"
GENE = "gene"
TILE = 512
HALF = 256
ROWS = 16
VMEM_BYTES = 56 << 20
F32 = jnp.float32


BF16 = jnp.bfloat16
RATE = 600_000_000


def split(value):
    high = value.astype(BF16)
    return high, (value - high.astype(F32)).astype(BF16)


def whole(pair):
    return pair[0].astype(F32) + pair[1].astype(F32)


def dot(left, right, left_dim, right_dim):
    def one(a, b):
        return lax.dot_general(
            a,
            b,
            (((left_dim,), (right_dim,)), ((), ())),
            preferred_element_type=F32,
        )

    return one(left[0], right[0]) + (one(left[0], right[1]) + one(left[1], right[0]))


def kernel_call(
    body, grid, in_specs, out_specs, out_shape, micros, order=None, scratch=(), after=(),
    onto=(),
):
    leading = 0 if order is None else 1
    held = leading + len(in_specs)

    def run(*refs):
        body(*refs[:held], *refs[held + len(after) :])

    call = pl.pallas_call(
        run,
        grid_spec=pltpu.PrefetchScalarGridSpec(
            num_scalar_prefetch=leading,
            grid=grid,
            in_specs=list(in_specs) + [pl.BlockSpec(memory_space=pl.ANY)] * len(after),
            out_specs=out_specs,
            scratch_shapes=list(scratch),
        ),
        out_shape=out_shape,
        input_output_aliases={held + k: out for k, out in enumerate(onto)},
        compiler_params=pltpu.CompilerParams(vmem_limit_bytes=VMEM_BYTES),
        cost_estimate=pl.CostEstimate(
            flops=int(micros * RATE), bytes_accessed=1024, transcendentals=0
        ),
    )
    prefetch = () if order is None else (order,)
    return lambda *args: call(*prefetch, *args, *after)


def shape(*dims, dtype=F32):
    return jax.ShapeDtypeStruct(dims, dtype)


def full(*dims):
    return pl.BlockSpec(dims, lambda *_: (0,) * len(dims))


def tile(rows):
    return pl.BlockSpec((rows, TILE), lambda j, *_: (0, j))


def pair_of(spec):
    return [spec, spec]


def sigmoid(value):
    return 0.5 * jnp.tanh(0.5 * value) + 0.5


def silu_pair(value):
    sig = sigmoid(value)
    act = value * sig
    return act, sig + act * (1.0 - sig)


def start_or_add(ref, value, first):
    @pl.when(first)
    def _():
        ref[...] = value

    @pl.when(jnp.logical_not(first))
    def _():
        ref[...] += value


def fold(value):
    width = value.shape[1]
    if width % 128:
        return jnp.broadcast_to(
            jnp.sum(value, axis=1, keepdims=True) / 128.0, (value.shape[0], 128)
        )
    return sum(
        value[:, at : at + 128] for at in range(128, width, 128)
    ) + value[:, :128] if width > 128 else value


def rows_of(*folded):
    return jnp.concatenate(
        [jnp.sum(value, axis=1, keepdims=True) for value in folded], axis=1
    ).T


def moments(pre):
    mean = jnp.mean(pre, axis=1, keepdims=True)
    cent = pre - mean
    return jnp.concatenate(
        [mean, jnp.sum(cent * cent, axis=1, keepdims=True)], axis=1
    ).T


def wide(column):
    return jnp.concatenate([column] * (TILE // 128), axis=1)


def spread(column):
    return jnp.broadcast_to(column, (column.shape[0], 128))


def split_scaled(counts, factor, mask, high, low):
    column = mask[...].T
    scale = factor[...]
    for at in range(0, counts.shape[0], ROWS):
        rows = pl.ds(at, ROWS)
        high[rows, :], low[rows, :] = split(
            counts[rows, :] * scale * column[at : at + ROWS]
        )


def gene_cuts(genes):
    return [0, 512, genes] if genes > 512 else [0, genes]


def turn_kernel(counts, factor, mask, *outs):
    turned = counts[...].T * factor[...].T * mask[...]
    cuts = gene_cuts(turned.shape[1])
    for place, (begin, end) in enumerate(zip(cuts, cuts[1:])):
        outs[2 * place][...], outs[2 * place + 1][...] = split(turned[:, begin:end])


def turn_counts(counts, factor, mask, after):
    genes, here = counts.shape
    cuts = gene_cuts(genes)
    widths = [end - begin for begin, end in zip(cuts, cuts[1:]) for _ in range(2)]
    out = kernel_call(
        turn_kernel,
        (here // TILE,),
        [tile(genes), tile(1), full(1, genes)],
        [pl.BlockSpec((TILE, width), lambda j: (j, 0)) for width in widths],
        [shape(here, width, dtype=BF16) for width in widths],
        5,
        after=after,
    )(counts, factor, mask)
    return [tuple(out[2 * k : 2 * k + 2]) for k in range(len(out) // 2)]


def encode_kernel(order, counts, factor, mask, w_enc_t, *refs):
    *outs, high, low, scaled_high, scaled_low = refs
    step = pl.program_id(0)

    @pl.when(step == 0)
    def _():
        for at in range(0, high.shape[0], ROWS):
            rows = pl.ds(at, ROWS)
            high[rows, :], low[rows, :] = split(w_enc_t[rows, :])

    split_scaled(counts, factor, mask, scaled_high, scaled_low)
    product = dot(
        (high[...], low[...]), (scaled_high[...], scaled_low[...]), 1, 0
    )
    side = order[0] == 0
    for place in range(len(outs) // 3):
        other, own, both = outs[3 * place : 3 * place + 3]
        rows = other.shape[0]

        @pl.when(step == place)
        def _():
            if rows < product.shape[0]:
                both[...] = product[rows:]

        @pl.when((step == place) & side)
        def _():
            other[...] = product[:rows, HALF:]
            own[...] = product[:rows, :HALF]

        @pl.when((step == place) & jnp.logical_not(side))
        def _():
            other[...] = product[:rows, :HALF]
            own[...] = product[:rows, HALF:]


def encode_products(side, order, counts, factor, mask, w_enc_t, rest, after=()):
    genes = counts.shape[0]
    hidden = w_enc_t.shape[0]
    blocks = order.shape[0]
    cells = lambda j, order: (0, order[j + 1])
    sizes = [(hidden - rest, HALF)] * 2 + [(max(rest, 8), TILE)]
    return kernel_call(
        encode_kernel,
        (blocks,),
        [
            pl.BlockSpec((genes, TILE), cells),
            pl.BlockSpec((1, TILE), cells),
            full(1, genes),
            full(hidden, genes),
        ],
        [full(*size) for size in sizes] * blocks,
        [shape(*size) for size in sizes] * blocks,
        4 * blocks,
        order=jnp.concatenate([side[None], order]).astype(jnp.int32),
        scratch=[pltpu.VMEM((hidden, genes), BF16)] * 2
        + [pltpu.VMEM((genes, TILE), BF16)] * 2,
        after=after,
    )(counts, factor, mask, w_enc_t)


def prepare_kernel(w_out_t, w_enc_t, w_lat, w_dec, out_high, out_low, turn_high, turn_low,
                   enc_high, enc_low, lat_high, lat_low, tal_high, tal_low,
                   dec_high, dec_low):
    out_high[...], out_low[...] = split(w_out_t[...])
    turn_high[...], turn_low[...] = split(w_out_t[...].T)
    enc_high[...], enc_low[...] = split(w_enc_t[...].T)
    lat_high[...], lat_low[...] = split(w_lat[...])
    tal_high[...], tal_low[...] = split(w_lat[...].T)
    dec_high[...], dec_low[...] = split(w_dec[...].T)


def prepare(w_out_t, w_enc_t, w_lat, w_dec, after):
    hidden, genes = w_out_t.shape
    latents, latent = w_lat.shape[0], w_dec.shape[0]
    sizes = [
        (hidden, genes),
        (genes, hidden),
        (genes, hidden),
        (latents, hidden),
        (hidden, latents),
        (hidden, latent),
    ]
    out = kernel_call(
        prepare_kernel,
        (),
        pair_of(full(hidden, genes)) + [full(latents, hidden), full(latent, hidden)],
        [full(*size) for size in sizes for _ in range(2)],
        [shape(*size, dtype=BF16) for size in sizes for _ in range(2)],
        6,
        after=after,
    )(w_out_t, w_enc_t, w_lat, w_dec)
    return [tuple(out[2 * k : 2 * k + 2]) for k in range(len(sizes))]


def own_kernel(main, *refs):
    *parts, pre_out, stats = refs
    rows = parts[0].shape[0]
    pre_out[:rows] = sum(part[...] for part in parts[1:main]) + parts[0][...]
    if main < len(parts):
        pre_out[rows:] = sum(part[...] for part in parts[main:])
    stats[...] = moments(pre_out[...])


def own_moments(parts, rest, after=()):
    rows, columns = parts[0].shape
    rows += rest[0].shape[0] if rest else 0
    return kernel_call(
        lambda *refs: own_kernel(len(parts), *refs),
        (),
        [full(*part.shape) for part in (*parts, *rest)],
        [full(rows, columns), full(2, rows)],
        [shape(rows, columns), shape(2, rows)],
        3,
        after=after,
    )(*parts, *rest)


def normalize(pre, vector):
    columns = vector.T
    norm = (pre - columns[:, 0:1]) * lax.rsqrt(columns[:, 1:2] + BN_EPS)
    return norm, norm * columns[:, 2:3] + columns[:, 3:4]


def latent_kernel(pre, vector, lat_high, lat_low, b_lat, noise, z_out):
    _, value = normalize(pre[...], vector[...])
    act, _ = silu_pair(value)
    lat = dot((lat_high[...], lat_low[...]), split(act), 1, 0) + b_lat[...].T
    latent = noise.shape[0]
    z_out[...] = lat[:latent] + jnp.exp(0.5 * lat[latent:]) * noise[...]


def latent_own(pre, vector, lat_pair, b_lat, noise):
    return kernel_call(
        latent_kernel,
        (),
        [full(*a.shape) for a in (pre, vector, *lat_pair, b_lat, noise)],
        full(*noise.shape),
        shape(*noise.shape),
        3,
    )(pre, vector, *lat_pair, b_lat, noise)


def sides(order, mine, other):
    left = order[0] == 0
    return jnp.concatenate(
        [jnp.where(left, mine, other), jnp.where(left, other, mine)], axis=1
    )


def hidden_kernel(order, dec_high, dec_low, mine, other, z_all, pre_out, stats,
                  sums):
    for step in range(mine.shape[0]):
        spot = order[step + 1]
        z = sides(order, mine[spot], other[spot])
        columns = pl.ds(step * TILE, TILE)
        z_all[:, columns] = z
        pre = dot((dec_high[...], dec_low[...]), split(z), 1, 0)
        pre_out[:, columns] = pre
        if step == 0:
            sums[...] = fold(pre)
        else:
            sums[...] += fold(pre)
    hidden, here = pre_out.shape
    mean = jnp.sum(sums[...], axis=1, keepdims=True) * (1.0 / here)
    sums[...] = spread(mean)
    squares = []
    for at in range(0, hidden, ROWS):
        rows = pl.ds(at, ROWS)
        total = jnp.zeros((ROWS, 128), F32)
        for step in range(mine.shape[0]):
            cent = pre_out[rows, pl.ds(step * TILE, TILE)] - wide(sums[rows, :])
            total = total + fold(cent * cent)
        squares.append(total)
    square = jnp.sum(jnp.concatenate(squares, axis=0), axis=1, keepdims=True)
    stats[...] = jnp.concatenate([mean, square], axis=1).T


def decoder_hidden(order, dec_pair, mine, other):
    hidden, latent = dec_pair[0].shape
    cells = 2 * mine.shape[0] * HALF
    return kernel_call(
        hidden_kernel,
        (1,),
        pair_of(full(hidden, latent)) + [full(*mine.shape), full(*other.shape)],
        [full(latent, cells), full(hidden, cells), full(2, hidden)],
        [shape(latent, cells), shape(hidden, cells), shape(2, hidden)],
        8,
        order=order,
        scratch=[pltpu.VMEM((hidden, 128), F32)],
    )(*dec_pair, mine, other)


def decoder_kernel(cells, order, pre, vector, z, out_high, out_low, turn_high, turn_low,
                   counts, factor, mask, b_out, w_dec,
                   recon_out, grad_high, grad_low, act_high, act_low, z_other, z_own,
                   weight_out, sums, bias_out,
                   sum_term, sum_gain, sum_grad, mean_w, scale_w, shift_w, mask_w, bias_w,
                   dec_high, dec_low, slope, product, term_high, term_low):
    step = pl.program_id(0)
    hidden, genes = out_high.shape

    @pl.when(step == 0)
    def _():
        columns = vector[...].T
        rstd = lax.rsqrt(columns[:, 1:2] + BN_EPS)
        mean_w[...] = spread(columns[:, 0:1])
        scale_w[...] = spread(rstd * columns[:, 2:3])
        shift_w[...] = spread(columns[:, 3:4])
        mask_w[...] = spread(mask[...].T * (1.0 / cells))
        bias_w[...] = spread(b_out[...].T)
        dec_high[...], dec_low[...] = split(
            w_dec[...] * (vector[2:3, :] * lax.rsqrt(vector[1:2, :] + BN_EPS))
        )
        for ref in (sum_term, sum_gain, sum_grad, weight_out):
            ref[...] = jnp.zeros_like(ref)

    for at in range(0, hidden, ROWS):
        rows = pl.ds(at, ROWS)
        cent = pre[rows, :] - wide(mean_w[rows, :])
        act, slope[rows, :] = silu_pair(
            cent * wide(scale_w[rows, :]) + wide(shift_w[rows, :])
        )
        act_high[rows, :], act_low[rows, :] = split(act)
    product[:genes, :] = dot(
        (turn_high[...], turn_low[...]), (act_high[...], act_low[...]), 1, 0
    )
    scale = factor[...]
    for at in range(0, genes, ROWS):
        rows = pl.ds(at, ROWS)
        out = product[rows, :] + wide(bias_w[rows, :])
        recon = jnp.maximum(out, 0.0) + jnp.log(1.0 + jnp.exp(-jnp.abs(out)))
        recon_out[rows, :] = recon
        grad = (recon - counts[rows, :] * scale) * (wide(mask_w[rows, :]) * sigmoid(out))
        sum_grad[rows, :] += fold(grad)
        grad_high[rows, :], grad_low[rows, :] = split(grad)
    product[:hidden, :] = dot(
        (out_high[...], out_low[...]), (grad_high[...], grad_low[...]), 1, 0
    )
    for at in range(0, hidden, ROWS):
        rows = pl.ds(at, ROWS)
        term = product[rows, :] * slope[rows, :]
        cent = pre[rows, :] - wide(mean_w[rows, :])
        sum_term[rows, :] += fold(term)
        sum_gain[rows, :] += fold(term * cent)
        term_high[rows, :], term_low[rows, :] = split(term)
    terms = term_high[...], term_low[...]
    back = dot((dec_high[...], dec_low[...]), terms, 1, 0)
    left = order[0] == 0
    z_other[...] = jnp.where(left, back[:, HALF:], back[:, :HALF])
    z_own[...] = jnp.where(left, back[:, :HALF], back[:, HALF:])
    weight_out[...] += dot(terms, split(z[...]), 1, 1)

    @pl.when(step == pl.num_programs(0) - 1)
    def _():
        rstd = lax.rsqrt(vector[1:2, :] + BN_EPS)
        both = rows_of(sum_term[...], sum_gain[...])
        sums[...] = jnp.concatenate([both[0:1], both[1:2] * rstd], axis=0)
        bias_out[...] = rows_of(sum_grad[...])


def decoder(cells, order, pre, vector, z, out_pair, turn_pair, counts, factor, mask, b_out,
            w_dec):
    hidden, genes = out_pair[0].shape
    here = counts.shape[1]
    latent = w_dec.shape[0]
    most = max(hidden, genes)
    placed = pl.BlockSpec((latent, HALF), lambda j, order: (0, order[j + 1]))
    return kernel_call(
        lambda *refs: decoder_kernel(cells, *refs),
        (here // TILE,),
        [tile(hidden), full(4, hidden), tile(latent)]
        + pair_of(full(hidden, genes))
        + pair_of(full(genes, hidden))
        + [
            tile(genes),
            tile(1),
            full(1, genes),
            full(1, genes),
            full(latent, hidden),
        ],
        [tile(genes)]
        + pair_of(tile(genes))
        + pair_of(tile(hidden))
        + pair_of(placed)
        + [full(hidden, latent), full(2, hidden), full(1, genes)],
        [shape(genes, here)]
        + [shape(genes, here, dtype=BF16)] * 2
        + [shape(hidden, here, dtype=BF16)] * 2
        + [shape(latent, here // 2)] * 2
        + [shape(hidden, latent), shape(2, hidden), shape(1, genes)],
        42,
        order=order,
        scratch=[pltpu.VMEM((hidden, 128), F32)] * 2
        + [pltpu.VMEM((genes, 128), F32)]
        + [pltpu.VMEM((hidden, 128), F32)] * 3
        + [pltpu.VMEM((genes, 128), F32)] * 2
        + [pltpu.VMEM((latent, hidden), BF16)] * 2
        + [pltpu.VMEM((hidden, TILE), F32), pltpu.VMEM((most, TILE), F32)]
        + [pltpu.VMEM((hidden, TILE), BF16)] * 2,
    )(pre, vector, z, *out_pair, *turn_pair, counts, factor, mask, b_out, w_dec)


def start_halves(order, product, outs, first):
    if len(outs) == 1:
        start_or_add(outs[0], product, first)
        return
    rows = product.shape[0] // 2
    upper = order[0] != 0

    @pl.when(upper)
    def _():
        start_or_add(outs[0], product[rows:], first)
        start_or_add(outs[1], product[:rows], first)

    @pl.when(jnp.logical_not(upper))
    def _():
        start_or_add(outs[0], product[:rows], first)
        start_or_add(outs[1], product[rows:], first)


def weight_kernel(right_dim, order, left_high, left_low, right_high, right_low, *outs):
    product = dot(
        (left_high[...], left_low[...]), (right_high[...], right_low[...]), 1, right_dim
    )
    start_halves(order, product, outs, pl.program_id(0) == 0)


def weight_halves(order, halves, left, right, right_dim, width, after=()):
    hidden, here = left[0].shape
    rows = hidden // halves
    genes = right[0].shape[1 - right_dim]
    if right_dim:
        cells = pl.BlockSpec((genes, width), lambda j, order: (0, j))
    else:
        cells = pl.BlockSpec((width, genes), lambda j, order: (j, 0))
    return kernel_call(
        lambda *refs: weight_kernel(right_dim, *refs),
        (here // width,),
        pair_of(pl.BlockSpec((hidden, width), lambda j, order: (0, j))) + pair_of(cells),
        [full(rows, genes)] * halves,
        [shape(rows, genes)] * halves,
        10,
        order=order,
        after=after,
    )(*left, *right)


def latent_weight_kernel(lat, part, vector, out):
    _, value = normalize(part[...], vector[...])
    act, _ = silu_pair(value)
    product = dot(split(lat[...]), split(act), 1, 1)
    start_or_add(out, product, pl.program_id(0) == 0)


def latent_weight(lat, part, vector):
    latents, here = lat.shape
    share = part.shape[0]
    return kernel_call(
        latent_weight_kernel,
        (here // 1024,),
        [
            pl.BlockSpec((latents, 1024), lambda j: (0, j)),
            pl.BlockSpec((share, 1024), lambda j: (0, j)),
            full(4, share),
        ],
        full(latents, share),
        shape(latents, share),
        4,
    )(lat, part, vector)


def again_kernel(pre_enc, vector, lat_high, lat_low, b_lat, z, later,
                 lat_out, slope_out, gram, sum_out, later_out, act_high, act_low):
    later_out[...] = later[...]
    first = pl.program_id(0) == 0
    moved = z[...] - b_lat[:, : z.shape[0]].T
    pair = split(moved)
    start_or_add(gram, dot(pair, pair, 1, 1), first)
    start_or_add(sum_out, rows_of(moved), first)
    columns = vector[...].T
    scale = lax.rsqrt(columns[:, 1:2] + BN_EPS) * columns[:, 2:3]
    for at in range(0, pre_enc.shape[0], ROWS):
        rows = pl.ds(at, ROWS)
        part = slice(at, at + ROWS)
        act, slope_out[rows, :] = silu_pair(
            (pre_enc[rows, :] - columns[part, 0:1]) * scale[part] + columns[part, 3:4]
        )
        act_high[rows, :], act_low[rows, :] = split(act)
    lat_out[...] = (
        dot((lat_high[...], lat_low[...]), (act_high[...], act_low[...]), 1, 0)
        + b_lat[...].T
    )


def encode_again(pre_enc, vector, lat_pair, b_lat, z, later, after=()):
    latent = z.shape[0]
    hidden, here = pre_enc.shape
    latents = lat_pair[0].shape[0]
    return kernel_call(
        again_kernel,
        (here // TILE,),
        [tile(hidden), full(4, hidden)]
        + pair_of(full(latents, hidden))
        + [full(1, latents), tile(latent), full(*later.shape)],
        [
            tile(latents),
            tile(hidden),
            full(latent, latent),
            full(1, latent),
            full(*later.shape),
        ],
        [
            shape(latents, here),
            shape(hidden, here),
            shape(latent, latent),
            shape(1, latent),
            shape(*later.shape),
        ],
        10,
        scratch=[pltpu.VMEM((hidden, TILE), BF16)] * 2,
        after=after,
    )(pre_enc, vector, *lat_pair, b_lat, z, later)


def fix_kernel(cells, w_dec, vector, sums, b_lat, matrix_out, column_out):
    weight = w_dec[...]
    rstd = lax.rsqrt(vector[1:2, :] + BN_EPS)
    scaled = weight * (vector[2:3, :] * rstd * (1.0 / cells))
    gained = scaled * (sums[1:2, :] * rstd)
    matrix_out[...] = dot(split(gained), split(weight), 1, 1)
    bias = b_lat[:, : weight.shape[0]].T
    mean = vector[0:1, :] - jnp.sum(weight * bias, axis=0, keepdims=True)
    column_out[...] = spread(
        jnp.sum(scaled * sums[0:1, :] - gained * mean, axis=1, keepdims=True)
    )


def fix_terms(cells, w_dec, vector, sums, b_lat):
    latent, hidden = w_dec.shape
    return kernel_call(
        lambda *refs: fix_kernel(cells, *refs),
        (),
        [full(latent, hidden), full(4, hidden), full(2, hidden), full(*b_lat.shape)],
        [full(latent, latent), full(latent, 128)],
        [shape(latent, latent), shape(latent, 128)],
        2,
    )(w_dec, vector, sums, b_lat)


def latent_back_kernel(cells, order, mine, other, z, matrix, column, b_lat, lat, noise,
                       tal_high, tal_low, slope, pre, vector, grad_out, sums, lat_out, bias_out,
                       sum_grad, sum_gain, sum_lat, product):
    step = pl.program_id(0)

    @pl.when(step == 0)
    def _():
        for ref in (sum_grad, sum_gain, sum_lat):
            ref[...] = jnp.zeros_like(ref)

    latent = noise.shape[0]
    moved = z[...] - b_lat[:, :latent].T
    fix = dot(split(matrix[...]), split(moved), 1, 0) + wide(column[...])
    grad_z = sides(order, mine[:latent, :], other[:latent, :]) - fix
    mu = lat[:latent, :]
    spread_z = jnp.exp(0.5 * lat[latent:, :])
    grad_mu = grad_z + (ALPHA / cells) * mu
    grad_logvar = 0.5 * grad_z * noise[...] * spread_z + (0.5 * ALPHA / cells) * (
        spread_z * spread_z - 1.0
    )
    grad_lat = jnp.concatenate([grad_mu, grad_logvar], axis=0)
    lat_out[...] = grad_lat
    sum_lat[...] += fold(grad_lat)
    product[...] = dot((tal_high[...], tal_low[...]), split(grad_lat), 1, 0)
    mean = vector[0:1, :].T
    for at in range(0, product.shape[0], ROWS):
        rows = pl.ds(at, ROWS)
        grad = product[rows, :] * slope[rows, :]
        grad_out[rows, :] = grad
        sum_grad[rows, :] += fold(grad)
        sum_gain[rows, :] += fold(grad * (pre[rows, :] - mean[at : at + ROWS]))

    @pl.when(step == pl.num_programs(0) - 1)
    def _():
        both = rows_of(sum_grad[...], sum_gain[...])
        sums[...] = jnp.concatenate(
            [both[0:1], both[1:2] * lax.rsqrt(vector[1:2, :] + BN_EPS)], axis=0
        )
        bias_out[...] = rows_of(sum_lat[...])


def latent_back(cells, order, mine, other, z, fix, b_lat, lat, noise, tal_pair, slope, pre,
                vector, after=()):
    hidden, here = pre.shape
    latents = lat.shape[0]
    latent = noise.shape[0]
    block = pl.BlockSpec(
        (None, mine.shape[1], HALF), lambda j, order: (order[j + 1], 0, 0)
    )
    return kernel_call(
        lambda *refs: latent_back_kernel(cells, *refs),
        (here // TILE,),
        [block, block, tile(latent), full(latent, latent), full(latent, 128)]
        + [full(1, latents), tile(latents), tile(latent)]
        + pair_of(full(hidden, latents))
        + [tile(hidden), tile(hidden), full(4, hidden)],
        [tile(hidden), full(2, hidden), tile(latents), full(1, latents)],
        [
            shape(hidden, here),
            shape(2, hidden),
            shape(latents, here),
            shape(1, latents),
        ],
        12,
        order=order,
        scratch=[
            pltpu.VMEM((hidden, 128), F32),
            pltpu.VMEM((hidden, 128), F32),
            pltpu.VMEM((latents, 128), F32),
            pltpu.VMEM((hidden, TILE), F32),
        ],
        after=after,
    )(mine, other, z, *fix, b_lat, lat, noise, *tal_pair, slope, pre, vector)


def encoder_weight_kernel(cells, order, grad_in, pre, vector, scaled_high, scaled_low,
                          high, low, *outs):
    columns = vector[...].T
    scale = lax.rsqrt(columns[:, 1:2] + BN_EPS)
    outer = columns[:, 2:3] * scale
    shift = columns[:, 4:5] * (1.0 / cells)
    gain = columns[:, 5:6] * (1.0 / cells) * scale
    for at in range(0, grad_in.shape[0], ROWS):
        rows = pl.ds(at, ROWS)
        part = slice(at, at + ROWS)
        grad = outer[part] * (
            grad_in[rows, :]
            - shift[part]
            - (pre[rows, :] - columns[part, 0:1]) * gain[part]
        )
        high[rows, :], low[rows, :] = split(grad)
    product = dot((high[...], low[...]), (scaled_high[...], scaled_low[...]), 1, 0)
    start_halves(order, product, outs, pl.program_id(0) == 0)


def encoder_weight(cells, order, halves, grad_in, pre, vector, scaled):
    hidden, here = pre.shape
    genes = scaled[0].shape[1]
    rows = hidden // halves
    return kernel_call(
        lambda *refs: encoder_weight_kernel(cells, *refs),
        (here // TILE,),
        [tile(hidden), tile(hidden), full(6, hidden)]
        + pair_of(pl.BlockSpec((TILE, genes), lambda j, order: (j, 0))),
        pair_of(tile(hidden)) + [full(rows, genes)] * halves,
        [shape(hidden, here, dtype=BF16)] * 2 + [shape(rows, genes)] * halves,
        12,
        order=order,
    )(grad_in, pre, vector, *scaled)


def counts_kernel(cells, enc_high, enc_low, high, low, recon, counts, factor, mask, out,
                  product):
    product[...] = dot((enc_high[...], enc_low[...]), (high[...], low[...]), 1, 0)
    mask_column = mask[...].T
    scale = factor[...]
    for at in range(0, out.shape[0], ROWS):
        rows = pl.ds(at, ROWS)
        column = mask_column[at : at + ROWS]
        diff = (recon[rows, :] - counts[rows, :] * scale) * (column * (1.0 / cells))
        out[rows, :] = (product[rows, :] - diff) * (scale * column)


def counts_back(cells, enc_pair, grads, recon, counts, factor, mask, after=()):
    genes, hidden = enc_pair[0].shape
    here = counts.shape[1]
    return kernel_call(
        lambda *refs: counts_kernel(cells, *refs),
        (here // TILE,),
        pair_of(full(genes, hidden))
        + pair_of(tile(hidden))
        + [tile(genes), tile(genes), tile(1), full(1, genes)],
        tile(genes),
        shape(genes, here),
        16,
        scratch=[pltpu.VMEM((genes, TILE), F32)],
        after=after,
    )(*enc_pair, *grads, recon, counts, factor, mask)


def token_kernel(out):
    out[...] = jnp.zeros_like(out)


def token(after):
    return kernel_call(
        token_kernel, (), [], full(1, 1), shape(1, 1), 0, after=after
    )()[0, 0]


def swap(value, axis, bit):
    size = lax.axis_size(axis)
    return lax.ppermute(value, axis, [(i, i ^ bit) for i in range(size)])


def bits(axis):
    size, bit, out = lax.axis_size(axis), 1, []
    while bit < size:
        out.append(bit)
        bit *= 2
    return out


def add_all(value, axes):
    for axis in axes:
        for bit in bits(axis):
            value = value + swap(value, axis, bit)
    return value


def moments_all(both, count, axes, others=None):
    for axis in axes:
        if axis == GENE and others is not None:
            both = jnp.concatenate([both, others])
        for bit in bits(axis):
            other = swap(both, axis, bit)
            gap = both[0] - other[0]
            rows = [
                0.5 * (both[0] + other[0]),
                both[1] + other[1] + gap * gap * (0.5 * count),
            ]
            both = jnp.concatenate([jnp.stack(rows), both[2:] + other[2:]])
            count = 2 * count
    return both[0], both[1] / count, both[2:]


def rows_wide(vector, share):
    size = vector.shape[0]
    lines = -(-size // share)
    return jnp.pad(vector, (0, lines * share - size)).reshape(lines, share)


def scatter_gene_blocks(value, times):
    me = lax.axis_index(GENE)
    for place, bit in enumerate(reversed(bits(GENE))):
        half = value.shape[0] // 2
        upper = (me & bit) != 0
        sent = jnp.where(upper, value[:half], value[half:])
        kept = jnp.where(upper, value[half:], value[:half])
        value = kept + swap(sent, GENE, bit)
        if place < len(times):
            value = value + token(times[place : place + 1])
    return value[0]


def gene_pairs(links):
    return [(2 * a + y, 2 * b + y) for a, b in links for y in (0, 1)]


OUTER = gene_pairs([(0, 1), (3, 2)])
MIDDLE = gene_pairs([(1, 2), (2, 1)])
SIDES = gene_pairs([(0, 1), (1, 0), (2, 3), (3, 2)])


def line_order(z):
    low = z < 2
    return [
        jnp.where(low, z + 3, z + 1) % 4,
        (z + 2) % 4,
        jnp.where(low, z + 1, z + 3) % 4,
        z,
    ]


def by_line(here):
    return lax.axis_size(GENE) == 8 and here == 8 * HALF


def scatter_encoded(counts, factor, mask, w_enc_t, others):
    here = counts.shape[1]
    hidden = w_enc_t.shape[0]
    me = lax.axis_index(GENE)
    if not by_line(here):
        side = 0 * me
        order = jnp.arange(here // TILE, dtype=jnp.int32)
        blocks = encode_products(side, order, counts, factor, mask, w_enc_t, 0)
        pre = [blocks[3 * k + i] for k in range(len(blocks) // 3) for i in (1, 0)]
        pre = lax.psum_scatter(
            jnp.concatenate(pre, axis=1), GENE, scatter_dimension=1, tiled=True
        )
        scaled = turn_counts(counts, factor, mask, (blocks[0],))
        return [pre], [], scaled, prepare(*others, scaled[0])
    z, y = me // 2, me % 2
    rest = hidden // 6 // 16 * 16
    order = jnp.stack(line_order(z)).astype(jnp.int32)

    def products(first, last, after=()):
        return encode_products(
            y, order[first:last], counts, factor, mask, w_enc_t, rest, after
        )

    middle = (z == 1) | (z == 2)
    blocks = products(0, 1)
    step1 = lax.ppermute(blocks[2], GENE, OUTER)
    blocks += products(1, 2, blocks[:1])
    blocks += products(2, 3, (step1, blocks[3]))
    blocks += products(3, 4, blocks[6:7])
    part = [blocks[3 * k + 1] + swap(blocks[3 * k], GENE, 1) for k in range(4)]
    tail = blocks[2::3]
    step2 = lax.ppermute(tail[1], GENE, OUTER)
    across = lax.ppermute(tail[1] + step1, GENE, MIDDLE)
    scaled = turn_counts(counts, factor, mask, (step2, across, blocks[6]))
    side = lax.ppermute(jnp.where(middle, tail[0] + across, tail[2]), GENE, SIDES)
    inner = lax.ppermute(tail[2] + step2, GENE, MIDDLE)
    weights = prepare(*others, (side, inner, scaled[0][0]))
    tail = tail[3] + side + inner
    left, right = tail[:, :HALF], tail[:, HALF:]
    mine = jnp.where(y == 0, left, right)
    step1 = lax.ppermute(part[0], GENE, OUTER)
    step2 = lax.ppermute(part[1], GENE, OUTER)
    across = lax.ppermute(part[1] + step1, GENE, MIDDLE)
    side = lax.ppermute(jnp.where(middle, part[0] + across, part[2]), GENE, SIDES)
    inner = lax.ppermute(part[2] + step2, GENE, MIDDLE)
    back = swap(jnp.where(y == 0, right, left), GENE, 1)
    return [part[3], side, inner], [mine, back], scaled, weights


def gather_blocks(value, before=None):
    rows, own = value.shape
    if not by_line(own * lax.axis_size(GENE)):
        value = lax.all_gather(value, GENE, axis=1, tiled=True)
        blocks = value.shape[1] // TILE
        stack = jnp.moveaxis(value.reshape(rows, blocks, 2, HALF), 0, 2)
        order = jnp.concatenate([jnp.zeros(1), jnp.arange(blocks)])
        return stack[:, 0], stack[:, 1], order.astype(jnp.int32)
    me = lax.axis_index(GENE)
    mine = jnp.stack([value] + [swap(value, GENE, bit) for bit in (2, 4, 6)])
    if before is not None:
        mine = mine + token(before)
    other = swap(mine, GENE, 1)
    order = jnp.concatenate([(me % 2)[None], (me // 2) ^ jnp.arange(4)])
    return mine, other, order.astype(jnp.int32)


def term_order(here):
    blocks = jnp.arange(here // TILE)
    if not by_line(here):
        return jnp.concatenate([jnp.zeros(1), blocks]).astype(jnp.int32)
    me = lax.axis_index(GENE)
    return jnp.concatenate([(me % 2)[None], ((me // 2 ^ blocks) + 3) % 4]).astype(
        jnp.int32
    )


def scatter_sides(other, own, sums):
    rows, half = own.shape
    if not by_line(2 * half):
        value = jnp.stack(
            [own.reshape(rows, -1, HALF), other.reshape(rows, -1, HALF)], axis=2
        ).reshape(rows, 2 * half)
        return value, add_all(sums, (BATCH, GENE))
    z = lax.axis_index(GENE) // 2
    sums = add_all(sums, (BATCH,))
    sums = sums + swap(sums, GENE, 1)
    quarter = sums.shape[1] // 4
    quarters = [
        jnp.pad(
            lax.dynamic_slice_in_dim(sums, (z ^ k) * quarter, quarter, 1),
            ((0, 0), (0, HALF - quarter)),
        )
        for k in (1, 2, 3, 0)
    ]
    return jnp.concatenate(
        [own + swap(other, GENE, 1), jnp.concatenate(quarters, axis=1)], axis=0
    ), sums


def scatter_terms(part, before):
    if not by_line(2 * part.shape[1]):
        return lax.psum_scatter(part, GENE, scatter_dimension=1, tiled=True)
    total = part[:, 3 * HALF :] + token(before)
    for k in (1, 2, 3):
        total = total + swap(part[:, (k - 1) * HALF : k * HALF], GENE, 2 * k)
    return total


def gather_sums(stack, sums):
    if stack.shape[0] != 4 or not by_line(8 * stack.shape[2]):
        return sums
    z = lax.axis_index(GENE) // 2
    quarter = sums.shape[1] // 4
    quarters = stack[:, -sums.shape[0] :, :quarter]
    return jnp.concatenate(
        [
            lax.dynamic_index_in_dim(quarters, z ^ place, 0, keepdims=False)
            for place in range(4)
        ],
        axis=1,
    )


def add_cores(chunks, zero):
    if len(chunks[0]) == 1:
        return chunks
    return [own + swap(other, BATCH, 1) + zero for other, own in chunks]


def swap_chips(part, zero=0.0):
    if lax.axis_size(BATCH) != 4:
        return part
    return part + swap(part, BATCH, 2) + zero


def join_cores(order, chunks):
    if lax.axis_size(BATCH) != 4:
        return lax.psum(jnp.concatenate([chunk[0] for chunk in chunks], axis=1), BATCH)
    low = order[0] != 0
    other = [swap(part, BATCH, 1) for part in chunks]
    return jnp.concatenate(
        [
            jnp.concatenate([jnp.where(low, a, b), jnp.where(low, b, a)], axis=0)
            for a, b in zip(chunks, other)
        ],
        axis=1,
    )


def on_device(
    counts_in,
    umi_total,
    gene_mask,
    noise,
    w_enc,
    gain_enc,
    shift_enc,
    w_lat,
    b_lat,
    w_dec,
    gain_dec,
    shift_dec,
    w_out,
    b_out,
    mean_enc,
    var_enc,
    mean_dec,
    var_dec,
):
    here = counts_in.shape[1]
    cells = here * lax.axis_size(BATCH)
    hidden = w_enc.shape[1]
    ranks = lax.axis_size(GENE)
    share = hidden // ranks
    own = here // ranks
    latent = noise.shape[0]
    me = lax.axis_index(GENE)
    both = (BATCH, GENE)
    core = lax.axis_index(BATCH) % 2
    halves = 2 if lax.axis_size(BATCH) == 4 else 1
    order = (1 - core).astype(jnp.int32)[None]

    def hidden_part(vector):
        return lax.dynamic_slice_in_dim(vector, me * share, share, vector.ndim - 1)

    def hidden_placed(part):
        empty = jnp.zeros((part.shape[0], hidden), F32)
        return lax.dynamic_update_slice_in_dim(empty, part, me * share, 1)

    factor = (UMI_SCALE / umi_total.astype(F32))[None, :]
    mask = gene_mask.astype(F32)[None, :]
    w_enc_t = w_enc.T
    w_out_t = w_out.T
    b_lat_row = b_lat[None, :]
    noise_own = lax.dynamic_slice_in_dim(noise, me * own, own, 1)

    parts, rest, scaled, weights = scatter_encoded(
        counts_in, factor, mask, w_enc_t, (w_out_t, w_enc_t, w_lat, w_dec)
    )
    out_pair, turn_pair, enc_pair, lat_pair, tal_pair, dec_pair = weights
    affine1 = hidden_placed(jnp.stack([gain_enc, shift_enc]))
    pre_own, stats1 = own_moments(
        parts, rest, after=(affine1, noise_own, out_pair[0])
    )
    pre_enc = lax.all_gather(pre_own, GENE, axis=1, tiled=True)
    mean1, var1, affine1 = moments_all(stats1, own, both, affine1)
    vector1 = jnp.concatenate([mean1[None], var1[None], affine1])
    z_own = latent_own(pre_own, vector1, lat_pair, b_lat_row, noise_own)

    z_mine, z_other, z_order = gather_blocks(z_own)
    z, pre_dec, stats2 = decoder_hidden(z_order, dec_pair, z_mine, z_other)
    mean2, var2, _ = moments_all(stats2, here, (BATCH,))
    vector2 = jnp.stack([mean2, var2, gain_dec, shift_dec])
    recon, grad_high, grad_low, act_high, act_low, *terms, term_w_dec, sums2, grad_b_out = (
        decoder(
            cells, term_order(here), pre_dec, vector2, z, out_pair, turn_pair, counts_in,
            factor, mask, b_out[None, :], w_dec
        )
    )

    part, sums2 = scatter_sides(*terms, sums2)
    grad_w_out = weight_halves(
        order, halves, (act_high, act_low), (grad_high, grad_low), 1, 1024, after=(part,)
    )
    total = scatter_terms(part, (grad_w_out[0],))
    zero = token((total,))
    grad_w_out = add_cores([[grad_w_out[0] + zero, *grad_w_out[1:]]], 0.0)
    lat, slope1, gram_z, sum_z, term_w_dec = encode_again(
        pre_enc, vector1, lat_pair, b_lat_row, z, term_w_dec
    )
    term_mine, term_other, z_order = gather_blocks(total, (lat,))
    sums2 = gather_sums(term_mine, sums2)
    fix_z = fix_terms(cells, w_dec, vector2, sums2, b_lat_row)

    grad_in1, sums1, grad_lat, grad_b_lat = latent_back(
        cells, z_order, term_mine, term_other, z, fix_z, b_lat_row, lat, noise, tal_pair,
        slope1, pre_enc, vector1
    )
    sums1 = add_all(
        jnp.concatenate([sums1.reshape(-1), grad_b_lat[0], grad_b_out[0]]),
        (BATCH,),
    )
    grad_b_lat = sums1[2 * hidden : 2 * hidden + 2 * latent]
    grad_b_out = sums1[2 * hidden + 2 * latent :]
    sums1 = sums1[: 2 * hidden].reshape(2, hidden)
    grad_w_lat = latent_weight(
        grad_lat, lax.dynamic_slice_in_dim(pre_enc, me * share, share, 0),
        hidden_part(vector1)
    )
    vector6 = jnp.concatenate([vector1, sums1])
    high, low, *weight_part = encoder_weight(
        cells, order, halves, grad_in1, pre_enc, vector6, scaled[0]
    )
    term_w_dec = scatter_gene_blocks(
        term_w_dec.reshape(ranks, share, latent), (fix_z[0], grad_lat, high)
    ).T
    small = jnp.concatenate(
        [
            term_w_dec,
            grad_w_lat,
            rows_wide(gram_z.reshape(-1), share),
            rows_wide(sum_z[0], share),
        ]
    )
    small = small + swap(small, BATCH, 1)

    if halves == 2:
        cuts = [0, 256, 512, counts_in.shape[0]]
        times = [lat, term_mine, high]
        grad_w_out = [
            swap_chips(grad_w_out[0][:, a:b], token((time,)))
            for a, b, time in zip(cuts, cuts[1:], times)
        ]
    weight_parts = [weight_part]
    for right in scaled[1:]:
        weight_parts.append(
            weight_halves(order, halves, (high, low), right, 0, 1024, (small,))
        )
    for bit in bits(BATCH)[1:]:
        small = small + swap(small, BATCH, bit)

    if halves == 2:
        part = add_cores(weight_parts[:1], 0.0)[0]
        early, late = swap_chips(part[:, :256]), part[:, 256:]
        other, mine = weight_parts[1]
        other = other + token((early,))
        weight_parts = [late, *add_cores([(other, mine)], token((small,)))]
    grad_counts = counts_back(
        cells, enc_pair, (high, low), recon, counts_in, factor, mask,
        after=[early, *weight_parts] if halves == 2 else ()
    )
    grad_w_out = join_cores(order, grad_w_out).T
    if halves == 2:
        zero = token((grad_counts,))
        weight_parts = [early] + [swap_chips(part, zero) for part in weight_parts]
    grad_w_enc = join_cores(order, weight_parts).T
    term_w_dec = small[:latent]
    grad_w_lat = small[latent : 3 * latent]
    lines = -(-latent // share)
    gram_z = small[3 * latent : -lines].reshape(-1)[: latent * latent]
    gram_z = gram_z.reshape(latent, latent)
    sum_z = small[-lines:].reshape(-1)[:latent]
    grad_shift2 = hidden_part(sums2[0])
    grad_gain2 = hidden_part(sums2[1])
    rstd2 = hidden_part(lax.rsqrt(var2 + BN_EPS))
    cov_z = gram_z - sum_z[:, None] * (sum_z / cells)[None, :]
    pair_w_dec = rstd2[None, :] * jnp.dot(
        cov_z, hidden_part(w_dec), precision=lax.Precision.HIGHEST
    )
    sum_z = sum_z + cells * b_lat[:latent]
    grad_w_dec = (hidden_part(gain_dec) * rstd2)[None, :] * (
        term_w_dec
        - sum_z[:, None] * (grad_shift2 / cells)[None, :]
        - pair_w_dec * (grad_gain2 / cells)[None, :]
    )

    correct = cells / (cells - 1.0)
    new_mean_enc = (1.0 - MOMENTUM) * mean_enc + MOMENTUM * hidden_part(mean1)
    new_var_enc = (1.0 - MOMENTUM) * var_enc + MOMENTUM * hidden_part(var1) * correct
    new_mean_dec = (1.0 - MOMENTUM) * mean_dec + MOMENTUM * mean2
    new_var_dec = (1.0 - MOMENTUM) * var_dec + MOMENTUM * var2 * correct
    return (
        recon,
        grad_counts,
        grad_w_enc,
        hidden_part(sums1[1]),
        hidden_part(sums1[0]),
        grad_w_lat,
        grad_b_lat,
        grad_w_dec,
        grad_gain2,
        grad_shift2,
        grad_w_out,
        grad_b_out,
        new_mean_enc,
        new_var_enc,
        new_mean_dec,
        new_var_dec,
    )


def solution(mesh):
    return jax.shard_map(
        on_device,
        mesh=mesh,
        in_specs=(
            P(GENE, BATCH),
            P(BATCH),
            P(GENE),
            P(None, BATCH),
            P(GENE, None),
            P(GENE),
            P(GENE),
            P(),
            P(),
            P(),
            P(),
            P(),
            P(GENE, None),
            P(GENE),
            P(GENE),
            P(GENE),
            P(),
            P(),
        ),
        out_specs=(
            P(GENE, BATCH),
            P(GENE, BATCH),
            P(GENE, None),
            P(GENE),
            P(GENE),
            P(None, GENE),
            P(),
            P(None, GENE),
            P(GENE),
            P(GENE),
            P(GENE, None),
            P(GENE),
            P(GENE),
            P(GENE),
            P(),
            P(),
        ),
        check_vma=False,
    )
```

```python
import jax
import jax.numpy as jnp
from jax import lax
from jax.experimental import pallas as pl
from jax.experimental.pallas import tpu as pltpu
from jax.sharding import PartitionSpec as P

ALPHA = 0.002
BN_EPS = 1e-05
MOMENTUM = 0.1
UMI_SCALE = 10000.0
BATCH = "batch"
GENE = "gene"
TILE = 512
HALF = 256
ROWS = 16
VMEM_BYTES = 56 << 20
F32 = jnp.float32


BF16 = jnp.bfloat16
RATE = 600_000_000


def split(value):
    high = value.astype(BF16)
    return high, (value - high.astype(F32)).astype(BF16)


def whole(pair):
    return pair[0].astype(F32) + pair[1].astype(F32)


def dot(left, right, left_dim, right_dim):
    def one(a, b):
        return lax.dot_general(
            a,
            b,
            (((left_dim,), (right_dim,)), ((), ())),
            preferred_element_type=F32,
        )

    return one(left[0], right[0]) + (one(left[0], right[1]) + one(left[1], right[0]))


def kernel_call(
    body, grid, in_specs, out_specs, out_shape, micros, order=None, scratch=(), after=(),
    onto=(),
):
    leading = 0 if order is None else 1
    held = leading + len(in_specs)

    def run(*refs):
        body(*refs[:held], *refs[held + len(after) :])

    call = pl.pallas_call(
        run,
        grid_spec=pltpu.PrefetchScalarGridSpec(
            num_scalar_prefetch=leading,
            grid=grid,
            in_specs=list(in_specs) + [pl.BlockSpec(memory_space=pl.ANY)] * len(after),
            out_specs=out_specs,
            scratch_shapes=list(scratch),
        ),
        out_shape=out_shape,
        input_output_aliases={held + k: out for k, out in enumerate(onto)},
        compiler_params=pltpu.CompilerParams(vmem_limit_bytes=VMEM_BYTES),
        cost_estimate=pl.CostEstimate(
            flops=int(micros * RATE), bytes_accessed=1024, transcendentals=0
        ),
    )
    prefetch = () if order is None else (order,)
    return lambda *args: call(*prefetch, *args, *after)


def shape(*dims, dtype=F32):
    return jax.ShapeDtypeStruct(dims, dtype)


def full(*dims):
    return pl.BlockSpec(dims, lambda *_: (0,) * len(dims))


def tile(rows):
    return pl.BlockSpec((rows, TILE), lambda j, *_: (0, j))


def pair_of(spec):
    return [spec, spec]


def sigmoid(value):
    return 0.5 * jnp.tanh(0.5 * value) + 0.5


def silu_pair(value):
    sig = sigmoid(value)
    act = value * sig
    return act, sig + act * (1.0 - sig)


def start_or_add(ref, value, first):
    @pl.when(first)
    def _():
        ref[...] = value

    @pl.when(jnp.logical_not(first))
    def _():
        ref[...] += value


def fold(value):
    width = value.shape[1]
    if width % 128:
        return jnp.broadcast_to(
            jnp.sum(value, axis=1, keepdims=True) / 128.0, (value.shape[0], 128)
        )
    return sum(
        value[:, at : at + 128] for at in range(128, width, 128)
    ) + value[:, :128] if width > 128 else value


def rows_of(*folded):
    return jnp.concatenate(
        [jnp.sum(value, axis=1, keepdims=True) for value in folded], axis=1
    ).T


def moments(pre):
    mean = jnp.mean(pre, axis=1, keepdims=True)
    cent = pre - mean
    return jnp.concatenate(
        [mean, jnp.sum(cent * cent, axis=1, keepdims=True)], axis=1
    ).T


def wide(column):
    return jnp.concatenate([column] * (TILE // 128), axis=1)


def spread(column):
    return jnp.broadcast_to(column, (column.shape[0], 128))


def split_scaled(counts, factor, mask, high, low):
    column = mask[...].T
    scale = factor[...]
    for at in range(0, counts.shape[0], ROWS):
        rows = pl.ds(at, ROWS)
        high[rows, :], low[rows, :] = split(
            counts[rows, :] * scale * column[at : at + ROWS]
        )


def gene_cuts(genes):
    return [0, 512, genes] if genes > 512 else [0, genes]


def turn_kernel(counts, factor, mask, *outs):
    turned = counts[...].T * factor[...].T * mask[...]
    cuts = gene_cuts(turned.shape[1])
    for place, (begin, end) in enumerate(zip(cuts, cuts[1:])):
        outs[2 * place][...], outs[2 * place + 1][...] = split(turned[:, begin:end])


def turn_counts(counts, factor, mask, after):
    genes, here = counts.shape
    cuts = gene_cuts(genes)
    widths = [end - begin for begin, end in zip(cuts, cuts[1:]) for _ in range(2)]
    out = kernel_call(
        turn_kernel,
        (here // TILE,),
        [tile(genes), tile(1), full(1, genes)],
        [pl.BlockSpec((TILE, width), lambda j: (j, 0)) for width in widths],
        [shape(here, width, dtype=BF16) for width in widths],
        5,
        after=after,
    )(counts, factor, mask)
    return [tuple(out[2 * k : 2 * k + 2]) for k in range(len(out) // 2)]


def encode_kernel(order, counts, factor, mask, w_enc_t, *refs):
    *outs, high, low, scaled_high, scaled_low = refs
    step = pl.program_id(0)

    @pl.when(step == 0)
    def _():
        for at in range(0, high.shape[0], ROWS):
            rows = pl.ds(at, ROWS)
            high[rows, :], low[rows, :] = split(w_enc_t[rows, :])

    split_scaled(counts, factor, mask, scaled_high, scaled_low)
    product = dot(
        (high[...], low[...]), (scaled_high[...], scaled_low[...]), 1, 0
    )
    side = order[0] == 0
    for place in range(len(outs) // 3):
        other, own, both = outs[3 * place : 3 * place + 3]
        rows = other.shape[0]

        @pl.when(step == place)
        def _():
            if rows < product.shape[0]:
                both[...] = product[rows:]

        @pl.when((step == place) & side)
        def _():
            other[...] = product[:rows, HALF:]
            own[...] = product[:rows, :HALF]

        @pl.when((step == place) & jnp.logical_not(side))
        def _():
            other[...] = product[:rows, :HALF]
            own[...] = product[:rows, HALF:]


def encode_products(side, order, counts, factor, mask, w_enc_t, rest, after=()):
    genes = counts.shape[0]
    hidden = w_enc_t.shape[0]
    blocks = order.shape[0]
    cells = lambda j, order: (0, order[j + 1])
    sizes = [(hidden - rest, HALF)] * 2 + [(max(rest, 8), TILE)]
    return kernel_call(
        encode_kernel,
        (blocks,),
        [
            pl.BlockSpec((genes, TILE), cells),
            pl.BlockSpec((1, TILE), cells),
            full(1, genes),
            full(hidden, genes),
        ],
        [full(*size) for size in sizes] * blocks,
        [shape(*size) for size in sizes] * blocks,
        4 * blocks,
        order=jnp.concatenate([side[None], order]).astype(jnp.int32),
        scratch=[pltpu.VMEM((hidden, genes), BF16)] * 2
        + [pltpu.VMEM((genes, TILE), BF16)] * 2,
        after=after,
    )(counts, factor, mask, w_enc_t)


def prepare_kernel(w_out_t, w_enc_t, w_lat, w_dec, out_high, out_low, turn_high, turn_low,
                   enc_high, enc_low, lat_high, lat_low, tal_high, tal_low,
                   dec_high, dec_low):
    out_high[...], out_low[...] = split(w_out_t[...])
    turn_high[...], turn_low[...] = split(w_out_t[...].T)
    enc_high[...], enc_low[...] = split(w_enc_t[...].T)
    lat_high[...], lat_low[...] = split(w_lat[...])
    tal_high[...], tal_low[...] = split(w_lat[...].T)
    dec_high[...], dec_low[...] = split(w_dec[...].T)


def prepare(w_out_t, w_enc_t, w_lat, w_dec, after):
    hidden, genes = w_out_t.shape
    latents, latent = w_lat.shape[0], w_dec.shape[0]
    sizes = [
        (hidden, genes),
        (genes, hidden),
        (genes, hidden),
        (latents, hidden),
        (hidden, latents),
        (hidden, latent),
    ]
    out = kernel_call(
        prepare_kernel,
        (),
        pair_of(full(hidden, genes)) + [full(latents, hidden), full(latent, hidden)],
        [full(*size) for size in sizes for _ in range(2)],
        [shape(*size, dtype=BF16) for size in sizes for _ in range(2)],
        6,
        after=after,
    )(w_out_t, w_enc_t, w_lat, w_dec)
    return [tuple(out[2 * k : 2 * k + 2]) for k in range(len(sizes))]


def own_kernel(main, *refs):
    *parts, pre_out, stats = refs
    rows = parts[0].shape[0]
    pre_out[:rows] = sum(part[...] for part in parts[1:main]) + parts[0][...]
    if main < len(parts):
        pre_out[rows:] = sum(part[...] for part in parts[main:])
    stats[...] = moments(pre_out[...])


def own_moments(parts, rest, after=()):
    rows, columns = parts[0].shape
    rows += rest[0].shape[0] if rest else 0
    return kernel_call(
        lambda *refs: own_kernel(len(parts), *refs),
        (),
        [full(*part.shape) for part in (*parts, *rest)],
        [full(rows, columns), full(2, rows)],
        [shape(rows, columns), shape(2, rows)],
        3,
        after=after,
    )(*parts, *rest)


def normalize(pre, vector):
    columns = vector.T
    norm = (pre - columns[:, 0:1]) * lax.rsqrt(columns[:, 1:2] + BN_EPS)
    return norm, norm * columns[:, 2:3] + columns[:, 3:4]


def latent_kernel(pre, vector, lat_high, lat_low, b_lat, noise, z_out):
    _, value = normalize(pre[...], vector[...])
    act, _ = silu_pair(value)
    lat = dot((lat_high[...], lat_low[...]), split(act), 1, 0) + b_lat[...].T
    latent = noise.shape[0]
    z_out[...] = lat[:latent] + jnp.exp(0.5 * lat[latent:]) * noise[...]


def latent_own(pre, vector, lat_pair, b_lat, noise):
    return kernel_call(
        latent_kernel,
        (),
        [full(*a.shape) for a in (pre, vector, *lat_pair, b_lat, noise)],
        full(*noise.shape),
        shape(*noise.shape),
        3,
    )(pre, vector, *lat_pair, b_lat, noise)


def sides(order, mine, other):
    left = order[0] == 0
    return jnp.concatenate(
        [jnp.where(left, mine, other), jnp.where(left, other, mine)], axis=1
    )


def hidden_kernel(order, dec_high, dec_low, mine, other, z_all, pre_out, stats,
                  sums):
    for step in range(mine.shape[0]):
        spot = order[step + 1]
        z = sides(order, mine[spot], other[spot])
        columns = pl.ds(step * TILE, TILE)
        z_all[:, columns] = z
        pre = dot((dec_high[...], dec_low[...]), split(z), 1, 0)
        pre_out[:, columns] = pre
        if step == 0:
            sums[...] = fold(pre)
        else:
            sums[...] += fold(pre)
    hidden, here = pre_out.shape
    mean = jnp.sum(sums[...], axis=1, keepdims=True) * (1.0 / here)
    sums[...] = spread(mean)
    squares = []
    for at in range(0, hidden, ROWS):
        rows = pl.ds(at, ROWS)
        total = jnp.zeros((ROWS, 128), F32)
        for step in range(mine.shape[0]):
            cent = pre_out[rows, pl.ds(step * TILE, TILE)] - wide(sums[rows, :])
            total = total + fold(cent * cent)
        squares.append(total)
    square = jnp.sum(jnp.concatenate(squares, axis=0), axis=1, keepdims=True)
    stats[...] = jnp.concatenate([mean, square], axis=1).T


def decoder_hidden(order, dec_pair, mine, other):
    hidden, latent = dec_pair[0].shape
    cells = 2 * mine.shape[0] * HALF
    return kernel_call(
        hidden_kernel,
        (1,),
        pair_of(full(hidden, latent)) + [full(*mine.shape), full(*other.shape)],
        [full(latent, cells), full(hidden, cells), full(2, hidden)],
        [shape(latent, cells), shape(hidden, cells), shape(2, hidden)],
        8,
        order=order,
        scratch=[pltpu.VMEM((hidden, 128), F32)],
    )(*dec_pair, mine, other)


def decoder_kernel(cells, order, pre, vector, z, out_high, out_low, turn_high, turn_low,
                   counts, factor, mask, b_out, w_dec,
                   recon_out, grad_high, grad_low, act_high, act_low, z_other, z_own,
                   weight_out, sums, bias_out,
                   sum_term, sum_gain, sum_grad, mean_w, scale_w, shift_w, mask_w, bias_w,
                   dec_high, dec_low, slope, product, term_high, term_low):
    step = pl.program_id(0)
    hidden, genes = out_high.shape

    @pl.when(step == 0)
    def _():
        columns = vector[...].T
        rstd = lax.rsqrt(columns[:, 1:2] + BN_EPS)
        mean_w[...] = spread(columns[:, 0:1])
        scale_w[...] = spread(rstd * columns[:, 2:3])
        shift_w[...] = spread(columns[:, 3:4])
        mask_w[...] = spread(mask[...].T * (1.0 / cells))
        bias_w[...] = spread(b_out[...].T)
        dec_high[...], dec_low[...] = split(
            w_dec[...] * (vector[2:3, :] * lax.rsqrt(vector[1:2, :] + BN_EPS))
        )
        for ref in (sum_term, sum_gain, sum_grad, weight_out):
            ref[...] = jnp.zeros_like(ref)

    for at in range(0, hidden, ROWS):
        rows = pl.ds(at, ROWS)
        cent = pre[rows, :] - wide(mean_w[rows, :])
        act, slope[rows, :] = silu_pair(
            cent * wide(scale_w[rows, :]) + wide(shift_w[rows, :])
        )
        act_high[rows, :], act_low[rows, :] = split(act)
    product[:genes, :] = dot(
        (turn_high[...], turn_low[...]), (act_high[...], act_low[...]), 1, 0
    )
    scale = factor[...]
    for at in range(0, genes, ROWS):
        rows = pl.ds(at, ROWS)
        out = product[rows, :] + wide(bias_w[rows, :])
        recon = jnp.maximum(out, 0.0) + jnp.log(1.0 + jnp.exp(-jnp.abs(out)))
        recon_out[rows, :] = recon
        grad = (recon - counts[rows, :] * scale) * (wide(mask_w[rows, :]) * sigmoid(out))
        sum_grad[rows, :] += fold(grad)
        grad_high[rows, :], grad_low[rows, :] = split(grad)
    product[:hidden, :] = dot(
        (out_high[...], out_low[...]), (grad_high[...], grad_low[...]), 1, 0
    )
    for at in range(0, hidden, ROWS):
        rows = pl.ds(at, ROWS)
        term = product[rows, :] * slope[rows, :]
        cent = pre[rows, :] - wide(mean_w[rows, :])
        sum_term[rows, :] += fold(term)
        sum_gain[rows, :] += fold(term * cent)
        term_high[rows, :], term_low[rows, :] = split(term)
    terms = term_high[...], term_low[...]
    back = dot((dec_high[...], dec_low[...]), terms, 1, 0)
    left = order[0] == 0
    z_other[...] = jnp.where(left, back[:, HALF:], back[:, :HALF])
    z_own[...] = jnp.where(left, back[:, :HALF], back[:, HALF:])
    weight_out[...] += dot(terms, split(z[...]), 1, 1)

    @pl.when(step == pl.num_programs(0) - 1)
    def _():
        rstd = lax.rsqrt(vector[1:2, :] + BN_EPS)
        both = rows_of(sum_term[...], sum_gain[...])
        sums[...] = jnp.concatenate([both[0:1], both[1:2] * rstd], axis=0)
        bias_out[...] = rows_of(sum_grad[...])


def decoder(cells, order, pre, vector, z, out_pair, turn_pair, counts, factor, mask, b_out,
            w_dec):
    hidden, genes = out_pair[0].shape
    here = counts.shape[1]
    latent = w_dec.shape[0]
    most = max(hidden, genes)
    placed = pl.BlockSpec((latent, HALF), lambda j, order: (0, order[j + 1]))
    return kernel_call(
        lambda *refs: decoder_kernel(cells, *refs),
        (here // TILE,),
        [tile(hidden), full(4, hidden), tile(latent)]
        + pair_of(full(hidden, genes))
        + pair_of(full(genes, hidden))
        + [
            tile(genes),
            tile(1),
            full(1, genes),
            full(1, genes),
            full(latent, hidden),
        ],
        [tile(genes)]
        + pair_of(tile(genes))
        + pair_of(tile(hidden))
        + pair_of(placed)
        + [full(hidden, latent), full(2, hidden), full(1, genes)],
        [shape(genes, here)]
        + [shape(genes, here, dtype=BF16)] * 2
        + [shape(hidden, here, dtype=BF16)] * 2
        + [shape(latent, here // 2)] * 2
        + [shape(hidden, latent), shape(2, hidden), shape(1, genes)],
        42,
        order=order,
        scratch=[pltpu.VMEM((hidden, 128), F32)] * 2
        + [pltpu.VMEM((genes, 128), F32)]
        + [pltpu.VMEM((hidden, 128), F32)] * 3
        + [pltpu.VMEM((genes, 128), F32)] * 2
        + [pltpu.VMEM((latent, hidden), BF16)] * 2
        + [pltpu.VMEM((hidden, TILE), F32), pltpu.VMEM((most, TILE), F32)]
        + [pltpu.VMEM((hidden, TILE), BF16)] * 2,
    )(pre, vector, z, *out_pair, *turn_pair, counts, factor, mask, b_out, w_dec)


def start_halves(order, product, outs, first):
    if len(outs) == 1:
        start_or_add(outs[0], product, first)
        return
    rows = product.shape[0] // 2
    upper = order[0] != 0

    @pl.when(upper)
    def _():
        start_or_add(outs[0], product[rows:], first)
        start_or_add(outs[1], product[:rows], first)

    @pl.when(jnp.logical_not(upper))
    def _():
        start_or_add(outs[0], product[:rows], first)
        start_or_add(outs[1], product[rows:], first)


def weight_kernel(right_dim, order, left_high, left_low, right_high, right_low, *outs):
    product = dot(
        (left_high[...], left_low[...]), (right_high[...], right_low[...]), 1, right_dim
    )
    start_halves(order, product, outs, pl.program_id(0) == 0)


def weight_halves(order, halves, left, right, right_dim, width, after=()):
    hidden, here = left[0].shape
    rows = hidden // halves
    genes = right[0].shape[1 - right_dim]
    if right_dim:
        cells = pl.BlockSpec((genes, width), lambda j, order: (0, j))
    else:
        cells = pl.BlockSpec((width, genes), lambda j, order: (j, 0))
    return kernel_call(
        lambda *refs: weight_kernel(right_dim, *refs),
        (here // width,),
        pair_of(pl.BlockSpec((hidden, width), lambda j, order: (0, j))) + pair_of(cells),
        [full(rows, genes)] * halves,
        [shape(rows, genes)] * halves,
        10,
        order=order,
        after=after,
    )(*left, *right)


def latent_weight_kernel(lat, part, vector, out):
    _, value = normalize(part[...], vector[...])
    act, _ = silu_pair(value)
    product = dot(split(lat[...]), split(act), 1, 1)
    start_or_add(out, product, pl.program_id(0) == 0)


def latent_weight(lat, part, vector, after):
    latents, here = lat.shape
    share = part.shape[0]
    return kernel_call(
        latent_weight_kernel,
        (here // 1024,),
        [
            pl.BlockSpec((latents, 1024), lambda j: (0, j)),
            pl.BlockSpec((share, 1024), lambda j: (0, j)),
            full(4, share),
        ],
        full(latents, share),
        shape(latents, share),
        4,
        after=after,
    )(lat, part, vector)


def again_kernel(pre_enc, vector, lat_high, lat_low, b_lat, z, later,
                 lat_out, slope_out, gram, sum_out, later_out, act_high, act_low):
    later_out[...] = later[...]
    first = pl.program_id(0) == 0
    moved = z[...] - b_lat[:, : z.shape[0]].T
    pair = split(moved)
    start_or_add(gram, dot(pair, pair, 1, 1), first)
    start_or_add(sum_out, rows_of(moved), first)
    columns = vector[...].T
    scale = lax.rsqrt(columns[:, 1:2] + BN_EPS) * columns[:, 2:3]
    for at in range(0, pre_enc.shape[0], ROWS):
        rows = pl.ds(at, ROWS)
        part = slice(at, at + ROWS)
        act, slope_out[rows, :] = silu_pair(
            (pre_enc[rows, :] - columns[part, 0:1]) * scale[part] + columns[part, 3:4]
        )
        act_high[rows, :], act_low[rows, :] = split(act)
    lat_out[...] = (
        dot((lat_high[...], lat_low[...]), (act_high[...], act_low[...]), 1, 0)
        + b_lat[...].T
    )


def encode_again(pre_enc, vector, lat_pair, b_lat, z, later, after=()):
    latent = z.shape[0]
    hidden, here = pre_enc.shape
    latents = lat_pair[0].shape[0]
    return kernel_call(
        again_kernel,
        (here // TILE,),
        [tile(hidden), full(4, hidden)]
        + pair_of(full(latents, hidden))
        + [full(1, latents), tile(latent), full(*later.shape)],
        [
            tile(latents),
            tile(hidden),
            full(latent, latent),
            full(1, latent),
            full(*later.shape),
        ],
        [
            shape(latents, here),
            shape(hidden, here),
            shape(latent, latent),
            shape(1, latent),
            shape(*later.shape),
        ],
        10,
        scratch=[pltpu.VMEM((hidden, TILE), BF16)] * 2,
        after=after,
    )(pre_enc, vector, *lat_pair, b_lat, z, later)


def fix_kernel(cells, w_dec, vector, sums, b_lat, matrix_out, column_out):
    weight = w_dec[...]
    rstd = lax.rsqrt(vector[1:2, :] + BN_EPS)
    scaled = weight * (vector[2:3, :] * rstd * (1.0 / cells))
    gained = scaled * (sums[1:2, :] * rstd)
    matrix_out[...] = dot(split(gained), split(weight), 1, 1)
    bias = b_lat[:, : weight.shape[0]].T
    mean = vector[0:1, :] - jnp.sum(weight * bias, axis=0, keepdims=True)
    column_out[...] = spread(
        jnp.sum(scaled * sums[0:1, :] - gained * mean, axis=1, keepdims=True)
    )


def fix_terms(cells, w_dec, vector, sums, b_lat):
    latent, hidden = w_dec.shape
    return kernel_call(
        lambda *refs: fix_kernel(cells, *refs),
        (),
        [full(latent, hidden), full(4, hidden), full(2, hidden), full(*b_lat.shape)],
        [full(latent, latent), full(latent, 128)],
        [shape(latent, latent), shape(latent, 128)],
        2,
    )(w_dec, vector, sums, b_lat)


def latent_back_kernel(cells, order, mine, other, z, matrix, column, b_lat, lat, noise,
                       tal_high, tal_low, slope, pre, vector, grad_out, sums, lat_out, bias_out,
                       sum_grad, sum_gain, sum_lat, product):
    step = pl.program_id(0)

    @pl.when(step == 0)
    def _():
        for ref in (sum_grad, sum_gain, sum_lat):
            ref[...] = jnp.zeros_like(ref)

    latent = noise.shape[0]
    moved = z[...] - b_lat[:, :latent].T
    fix = dot(split(matrix[...]), split(moved), 1, 0) + wide(column[...])
    grad_z = sides(order, mine[:latent, :], other[:latent, :]) - fix
    mu = lat[:latent, :]
    spread_z = jnp.exp(0.5 * lat[latent:, :])
    grad_mu = grad_z + (ALPHA / cells) * mu
    grad_logvar = 0.5 * grad_z * noise[...] * spread_z + (0.5 * ALPHA / cells) * (
        spread_z * spread_z - 1.0
    )
    grad_lat = jnp.concatenate([grad_mu, grad_logvar], axis=0)
    lat_out[...] = grad_lat
    sum_lat[...] += fold(grad_lat)
    product[...] = dot((tal_high[...], tal_low[...]), split(grad_lat), 1, 0)
    mean = vector[0:1, :].T
    for at in range(0, product.shape[0], ROWS):
        rows = pl.ds(at, ROWS)
        grad = product[rows, :] * slope[rows, :]
        grad_out[rows, :] = grad
        sum_grad[rows, :] += fold(grad)
        sum_gain[rows, :] += fold(grad * (pre[rows, :] - mean[at : at + ROWS]))

    @pl.when(step == pl.num_programs(0) - 1)
    def _():
        both = rows_of(sum_grad[...], sum_gain[...])
        sums[...] = jnp.concatenate(
            [both[0:1], both[1:2] * lax.rsqrt(vector[1:2, :] + BN_EPS)], axis=0
        )
        bias_out[...] = rows_of(sum_lat[...])


def latent_back(cells, order, mine, other, z, fix, b_lat, lat, noise, tal_pair, slope, pre,
                vector, after=()):
    hidden, here = pre.shape
    latents = lat.shape[0]
    latent = noise.shape[0]
    block = pl.BlockSpec(
        (None, mine.shape[1], HALF), lambda j, order: (order[j + 1], 0, 0)
    )
    return kernel_call(
        lambda *refs: latent_back_kernel(cells, *refs),
        (here // TILE,),
        [block, block, tile(latent), full(latent, latent), full(latent, 128)]
        + [full(1, latents), tile(latents), tile(latent)]
        + pair_of(full(hidden, latents))
        + [tile(hidden), tile(hidden), full(4, hidden)],
        [tile(hidden), full(2, hidden), tile(latents), full(1, latents)],
        [
            shape(hidden, here),
            shape(2, hidden),
            shape(latents, here),
            shape(1, latents),
        ],
        12,
        order=order,
        scratch=[
            pltpu.VMEM((hidden, 128), F32),
            pltpu.VMEM((hidden, 128), F32),
            pltpu.VMEM((latents, 128), F32),
            pltpu.VMEM((hidden, TILE), F32),
        ],
        after=after,
    )(mine, other, z, *fix, b_lat, lat, noise, *tal_pair, slope, pre, vector)


def encoder_weight_kernel(cells, order, grad_in, pre, vector, scaled_high, scaled_low,
                          high, low, *outs):
    columns = vector[...].T
    scale = lax.rsqrt(columns[:, 1:2] + BN_EPS)
    outer = columns[:, 2:3] * scale
    shift = columns[:, 4:5] * (1.0 / cells)
    gain = columns[:, 5:6] * (1.0 / cells) * scale
    for at in range(0, grad_in.shape[0], ROWS):
        rows = pl.ds(at, ROWS)
        part = slice(at, at + ROWS)
        grad = outer[part] * (
            grad_in[rows, :]
            - shift[part]
            - (pre[rows, :] - columns[part, 0:1]) * gain[part]
        )
        high[rows, :], low[rows, :] = split(grad)
    product = dot((high[...], low[...]), (scaled_high[...], scaled_low[...]), 1, 0)
    start_halves(order, product, outs, pl.program_id(0) == 0)


def encoder_weight(cells, order, halves, grad_in, pre, vector, scaled):
    hidden, here = pre.shape
    genes = scaled[0].shape[1]
    rows = hidden // halves
    return kernel_call(
        lambda *refs: encoder_weight_kernel(cells, *refs),
        (here // TILE,),
        [tile(hidden), tile(hidden), full(6, hidden)]
        + pair_of(pl.BlockSpec((TILE, genes), lambda j, order: (j, 0))),
        pair_of(tile(hidden)) + [full(rows, genes)] * halves,
        [shape(hidden, here, dtype=BF16)] * 2 + [shape(rows, genes)] * halves,
        12,
        order=order,
    )(grad_in, pre, vector, *scaled)


def counts_kernel(cells, enc_high, enc_low, high, low, recon, counts, factor, mask, out,
                  product):
    product[...] = dot((enc_high[...], enc_low[...]), (high[...], low[...]), 1, 0)
    mask_column = mask[...].T
    scale = factor[...]
    for at in range(0, out.shape[0], ROWS):
        rows = pl.ds(at, ROWS)
        column = mask_column[at : at + ROWS]
        diff = (recon[rows, :] - counts[rows, :] * scale) * (column * (1.0 / cells))
        out[rows, :] = (product[rows, :] - diff) * (scale * column)


def counts_back(cells, enc_pair, grads, recon, counts, factor, mask, after=()):
    genes, hidden = enc_pair[0].shape
    here = counts.shape[1]
    return kernel_call(
        lambda *refs: counts_kernel(cells, *refs),
        (here // TILE,),
        pair_of(full(genes, hidden))
        + pair_of(tile(hidden))
        + [tile(genes), tile(genes), tile(1), full(1, genes)],
        tile(genes),
        shape(genes, here),
        16,
        scratch=[pltpu.VMEM((genes, TILE), F32)],
        after=after,
    )(*enc_pair, *grads, recon, counts, factor, mask)


def token_kernel(out):
    out[...] = jnp.zeros_like(out)


def token(after):
    return kernel_call(
        token_kernel, (), [], full(1, 1), shape(1, 1), 0, after=after
    )()[0, 0]


def swap(value, axis, bit):
    size = lax.axis_size(axis)
    return lax.ppermute(value, axis, [(i, i ^ bit) for i in range(size)])


def bits(axis):
    size, bit, out = lax.axis_size(axis), 1, []
    while bit < size:
        out.append(bit)
        bit *= 2
    return out


def add_all(value, axes):
    for axis in axes:
        for bit in bits(axis):
            value = value + swap(value, axis, bit)
    return value


def moments_all(both, count, axes, others=None):
    for axis in axes:
        if axis == GENE and others is not None:
            both = jnp.concatenate([both, others])
        for bit in bits(axis):
            other = swap(both, axis, bit)
            gap = both[0] - other[0]
            rows = [
                0.5 * (both[0] + other[0]),
                both[1] + other[1] + gap * gap * (0.5 * count),
            ]
            both = jnp.concatenate([jnp.stack(rows), both[2:] + other[2:]])
            count = 2 * count
    return both[0], both[1] / count, both[2:]


def rows_wide(vector, share):
    size = vector.shape[0]
    lines = -(-size // share)
    return jnp.pad(vector, (0, lines * share - size)).reshape(lines, share)


def scatter_gene_blocks(value, times):
    me = lax.axis_index(GENE)
    for place, bit in enumerate(reversed(bits(GENE))):
        half = value.shape[0] // 2
        upper = (me & bit) != 0
        sent = jnp.where(upper, value[:half], value[half:])
        kept = jnp.where(upper, value[half:], value[:half])
        value = kept + swap(sent, GENE, bit)
        if place < len(times):
            value = value + token(times[place : place + 1])
    return value[0]


def gene_pairs(links):
    return [(2 * a + y, 2 * b + y) for a, b in links for y in (0, 1)]


OUTER = gene_pairs([(0, 1), (3, 2)])
MIDDLE = gene_pairs([(1, 2), (2, 1)])
SIDES = gene_pairs([(0, 1), (1, 0), (2, 3), (3, 2)])


def line_order(z):
    low = z < 2
    return [
        jnp.where(low, z + 3, z + 1) % 4,
        (z + 2) % 4,
        jnp.where(low, z + 1, z + 3) % 4,
        z,
    ]


def by_line(here):
    return lax.axis_size(GENE) == 8 and here == 8 * HALF


def scatter_encoded(counts, factor, mask, w_enc_t, others):
    here = counts.shape[1]
    hidden = w_enc_t.shape[0]
    me = lax.axis_index(GENE)
    if not by_line(here):
        side = 0 * me
        order = jnp.arange(here // TILE, dtype=jnp.int32)
        blocks = encode_products(side, order, counts, factor, mask, w_enc_t, 0)
        pre = [blocks[3 * k + i] for k in range(len(blocks) // 3) for i in (1, 0)]
        pre = lax.psum_scatter(
            jnp.concatenate(pre, axis=1), GENE, scatter_dimension=1, tiled=True
        )
        scaled = turn_counts(counts, factor, mask, (blocks[0],))
        return [pre], [], scaled, prepare(*others, scaled[0])
    z, y = me // 2, me % 2
    rest = hidden // 6 // 16 * 16
    order = jnp.stack(line_order(z)).astype(jnp.int32)

    def products(first, last, after=()):
        return encode_products(
            y, order[first:last], counts, factor, mask, w_enc_t, rest, after
        )

    middle = (z == 1) | (z == 2)
    blocks = products(0, 1)
    step1 = lax.ppermute(blocks[2], GENE, OUTER)
    blocks += products(1, 2, (step1,))
    blocks += products(2, 3, blocks[3:4])
    blocks += products(3, 4, blocks[6:7])
    part = [blocks[3 * k + 1] + swap(blocks[3 * k], GENE, 1) for k in range(4)]
    tail = blocks[2::3]
    step2 = lax.ppermute(tail[1], GENE, OUTER)
    across = lax.ppermute(tail[1] + step1, GENE, MIDDLE)
    scaled = turn_counts(counts, factor, mask, (step2, across, blocks[6]))
    side = lax.ppermute(jnp.where(middle, tail[0] + across, tail[2]), GENE, SIDES)
    inner = lax.ppermute(tail[2] + step2, GENE, MIDDLE)
    weights = prepare(*others, (side, inner, scaled[0][0]))
    tail = tail[3] + side + inner
    left, right = tail[:, :HALF], tail[:, HALF:]
    mine = jnp.where(y == 0, left, right)
    step1 = lax.ppermute(part[0], GENE, OUTER)
    step2 = lax.ppermute(part[1], GENE, OUTER)
    across = lax.ppermute(part[1] + step1, GENE, MIDDLE)
    side = lax.ppermute(jnp.where(middle, part[0] + across, part[2]), GENE, SIDES)
    inner = lax.ppermute(part[2] + step2, GENE, MIDDLE)
    back = swap(jnp.where(y == 0, right, left), GENE, 1)
    return [part[3], side, inner], [mine, back], scaled, weights


def gather_blocks(value, before=None):
    rows, own = value.shape
    if not by_line(own * lax.axis_size(GENE)):
        value = lax.all_gather(value, GENE, axis=1, tiled=True)
        blocks = value.shape[1] // TILE
        stack = jnp.moveaxis(value.reshape(rows, blocks, 2, HALF), 0, 2)
        order = jnp.concatenate([jnp.zeros(1), jnp.arange(blocks)])
        return stack[:, 0], stack[:, 1], order.astype(jnp.int32)
    me = lax.axis_index(GENE)
    mine = jnp.stack([value] + [swap(value, GENE, bit) for bit in (2, 4, 6)])
    if before is not None:
        mine = mine + token(before)
    other = swap(mine, GENE, 1)
    order = jnp.concatenate([(me % 2)[None], (me // 2) ^ jnp.arange(4)])
    return mine, other, order.astype(jnp.int32)


def term_order(here):
    blocks = jnp.arange(here // TILE)
    if not by_line(here):
        return jnp.concatenate([jnp.zeros(1), blocks]).astype(jnp.int32)
    me = lax.axis_index(GENE)
    return jnp.concatenate([(me % 2)[None], ((me // 2 ^ blocks) + 3) % 4]).astype(
        jnp.int32
    )


def scatter_sides(other, own, sums):
    rows, half = own.shape
    if not by_line(2 * half):
        value = jnp.stack(
            [own.reshape(rows, -1, HALF), other.reshape(rows, -1, HALF)], axis=2
        ).reshape(rows, 2 * half)
        return value, add_all(sums, (BATCH, GENE))
    z = lax.axis_index(GENE) // 2
    sums = add_all(sums, (BATCH,))
    sums = sums + swap(sums, GENE, 1)
    quarter = sums.shape[1] // 4
    quarters = [
        jnp.pad(
            lax.dynamic_slice_in_dim(sums, (z ^ k) * quarter, quarter, 1),
            ((0, 0), (0, HALF - quarter)),
        )
        for k in (1, 2, 3, 0)
    ]
    return jnp.concatenate(
        [own + swap(other, GENE, 1), jnp.concatenate(quarters, axis=1)], axis=0
    ), sums


def scatter_terms(part, before):
    if not by_line(2 * part.shape[1]):
        return lax.psum_scatter(part, GENE, scatter_dimension=1, tiled=True)
    total = part[:, 3 * HALF :] + token(before)
    for k in (1, 2, 3):
        total = total + swap(part[:, (k - 1) * HALF : k * HALF], GENE, 2 * k)
    return total


def gather_sums(stack, sums):
    if stack.shape[0] != 4 or not by_line(8 * stack.shape[2]):
        return sums
    z = lax.axis_index(GENE) // 2
    quarter = sums.shape[1] // 4
    quarters = stack[:, -sums.shape[0] :, :quarter]
    return jnp.concatenate(
        [
            lax.dynamic_index_in_dim(quarters, z ^ place, 0, keepdims=False)
            for place in range(4)
        ],
        axis=1,
    )


def add_cores(chunks, zero):
    if len(chunks[0]) == 1:
        return chunks
    return [own + swap(other, BATCH, 1) + zero for other, own in chunks]


def swap_chips(part, zero=0.0):
    if lax.axis_size(BATCH) != 4:
        return part
    return part + swap(part, BATCH, 2) + zero


def join_cores(order, chunks, zero):
    if lax.axis_size(BATCH) != 4:
        return lax.psum(jnp.concatenate([chunk[0] for chunk in chunks], axis=1), BATCH)
    low = order[0] != 0
    other = [swap(part + zero, BATCH, 1) for part in chunks]
    return jnp.concatenate(
        [
            jnp.concatenate([jnp.where(low, a, b), jnp.where(low, b, a)], axis=0)
            for a, b in zip(chunks, other)
        ],
        axis=1,
    )


def on_device(
    counts_in,
    umi_total,
    gene_mask,
    noise,
    w_enc,
    gain_enc,
    shift_enc,
    w_lat,
    b_lat,
    w_dec,
    gain_dec,
    shift_dec,
    w_out,
    b_out,
    mean_enc,
    var_enc,
    mean_dec,
    var_dec,
):
    here = counts_in.shape[1]
    cells = here * lax.axis_size(BATCH)
    hidden = w_enc.shape[1]
    ranks = lax.axis_size(GENE)
    share = hidden // ranks
    own = here // ranks
    latent = noise.shape[0]
    me = lax.axis_index(GENE)
    both = (BATCH, GENE)
    core = lax.axis_index(BATCH) % 2
    halves = 2 if lax.axis_size(BATCH) == 4 else 1
    order = (1 - core).astype(jnp.int32)[None]

    def hidden_part(vector):
        return lax.dynamic_slice_in_dim(vector, me * share, share, vector.ndim - 1)

    def hidden_placed(part):
        empty = jnp.zeros((part.shape[0], hidden), F32)
        return lax.dynamic_update_slice_in_dim(empty, part, me * share, 1)

    factor = (UMI_SCALE / umi_total.astype(F32))[None, :]
    mask = gene_mask.astype(F32)[None, :]
    w_enc_t = w_enc.T
    w_out_t = w_out.T
    b_lat_row = b_lat[None, :]
    noise_own = lax.dynamic_slice_in_dim(noise, me * own, own, 1)

    parts, rest, scaled, weights = scatter_encoded(
        counts_in, factor, mask, w_enc_t, (w_out_t, w_enc_t, w_lat, w_dec)
    )
    out_pair, turn_pair, enc_pair, lat_pair, tal_pair, dec_pair = weights
    affine1 = hidden_placed(jnp.stack([gain_enc, shift_enc]))
    pre_own, stats1 = own_moments(
        parts, rest, after=(affine1, noise_own, out_pair[0])
    )
    mean1, var1, affine1 = moments_all(stats1, own, both, affine1)
    vector1 = jnp.concatenate([mean1[None], var1[None], affine1])
    z_own = latent_own(pre_own, vector1, lat_pair, b_lat_row, noise_own)

    z_mine, z_other, z_order = gather_blocks(z_own)
    zero = token((z_mine, z_other))
    pre_enc = lax.all_gather(pre_own + zero, GENE, axis=1, tiled=True)
    z, pre_dec, stats2 = decoder_hidden(z_order, dec_pair, z_mine, z_other)
    mean2, var2, _ = moments_all(stats2, here, (BATCH,))
    vector2 = jnp.stack([mean2, var2, gain_dec, shift_dec])
    recon, grad_high, grad_low, act_high, act_low, *terms, term_w_dec, sums2, grad_b_out = (
        decoder(
            cells, term_order(here), pre_dec, vector2, z, out_pair, turn_pair, counts_in,
            factor, mask, b_out[None, :], w_dec
        )
    )

    part, sums2 = scatter_sides(*terms, sums2)
    grad_w_out = weight_halves(
        order, halves, (act_high, act_low), (grad_high, grad_low), 1, 1024, after=(part,)
    )
    total = scatter_terms(part, (grad_w_out[0],))
    zero = token((total,))
    grad_w_out = add_cores([[grad_w_out[0] + zero, *grad_w_out[1:]]], 0.0)
    lat, slope1, gram_z, sum_z, term_w_dec = encode_again(
        pre_enc, vector1, lat_pair, b_lat_row, z, term_w_dec
    )
    term_mine, term_other, z_order = gather_blocks(total, (lat,))
    sums2 = gather_sums(term_mine, sums2)
    fix_z = fix_terms(cells, w_dec, vector2, sums2, b_lat_row)

    when = []
    if halves == 2:
        cuts = [0, 256, 512, counts_in.shape[0]]
        last = grad_w_out[0][:, cuts[2] :]
        grad_w_out = [
            swap_chips(grad_w_out[0][:, a:b], token((time,)))
            for a, b, time in zip(cuts, cuts[1:], [lat, term_mine])
        ]
        when = grad_w_out

    grad_in1, sums1, grad_lat, grad_b_lat = latent_back(
        cells, z_order, term_mine, term_other, z, fix_z, b_lat_row, lat, noise, tal_pair,
        slope1, pre_enc, vector1, when
    )
    if halves == 2:
        grad_w_out = [*grad_w_out, swap_chips(last, token((grad_lat,)))]
    sums1 = add_all(
        jnp.concatenate([sums1.reshape(-1), grad_b_lat[0], grad_b_out[0]]),
        (BATCH,),
    )
    grad_b_lat = sums1[2 * hidden : 2 * hidden + 2 * latent]
    grad_b_out = sums1[2 * hidden + 2 * latent :]
    sums1 = sums1[: 2 * hidden].reshape(2, hidden)
    grad_w_lat = latent_weight(
        grad_lat, lax.dynamic_slice_in_dim(pre_enc, me * share, share, 0),
        hidden_part(vector1), grad_w_out[2:]
    )
    vector6 = jnp.concatenate([vector1, sums1])
    high, low, *weight_part = encoder_weight(
        cells, order, halves, grad_in1, pre_enc, vector6, scaled[0]
    )
    term_w_dec = scatter_gene_blocks(
        term_w_dec.reshape(ranks, share, latent), (grad_lat, grad_w_lat, high)
    ).T
    small = jnp.concatenate(
        [
            term_w_dec,
            grad_w_lat,
            rows_wide(gram_z.reshape(-1), share),
            rows_wide(sum_z[0], share),
        ]
    )
    small = small + swap(small, BATCH, 1)

    weight_parts = [weight_part]
    for right in scaled[1:]:
        weight_parts.append(
            weight_halves(order, halves, (high, low), right, 0, 1024, (small,))
        )
    for bit in bits(BATCH)[1:]:
        small = small + swap(small, BATCH, bit)

    if halves == 2:
        part = add_cores(weight_parts[:1], 0.0)[0]
        early, late = swap_chips(part[:, :256]), part[:, 256:]
        other, mine = weight_parts[1]
        other = other + token((early,))
        weight_parts = [late, *add_cores([(other, mine)], token((small,)))]
    grad_counts = counts_back(
        cells, enc_pair, (high, low), recon, counts_in, factor, mask,
        after=[early, *weight_parts] if halves == 2 else ()
    )
    if halves == 2:
        grad_w_out = join_cores(order, grad_w_out, token((early, weight_parts[1]))).T
    else:
        grad_w_out = join_cores(order, grad_w_out, 0.0).T
    if halves == 2:
        zero = token((grad_counts,))
        weight_parts = [early] + [swap_chips(part, zero) for part in weight_parts]
    grad_w_enc = join_cores(order, weight_parts, 0.0).T
    term_w_dec = small[:latent]
    grad_w_lat = small[latent : 3 * latent]
    lines = -(-latent // share)
    gram_z = small[3 * latent : -lines].reshape(-1)[: latent * latent]
    gram_z = gram_z.reshape(latent, latent)
    sum_z = small[-lines:].reshape(-1)[:latent]
    grad_shift2 = hidden_part(sums2[0])
    grad_gain2 = hidden_part(sums2[1])
    rstd2 = hidden_part(lax.rsqrt(var2 + BN_EPS))
    cov_z = gram_z - sum_z[:, None] * (sum_z / cells)[None, :]
    pair_w_dec = rstd2[None, :] * jnp.dot(
        cov_z, hidden_part(w_dec), precision=lax.Precision.HIGHEST
    )
    sum_z = sum_z + cells * b_lat[:latent]
    grad_w_dec = (hidden_part(gain_dec) * rstd2)[None, :] * (
        term_w_dec
        - sum_z[:, None] * (grad_shift2 / cells)[None, :]
        - pair_w_dec * (grad_gain2 / cells)[None, :]
    )

    correct = cells / (cells - 1.0)
    new_mean_enc = (1.0 - MOMENTUM) * mean_enc + MOMENTUM * hidden_part(mean1)
    new_var_enc = (1.0 - MOMENTUM) * var_enc + MOMENTUM * hidden_part(var1) * correct
    new_mean_dec = (1.0 - MOMENTUM) * mean_dec + MOMENTUM * mean2
    new_var_dec = (1.0 - MOMENTUM) * var_dec + MOMENTUM * var2 * correct
    return (
        recon,
        grad_counts,
        grad_w_enc,
        hidden_part(sums1[1]),
        hidden_part(sums1[0]),
        grad_w_lat,
        grad_b_lat,
        grad_w_dec,
        grad_gain2,
        grad_shift2,
        grad_w_out,
        grad_b_out,
        new_mean_enc,
        new_var_enc,
        new_mean_dec,
        new_var_dec,
    )


def solution(mesh):
    return jax.shard_map(
        on_device,
        mesh=mesh,
        in_specs=(
            P(GENE, BATCH),
            P(BATCH),
            P(GENE),
            P(None, BATCH),
            P(GENE, None),
            P(GENE),
            P(GENE),
            P(),
            P(),
            P(),
            P(),
            P(),
            P(GENE, None),
            P(GENE),
            P(GENE),
            P(GENE),
            P(),
            P(),
        ),
        out_specs=(
            P(GENE, BATCH),
            P(GENE, BATCH),
            P(GENE, None),
            P(GENE),
            P(GENE),
            P(None, GENE),
            P(),
            P(None, GENE),
            P(GENE),
            P(GENE),
            P(GENE, None),
            P(GENE),
            P(GENE),
            P(GENE),
            P(),
            P(),
        ),
        check_vma=False,
    )
```

```python
import jax
import jax.numpy as jnp
from jax import lax
from jax.experimental import pallas as pl
from jax.experimental.pallas import tpu as pltpu
from jax.sharding import PartitionSpec as P

ALPHA = 0.002
BN_EPS = 1e-05
MOMENTUM = 0.1
UMI_SCALE = 10000.0
BATCH = "batch"
GENE = "gene"
TILE = 512
HALF = 256
ROWS = 16
VMEM_BYTES = 56 << 20
F32 = jnp.float32


BF16 = jnp.bfloat16
RATE = 600_000_000


def split(value):
    high = value.astype(BF16)
    return high, (value - high.astype(F32)).astype(BF16)


def whole(pair):
    return pair[0].astype(F32) + pair[1].astype(F32)


def dot(left, right, left_dim, right_dim):
    def one(a, b):
        return lax.dot_general(
            a,
            b,
            (((left_dim,), (right_dim,)), ((), ())),
            preferred_element_type=F32,
        )

    return one(left[0], right[0]) + (one(left[0], right[1]) + one(left[1], right[0]))


def kernel_call(
    body, grid, in_specs, out_specs, out_shape, micros, order=None, scratch=(), after=(),
    onto=(),
):
    leading = 0 if order is None else 1
    held = leading + len(in_specs)

    def run(*refs):
        body(*refs[:held], *refs[held + len(after) :])

    call = pl.pallas_call(
        run,
        grid_spec=pltpu.PrefetchScalarGridSpec(
            num_scalar_prefetch=leading,
            grid=grid,
            in_specs=list(in_specs) + [pl.BlockSpec(memory_space=pl.ANY)] * len(after),
            out_specs=out_specs,
            scratch_shapes=list(scratch),
        ),
        out_shape=out_shape,
        input_output_aliases={held + k: out for k, out in enumerate(onto)},
        compiler_params=pltpu.CompilerParams(vmem_limit_bytes=VMEM_BYTES),
        cost_estimate=pl.CostEstimate(
            flops=int(micros * RATE), bytes_accessed=1024, transcendentals=0
        ),
    )
    prefetch = () if order is None else (order,)
    return lambda *args: call(*prefetch, *args, *after)


def shape(*dims, dtype=F32):
    return jax.ShapeDtypeStruct(dims, dtype)


def full(*dims):
    return pl.BlockSpec(dims, lambda *_: (0,) * len(dims))


def tile(rows):
    return pl.BlockSpec((rows, TILE), lambda j, *_: (0, j))


def pair_of(spec):
    return [spec, spec]


def sigmoid(value):
    return 0.5 * jnp.tanh(0.5 * value) + 0.5


def silu_pair(value):
    sig = sigmoid(value)
    act = value * sig
    return act, sig + act * (1.0 - sig)


def start_or_add(ref, value, first):
    @pl.when(first)
    def _():
        ref[...] = value

    @pl.when(jnp.logical_not(first))
    def _():
        ref[...] += value


def fold(value):
    width = value.shape[1]
    if width % 128:
        return jnp.broadcast_to(
            jnp.sum(value, axis=1, keepdims=True) / 128.0, (value.shape[0], 128)
        )
    return sum(
        value[:, at : at + 128] for at in range(128, width, 128)
    ) + value[:, :128] if width > 128 else value


def rows_of(*folded):
    return jnp.concatenate(
        [jnp.sum(value, axis=1, keepdims=True) for value in folded], axis=1
    ).T


def moments(pre):
    mean = jnp.mean(pre, axis=1, keepdims=True)
    cent = pre - mean
    return jnp.concatenate(
        [mean, jnp.sum(cent * cent, axis=1, keepdims=True)], axis=1
    ).T


def wide(column):
    return jnp.concatenate([column] * (TILE // 128), axis=1)


def spread(column):
    return jnp.broadcast_to(column, (column.shape[0], 128))


def split_scaled(counts, factor, mask, high, low):
    column = mask[...].T
    scale = factor[...]
    for at in range(0, counts.shape[0], ROWS):
        rows = pl.ds(at, ROWS)
        high[rows, :], low[rows, :] = split(
            counts[rows, :] * scale * column[at : at + ROWS]
        )


def gene_cuts(genes):
    return [0, genes]


def turn_kernel(counts, factor, mask, *outs):
    turned = counts[...].T * factor[...].T * mask[...]
    cuts = gene_cuts(turned.shape[1])
    for place, (begin, end) in enumerate(zip(cuts, cuts[1:])):
        outs[2 * place][...], outs[2 * place + 1][...] = split(turned[:, begin:end])


def turn_counts(counts, factor, mask, after):
    genes, here = counts.shape
    cuts = gene_cuts(genes)
    widths = [end - begin for begin, end in zip(cuts, cuts[1:]) for _ in range(2)]
    out = kernel_call(
        turn_kernel,
        (here // TILE,),
        [tile(genes), tile(1), full(1, genes)],
        [pl.BlockSpec((TILE, width), lambda j: (j, 0)) for width in widths],
        [shape(here, width, dtype=BF16) for width in widths],
        5,
        after=after,
    )(counts, factor, mask)
    return [tuple(out[2 * k : 2 * k + 2]) for k in range(len(out) // 2)]


def encode_kernel(order, counts, factor, mask, w_enc_t, *refs):
    *outs, high, low, scaled_high, scaled_low = refs
    step = pl.program_id(0)

    @pl.when(step == 0)
    def _():
        for at in range(0, high.shape[0], ROWS):
            rows = pl.ds(at, ROWS)
            high[rows, :], low[rows, :] = split(w_enc_t[rows, :])

    split_scaled(counts, factor, mask, scaled_high, scaled_low)
    product = dot(
        (high[...], low[...]), (scaled_high[...], scaled_low[...]), 1, 0
    )
    side = order[0] == 0
    for place in range(len(outs) // 3):
        other, own, both = outs[3 * place : 3 * place + 3]
        rows = other.shape[0]

        @pl.when(step == place)
        def _():
            if rows < product.shape[0]:
                both[...] = product[rows:]

        @pl.when((step == place) & side)
        def _():
            other[...] = product[:rows, HALF:]
            own[...] = product[:rows, :HALF]

        @pl.when((step == place) & jnp.logical_not(side))
        def _():
            other[...] = product[:rows, :HALF]
            own[...] = product[:rows, HALF:]


def encode_products(side, order, counts, factor, mask, w_enc_t, rest, after=()):
    genes = counts.shape[0]
    hidden = w_enc_t.shape[0]
    blocks = order.shape[0]
    cells = lambda j, order: (0, order[j + 1])
    sizes = [(hidden - rest, HALF)] * 2 + [(max(rest, 8), TILE)]
    return kernel_call(
        encode_kernel,
        (blocks,),
        [
            pl.BlockSpec((genes, TILE), cells),
            pl.BlockSpec((1, TILE), cells),
            full(1, genes),
            full(hidden, genes),
        ],
        [full(*size) for size in sizes] * blocks,
        [shape(*size) for size in sizes] * blocks,
        4 * blocks,
        order=jnp.concatenate([side[None], order]).astype(jnp.int32),
        scratch=[pltpu.VMEM((hidden, genes), BF16)] * 2
        + [pltpu.VMEM((genes, TILE), BF16)] * 2,
        after=after,
    )(counts, factor, mask, w_enc_t)


def prepare_kernel(w_out_t, w_enc_t, w_lat, w_dec, out_high, out_low, turn_high, turn_low,
                   enc_high, enc_low, lat_high, lat_low, tal_high, tal_low,
                   dec_high, dec_low):
    out_high[...], out_low[...] = split(w_out_t[...])
    turn_high[...], turn_low[...] = split(w_out_t[...].T)
    enc_high[...], enc_low[...] = split(w_enc_t[...].T)
    lat_high[...], lat_low[...] = split(w_lat[...])
    tal_high[...], tal_low[...] = split(w_lat[...].T)
    dec_high[...], dec_low[...] = split(w_dec[...].T)


def prepare(w_out_t, w_enc_t, w_lat, w_dec, after):
    hidden, genes = w_out_t.shape
    latents, latent = w_lat.shape[0], w_dec.shape[0]
    sizes = [
        (hidden, genes),
        (genes, hidden),
        (genes, hidden),
        (latents, hidden),
        (hidden, latents),
        (hidden, latent),
    ]
    out = kernel_call(
        prepare_kernel,
        (),
        pair_of(full(hidden, genes)) + [full(latents, hidden), full(latent, hidden)],
        [full(*size) for size in sizes for _ in range(2)],
        [shape(*size, dtype=BF16) for size in sizes for _ in range(2)],
        6,
        after=after,
    )(w_out_t, w_enc_t, w_lat, w_dec)
    return [tuple(out[2 * k : 2 * k + 2]) for k in range(len(sizes))]


def own_kernel(main, *refs):
    *parts, pre_out, stats = refs
    rows = parts[0].shape[0]
    pre_out[:rows] = sum(part[...] for part in parts[1:main]) + parts[0][...]
    if main < len(parts):
        pre_out[rows:] = sum(part[...] for part in parts[main:])
    stats[...] = moments(pre_out[...])


def own_moments(parts, rest, after=()):
    rows, columns = parts[0].shape
    rows += rest[0].shape[0] if rest else 0
    return kernel_call(
        lambda *refs: own_kernel(len(parts), *refs),
        (),
        [full(*part.shape) for part in (*parts, *rest)],
        [full(rows, columns), full(2, rows)],
        [shape(rows, columns), shape(2, rows)],
        3,
        after=after,
    )(*parts, *rest)


def normalize(pre, vector):
    columns = vector.T
    norm = (pre - columns[:, 0:1]) * lax.rsqrt(columns[:, 1:2] + BN_EPS)
    return norm, norm * columns[:, 2:3] + columns[:, 3:4]


def latent_kernel(pre, vector, lat_high, lat_low, b_lat, noise, z_out):
    _, value = normalize(pre[...], vector[...])
    act, _ = silu_pair(value)
    lat = dot((lat_high[...], lat_low[...]), split(act), 1, 0) + b_lat[...].T
    latent = noise.shape[0]
    z_out[...] = lat[:latent] + jnp.exp(0.5 * lat[latent:]) * noise[...]


def latent_own(pre, vector, lat_pair, b_lat, noise):
    return kernel_call(
        latent_kernel,
        (),
        [full(*a.shape) for a in (pre, vector, *lat_pair, b_lat, noise)],
        full(*noise.shape),
        shape(*noise.shape),
        3,
    )(pre, vector, *lat_pair, b_lat, noise)


def sides(order, mine, other):
    left = order[0] == 0
    return jnp.concatenate(
        [jnp.where(left, mine, other), jnp.where(left, other, mine)], axis=1
    )


def hidden_kernel(order, dec_high, dec_low, mine, other, z_all, pre_out, stats,
                  sums):
    for step in range(mine.shape[0]):
        spot = order[step + 1]
        z = sides(order, mine[spot], other[spot])
        columns = pl.ds(step * TILE, TILE)
        z_all[:, columns] = z
        pre = dot((dec_high[...], dec_low[...]), split(z), 1, 0)
        pre_out[:, columns] = pre
        if step == 0:
            sums[...] = fold(pre)
        else:
            sums[...] += fold(pre)
    hidden, here = pre_out.shape
    mean = jnp.sum(sums[...], axis=1, keepdims=True) * (1.0 / here)
    sums[...] = spread(mean)
    squares = []
    for at in range(0, hidden, ROWS):
        rows = pl.ds(at, ROWS)
        total = jnp.zeros((ROWS, 128), F32)
        for step in range(mine.shape[0]):
            cent = pre_out[rows, pl.ds(step * TILE, TILE)] - wide(sums[rows, :])
            total = total + fold(cent * cent)
        squares.append(total)
    square = jnp.sum(jnp.concatenate(squares, axis=0), axis=1, keepdims=True)
    stats[...] = jnp.concatenate([mean, square], axis=1).T


def decoder_hidden(order, dec_pair, mine, other):
    hidden, latent = dec_pair[0].shape
    cells = 2 * mine.shape[0] * HALF
    return kernel_call(
        hidden_kernel,
        (1,),
        pair_of(full(hidden, latent)) + [full(*mine.shape), full(*other.shape)],
        [full(latent, cells), full(hidden, cells), full(2, hidden)],
        [shape(latent, cells), shape(hidden, cells), shape(2, hidden)],
        8,
        order=order,
        scratch=[pltpu.VMEM((hidden, 128), F32)],
    )(*dec_pair, mine, other)


def decoder_kernel(cells, order, pre, vector, z, out_high, out_low, turn_high, turn_low,
                   counts, factor, mask, b_out, w_dec,
                   recon_out, grad_high, grad_low, act_high, act_low, z_other, z_own,
                   weight_out, sums, bias_out,
                   sum_term, sum_gain, sum_grad, mean_w, scale_w, shift_w, mask_w, bias_w,
                   dec_high, dec_low, slope, product, term_high, term_low):
    step = pl.program_id(0)
    hidden, genes = out_high.shape

    @pl.when(step == 0)
    def _():
        columns = vector[...].T
        rstd = lax.rsqrt(columns[:, 1:2] + BN_EPS)
        mean_w[...] = spread(columns[:, 0:1])
        scale_w[...] = spread(rstd * columns[:, 2:3])
        shift_w[...] = spread(columns[:, 3:4])
        mask_w[...] = spread(mask[...].T * (1.0 / cells))
        bias_w[...] = spread(b_out[...].T)
        dec_high[...], dec_low[...] = split(
            w_dec[...] * (vector[2:3, :] * lax.rsqrt(vector[1:2, :] + BN_EPS))
        )
        for ref in (sum_term, sum_gain, sum_grad, weight_out):
            ref[...] = jnp.zeros_like(ref)

    for at in range(0, hidden, ROWS):
        rows = pl.ds(at, ROWS)
        cent = pre[rows, :] - wide(mean_w[rows, :])
        act, slope[rows, :] = silu_pair(
            cent * wide(scale_w[rows, :]) + wide(shift_w[rows, :])
        )
        act_high[rows, :], act_low[rows, :] = split(act)
    product[:genes, :] = dot(
        (turn_high[...], turn_low[...]), (act_high[...], act_low[...]), 1, 0
    )
    scale = factor[...]
    for at in range(0, genes, ROWS):
        rows = pl.ds(at, ROWS)
        out = product[rows, :] + wide(bias_w[rows, :])
        recon = jnp.maximum(out, 0.0) + jnp.log(1.0 + jnp.exp(-jnp.abs(out)))
        recon_out[rows, :] = recon
        grad = (recon - counts[rows, :] * scale) * (wide(mask_w[rows, :]) * sigmoid(out))
        sum_grad[rows, :] += fold(grad)
        grad_high[rows, :], grad_low[rows, :] = split(grad)
    product[:hidden, :] = dot(
        (out_high[...], out_low[...]), (grad_high[...], grad_low[...]), 1, 0
    )
    for at in range(0, hidden, ROWS):
        rows = pl.ds(at, ROWS)
        term = product[rows, :] * slope[rows, :]
        cent = pre[rows, :] - wide(mean_w[rows, :])
        sum_term[rows, :] += fold(term)
        sum_gain[rows, :] += fold(term * cent)
        term_high[rows, :], term_low[rows, :] = split(term)
    terms = term_high[...], term_low[...]
    back = dot((dec_high[...], dec_low[...]), terms, 1, 0)
    left = order[0] == 0
    z_other[...] = jnp.where(left, back[:, HALF:], back[:, :HALF])
    z_own[...] = jnp.where(left, back[:, :HALF], back[:, HALF:])
    weight_out[...] += dot(terms, split(z[...]), 1, 1)

    @pl.when(step == pl.num_programs(0) - 1)
    def _():
        rstd = lax.rsqrt(vector[1:2, :] + BN_EPS)
        both = rows_of(sum_term[...], sum_gain[...])
        sums[...] = jnp.concatenate([both[0:1], both[1:2] * rstd], axis=0)
        bias_out[...] = rows_of(sum_grad[...])


def decoder(cells, order, pre, vector, z, out_pair, turn_pair, counts, factor, mask, b_out,
            w_dec):
    hidden, genes = out_pair[0].shape
    here = counts.shape[1]
    latent = w_dec.shape[0]
    most = max(hidden, genes)
    placed = pl.BlockSpec((latent, HALF), lambda j, order: (0, order[j + 1]))
    return kernel_call(
        lambda *refs: decoder_kernel(cells, *refs),
        (here // TILE,),
        [tile(hidden), full(4, hidden), tile(latent)]
        + pair_of(full(hidden, genes))
        + pair_of(full(genes, hidden))
        + [
            tile(genes),
            tile(1),
            full(1, genes),
            full(1, genes),
            full(latent, hidden),
        ],
        [tile(genes)]
        + pair_of(tile(genes))
        + pair_of(tile(hidden))
        + pair_of(placed)
        + [full(hidden, latent), full(2, hidden), full(1, genes)],
        [shape(genes, here)]
        + [shape(genes, here, dtype=BF16)] * 2
        + [shape(hidden, here, dtype=BF16)] * 2
        + [shape(latent, here // 2)] * 2
        + [shape(hidden, latent), shape(2, hidden), shape(1, genes)],
        42,
        order=order,
        scratch=[pltpu.VMEM((hidden, 128), F32)] * 2
        + [pltpu.VMEM((genes, 128), F32)]
        + [pltpu.VMEM((hidden, 128), F32)] * 3
        + [pltpu.VMEM((genes, 128), F32)] * 2
        + [pltpu.VMEM((latent, hidden), BF16)] * 2
        + [pltpu.VMEM((hidden, TILE), F32), pltpu.VMEM((most, TILE), F32)]
        + [pltpu.VMEM((hidden, TILE), BF16)] * 2,
    )(pre, vector, z, *out_pair, *turn_pair, counts, factor, mask, b_out, w_dec)


def start_halves(order, product, outs, first):
    if len(outs) == 1:
        start_or_add(outs[0], product, first)
        return
    rows = product.shape[0] // 2
    upper = order[0] != 0

    @pl.when(upper)
    def _():
        start_or_add(outs[0], product[rows:], first)
        start_or_add(outs[1], product[:rows], first)

    @pl.when(jnp.logical_not(upper))
    def _():
        start_or_add(outs[0], product[:rows], first)
        start_or_add(outs[1], product[rows:], first)


def weight_kernel(right_dim, order, left_high, left_low, right_high, right_low, *outs):
    product = dot(
        (left_high[...], left_low[...]), (right_high[...], right_low[...]), 1, right_dim
    )
    start_halves(order, product, outs, pl.program_id(0) == 0)


def weight_halves(order, halves, left, right, right_dim, width, after=()):
    hidden, here = left[0].shape
    rows = hidden // halves
    genes = right[0].shape[1 - right_dim]
    if right_dim:
        cells = pl.BlockSpec((genes, width), lambda j, order: (0, j))
    else:
        cells = pl.BlockSpec((width, genes), lambda j, order: (j, 0))
    return kernel_call(
        lambda *refs: weight_kernel(right_dim, *refs),
        (here // width,),
        pair_of(pl.BlockSpec((hidden, width), lambda j, order: (0, j))) + pair_of(cells),
        [full(rows, genes)] * halves,
        [shape(rows, genes)] * halves,
        10,
        order=order,
        after=after,
    )(*left, *right)


def latent_weight_kernel(lat, part, vector, out):
    _, value = normalize(part[...], vector[...])
    act, _ = silu_pair(value)
    product = dot(split(lat[...]), split(act), 1, 1)
    start_or_add(out, product, pl.program_id(0) == 0)


def latent_weight(lat, part, vector, after):
    latents, here = lat.shape
    share = part.shape[0]
    return kernel_call(
        latent_weight_kernel,
        (here // 1024,),
        [
            pl.BlockSpec((latents, 1024), lambda j: (0, j)),
            pl.BlockSpec((share, 1024), lambda j: (0, j)),
            full(4, share),
        ],
        full(latents, share),
        shape(latents, share),
        4,
        after=after,
    )(lat, part, vector)


def again_kernel(pre_enc, vector, lat_high, lat_low, b_lat, z, later,
                 lat_out, slope_out, gram, sum_out, later_out, act_high, act_low):
    later_out[...] = later[...]
    first = pl.program_id(0) == 0
    moved = z[...] - b_lat[:, : z.shape[0]].T
    pair = split(moved)
    start_or_add(gram, dot(pair, pair, 1, 1), first)
    start_or_add(sum_out, rows_of(moved), first)
    columns = vector[...].T
    scale = lax.rsqrt(columns[:, 1:2] + BN_EPS) * columns[:, 2:3]
    for at in range(0, pre_enc.shape[0], ROWS):
        rows = pl.ds(at, ROWS)
        part = slice(at, at + ROWS)
        act, slope_out[rows, :] = silu_pair(
            (pre_enc[rows, :] - columns[part, 0:1]) * scale[part] + columns[part, 3:4]
        )
        act_high[rows, :], act_low[rows, :] = split(act)
    lat_out[...] = (
        dot((lat_high[...], lat_low[...]), (act_high[...], act_low[...]), 1, 0)
        + b_lat[...].T
    )


def encode_again(pre_enc, vector, lat_pair, b_lat, z, later, after=()):
    latent = z.shape[0]
    hidden, here = pre_enc.shape
    latents = lat_pair[0].shape[0]
    return kernel_call(
        again_kernel,
        (here // TILE,),
        [tile(hidden), full(4, hidden)]
        + pair_of(full(latents, hidden))
        + [full(1, latents), tile(latent), full(*later.shape)],
        [
            tile(latents),
            tile(hidden),
            full(latent, latent),
            full(1, latent),
            full(*later.shape),
        ],
        [
            shape(latents, here),
            shape(hidden, here),
            shape(latent, latent),
            shape(1, latent),
            shape(*later.shape),
        ],
        10,
        scratch=[pltpu.VMEM((hidden, TILE), BF16)] * 2,
        after=after,
    )(pre_enc, vector, *lat_pair, b_lat, z, later)


def fix_kernel(cells, w_dec, vector, sums, b_lat, matrix_out, column_out):
    weight = w_dec[...]
    rstd = lax.rsqrt(vector[1:2, :] + BN_EPS)
    scaled = weight * (vector[2:3, :] * rstd * (1.0 / cells))
    gained = scaled * (sums[1:2, :] * rstd)
    matrix_out[...] = dot(split(gained), split(weight), 1, 1)
    bias = b_lat[:, : weight.shape[0]].T
    mean = vector[0:1, :] - jnp.sum(weight * bias, axis=0, keepdims=True)
    column_out[...] = spread(
        jnp.sum(scaled * sums[0:1, :] - gained * mean, axis=1, keepdims=True)
    )


def fix_terms(cells, w_dec, vector, sums, b_lat):
    latent, hidden = w_dec.shape
    return kernel_call(
        lambda *refs: fix_kernel(cells, *refs),
        (),
        [full(latent, hidden), full(4, hidden), full(2, hidden), full(*b_lat.shape)],
        [full(latent, latent), full(latent, 128)],
        [shape(latent, latent), shape(latent, 128)],
        2,
    )(w_dec, vector, sums, b_lat)


def latent_back_kernel(cells, order, mine, other, z, matrix, column, b_lat, lat, noise,
                       tal_high, tal_low, slope, pre, vector, grad_out, sums, lat_out, bias_out,
                       sum_grad, sum_gain, sum_lat, product):
    step = pl.program_id(0)

    @pl.when(step == 0)
    def _():
        for ref in (sum_grad, sum_gain, sum_lat):
            ref[...] = jnp.zeros_like(ref)

    latent = noise.shape[0]
    moved = z[...] - b_lat[:, :latent].T
    fix = dot(split(matrix[...]), split(moved), 1, 0) + wide(column[...])
    grad_z = sides(order, mine[:latent, :], other[:latent, :]) - fix
    mu = lat[:latent, :]
    spread_z = jnp.exp(0.5 * lat[latent:, :])
    grad_mu = grad_z + (ALPHA / cells) * mu
    grad_logvar = 0.5 * grad_z * noise[...] * spread_z + (0.5 * ALPHA / cells) * (
        spread_z * spread_z - 1.0
    )
    grad_lat = jnp.concatenate([grad_mu, grad_logvar], axis=0)
    lat_out[...] = grad_lat
    sum_lat[...] += fold(grad_lat)
    product[...] = dot((tal_high[...], tal_low[...]), split(grad_lat), 1, 0)
    mean = vector[0:1, :].T
    for at in range(0, product.shape[0], ROWS):
        rows = pl.ds(at, ROWS)
        grad = product[rows, :] * slope[rows, :]
        grad_out[rows, :] = grad
        sum_grad[rows, :] += fold(grad)
        sum_gain[rows, :] += fold(grad * (pre[rows, :] - mean[at : at + ROWS]))

    @pl.when(step == pl.num_programs(0) - 1)
    def _():
        both = rows_of(sum_grad[...], sum_gain[...])
        sums[...] = jnp.concatenate(
            [both[0:1], both[1:2] * lax.rsqrt(vector[1:2, :] + BN_EPS)], axis=0
        )
        bias_out[...] = rows_of(sum_lat[...])


def latent_back(cells, order, mine, other, z, fix, b_lat, lat, noise, tal_pair, slope, pre,
                vector, after=()):
    hidden, here = pre.shape
    latents = lat.shape[0]
    latent = noise.shape[0]
    block = pl.BlockSpec(
        (None, mine.shape[1], HALF), lambda j, order: (order[j + 1], 0, 0)
    )
    return kernel_call(
        lambda *refs: latent_back_kernel(cells, *refs),
        (here // TILE,),
        [block, block, tile(latent), full(latent, latent), full(latent, 128)]
        + [full(1, latents), tile(latents), tile(latent)]
        + pair_of(full(hidden, latents))
        + [tile(hidden), tile(hidden), full(4, hidden)],
        [tile(hidden), full(2, hidden), tile(latents), full(1, latents)],
        [
            shape(hidden, here),
            shape(2, hidden),
            shape(latents, here),
            shape(1, latents),
        ],
        12,
        order=order,
        scratch=[
            pltpu.VMEM((hidden, 128), F32),
            pltpu.VMEM((hidden, 128), F32),
            pltpu.VMEM((latents, 128), F32),
            pltpu.VMEM((hidden, TILE), F32),
        ],
        after=after,
    )(mine, other, z, *fix, b_lat, lat, noise, *tal_pair, slope, pre, vector)


def encoder_weight_kernel(cells, order, grad_in, pre, vector, scaled_high, scaled_low,
                          high, low, *outs):
    columns = vector[...].T
    scale = lax.rsqrt(columns[:, 1:2] + BN_EPS)
    outer = columns[:, 2:3] * scale
    shift = columns[:, 4:5] * (1.0 / cells)
    gain = columns[:, 5:6] * (1.0 / cells) * scale
    for at in range(0, grad_in.shape[0], ROWS):
        rows = pl.ds(at, ROWS)
        part = slice(at, at + ROWS)
        grad = outer[part] * (
            grad_in[rows, :]
            - shift[part]
            - (pre[rows, :] - columns[part, 0:1]) * gain[part]
        )
        high[rows, :], low[rows, :] = split(grad)
    product = dot((high[...], low[...]), (scaled_high[...], scaled_low[...]), 1, 0)
    start_halves(order, product, outs, pl.program_id(0) == 0)


def encoder_weight(cells, order, halves, grad_in, pre, vector, scaled, after):
    hidden, here = pre.shape
    genes = scaled[0].shape[1]
    rows = hidden // halves
    return kernel_call(
        lambda *refs: encoder_weight_kernel(cells, *refs),
        (here // TILE,),
        [tile(hidden), tile(hidden), full(6, hidden)]
        + pair_of(pl.BlockSpec((TILE, genes), lambda j, order: (j, 0))),
        pair_of(tile(hidden)) + [full(rows, genes)] * halves,
        [shape(hidden, here, dtype=BF16)] * 2 + [shape(rows, genes)] * halves,
        12,
        order=order,
        after=after,
    )(grad_in, pre, vector, *scaled)


def counts_kernel(cells, enc_high, enc_low, high, low, recon, counts, factor, mask, out,
                  product):
    product[...] = dot((enc_high[...], enc_low[...]), (high[...], low[...]), 1, 0)
    mask_column = mask[...].T
    scale = factor[...]
    for at in range(0, out.shape[0], ROWS):
        rows = pl.ds(at, ROWS)
        column = mask_column[at : at + ROWS]
        diff = (recon[rows, :] - counts[rows, :] * scale) * (column * (1.0 / cells))
        out[rows, :] = (product[rows, :] - diff) * (scale * column)


def counts_back(cells, enc_pair, grads, recon, counts, factor, mask, after=()):
    genes, hidden = enc_pair[0].shape
    here = counts.shape[1]
    return kernel_call(
        lambda *refs: counts_kernel(cells, *refs),
        (here // TILE,),
        pair_of(full(genes, hidden))
        + pair_of(tile(hidden))
        + [tile(genes), tile(genes), tile(1), full(1, genes)],
        tile(genes),
        shape(genes, here),
        16,
        scratch=[pltpu.VMEM((genes, TILE), F32)],
        after=after,
    )(*enc_pair, *grads, recon, counts, factor, mask)


def token_kernel(out):
    out[...] = jnp.zeros_like(out)


def token(after):
    return kernel_call(
        token_kernel, (), [], full(1, 1), shape(1, 1), 0, after=after
    )()[0, 0]


def swap(value, axis, bit):
    size = lax.axis_size(axis)
    return lax.ppermute(value, axis, [(i, i ^ bit) for i in range(size)])


def bits(axis):
    size, bit, out = lax.axis_size(axis), 1, []
    while bit < size:
        out.append(bit)
        bit *= 2
    return out


def add_all(value, axes):
    for axis in axes:
        for bit in bits(axis):
            value = value + swap(value, axis, bit)
    return value


def moments_all(both, count, axes, others=None):
    for axis in axes:
        if axis == GENE and others is not None:
            both = jnp.concatenate([both, others])
        for bit in bits(axis):
            other = swap(both, axis, bit)
            gap = both[0] - other[0]
            rows = [
                0.5 * (both[0] + other[0]),
                both[1] + other[1] + gap * gap * (0.5 * count),
            ]
            both = jnp.concatenate([jnp.stack(rows), both[2:] + other[2:]])
            count = 2 * count
    return both[0], both[1] / count, both[2:]


def rows_wide(vector, share):
    size = vector.shape[0]
    lines = -(-size // share)
    return jnp.pad(vector, (0, lines * share - size)).reshape(lines, share)


def halve_blocks(value, bit):
    half = value.shape[0] // 2
    upper = (lax.axis_index(GENE) & bit) != 0
    sent = jnp.where(upper, value[:half], value[half:])
    kept = jnp.where(upper, value[half:], value[:half])
    return kept + swap(sent, GENE, bit)


def gene_pairs(links):
    return [(2 * a + y, 2 * b + y) for a, b in links for y in (0, 1)]


OUTER = gene_pairs([(0, 1), (3, 2)])
MIDDLE = gene_pairs([(1, 2), (2, 1)])
SIDES = gene_pairs([(0, 1), (1, 0), (2, 3), (3, 2)])


def line_order(z):
    low = z < 2
    return [
        jnp.where(low, z + 3, z + 1) % 4,
        (z + 2) % 4,
        jnp.where(low, z + 1, z + 3) % 4,
        z,
    ]


def by_line(here):
    return lax.axis_size(GENE) == 8 and here == 8 * HALF


def scatter_encoded(counts, factor, mask, w_enc_t, others):
    here = counts.shape[1]
    hidden = w_enc_t.shape[0]
    me = lax.axis_index(GENE)
    if not by_line(here):
        side = 0 * me
        order = jnp.arange(here // TILE, dtype=jnp.int32)
        blocks = encode_products(side, order, counts, factor, mask, w_enc_t, 0)
        pre = [blocks[3 * k + i] for k in range(len(blocks) // 3) for i in (1, 0)]
        pre = lax.psum_scatter(
            jnp.concatenate(pre, axis=1), GENE, scatter_dimension=1, tiled=True
        )
        scaled = turn_counts(counts, factor, mask, (blocks[0],))
        return [pre], [], scaled, prepare(*others, scaled[0])
    z, y = me // 2, me % 2
    rest = hidden // 6 // 16 * 16
    order = jnp.stack(line_order(z)).astype(jnp.int32)

    def products(first, last, after=()):
        return encode_products(
            y, order[first:last], counts, factor, mask, w_enc_t, rest, after
        )

    middle = (z == 1) | (z == 2)
    blocks = products(0, 1)
    step1 = lax.ppermute(blocks[2], GENE, OUTER)
    blocks += products(1, 2, (step1,))
    blocks += products(2, 3, blocks[3:4])
    blocks += products(3, 4, blocks[6:7])
    part = [blocks[3 * k + 1] + swap(blocks[3 * k], GENE, 1) for k in range(4)]
    tail = blocks[2::3]
    step2 = lax.ppermute(tail[1], GENE, OUTER)
    across = lax.ppermute(tail[1] + step1, GENE, MIDDLE)
    scaled = turn_counts(counts, factor, mask, (step2, across, blocks[6]))
    side = lax.ppermute(jnp.where(middle, tail[0] + across, tail[2]), GENE, SIDES)
    inner = lax.ppermute(tail[2] + step2, GENE, MIDDLE)
    weights = prepare(*others, (side, inner, scaled[0][0]))
    tail = tail[3] + side + inner
    left, right = tail[:, :HALF], tail[:, HALF:]
    mine = jnp.where(y == 0, left, right)
    step1 = lax.ppermute(part[0], GENE, OUTER)
    step2 = lax.ppermute(part[1], GENE, OUTER)
    across = lax.ppermute(part[1] + step1, GENE, MIDDLE)
    side = lax.ppermute(jnp.where(middle, part[0] + across, part[2]), GENE, SIDES)
    inner = lax.ppermute(part[2] + step2, GENE, MIDDLE)
    back = swap(jnp.where(y == 0, right, left), GENE, 1)
    return [part[3], side, inner], [mine, back], scaled, weights


def gather_blocks(value, before=None):
    rows, own = value.shape
    if not by_line(own * lax.axis_size(GENE)):
        value = lax.all_gather(value, GENE, axis=1, tiled=True)
        blocks = value.shape[1] // TILE
        stack = jnp.moveaxis(value.reshape(rows, blocks, 2, HALF), 0, 2)
        order = jnp.concatenate([jnp.zeros(1), jnp.arange(blocks)])
        return stack[:, 0], stack[:, 1], order.astype(jnp.int32)
    me = lax.axis_index(GENE)
    mine = jnp.stack([value] + [swap(value, GENE, bit) for bit in (2, 4, 6)])
    if before is not None:
        mine = mine + token(before)
    other = swap(mine, GENE, 1)
    order = jnp.concatenate([(me % 2)[None], (me // 2) ^ jnp.arange(4)])
    return mine, other, order.astype(jnp.int32)


def term_order(here):
    blocks = jnp.arange(here // TILE)
    if not by_line(here):
        return jnp.concatenate([jnp.zeros(1), blocks]).astype(jnp.int32)
    me = lax.axis_index(GENE)
    return jnp.concatenate([(me % 2)[None], ((me // 2 ^ blocks) + 3) % 4]).astype(
        jnp.int32
    )


def scatter_sides(other, own, sums):
    rows, half = own.shape
    if not by_line(2 * half):
        value = jnp.stack(
            [own.reshape(rows, -1, HALF), other.reshape(rows, -1, HALF)], axis=2
        ).reshape(rows, 2 * half)
        return value, add_all(sums, (BATCH, GENE))
    z = lax.axis_index(GENE) // 2
    sums = add_all(sums, (BATCH,))
    sums = sums + swap(sums, GENE, 1)
    quarter = sums.shape[1] // 4
    quarters = [
        jnp.pad(
            lax.dynamic_slice_in_dim(sums, (z ^ k) * quarter, quarter, 1),
            ((0, 0), (0, HALF - quarter)),
        )
        for k in (1, 2, 3, 0)
    ]
    return jnp.concatenate(
        [own + swap(other, GENE, 1), jnp.concatenate(quarters, axis=1)], axis=0
    ), sums


def scatter_terms(part, before):
    if not by_line(2 * part.shape[1]):
        return lax.psum_scatter(part, GENE, scatter_dimension=1, tiled=True)
    total = part[:, 3 * HALF :] + token(before)
    for k in (1, 2, 3):
        total = total + swap(part[:, (k - 1) * HALF : k * HALF], GENE, 2 * k)
    return total


def gather_sums(stack, sums):
    if stack.shape[0] != 4 or not by_line(8 * stack.shape[2]):
        return sums
    z = lax.axis_index(GENE) // 2
    quarter = sums.shape[1] // 4
    quarters = stack[:, -sums.shape[0] :, :quarter]
    return jnp.concatenate(
        [
            lax.dynamic_index_in_dim(quarters, z ^ place, 0, keepdims=False)
            for place in range(4)
        ],
        axis=1,
    )


def add_cores(chunks, zero):
    if len(chunks[0]) == 1:
        return chunks
    return [own + swap(other, BATCH, 1) + zero for other, own in chunks]


def swap_chips(part, zero=0.0):
    if lax.axis_size(BATCH) != 4:
        return part
    return part + swap(part, BATCH, 2) + zero


def join_cores(order, chunks, zero):
    if lax.axis_size(BATCH) != 4:
        return lax.psum(jnp.concatenate([chunk[0] for chunk in chunks], axis=1), BATCH)
    low = order[0] != 0
    other = [swap(part + zero, BATCH, 1) for part in chunks]
    return jnp.concatenate(
        [
            jnp.concatenate([jnp.where(low, a, b), jnp.where(low, b, a)], axis=0)
            for a, b in zip(chunks, other)
        ],
        axis=1,
    )


def on_device(
    counts_in,
    umi_total,
    gene_mask,
    noise,
    w_enc,
    gain_enc,
    shift_enc,
    w_lat,
    b_lat,
    w_dec,
    gain_dec,
    shift_dec,
    w_out,
    b_out,
    mean_enc,
    var_enc,
    mean_dec,
    var_dec,
):
    here = counts_in.shape[1]
    cells = here * lax.axis_size(BATCH)
    hidden = w_enc.shape[1]
    ranks = lax.axis_size(GENE)
    share = hidden // ranks
    own = here // ranks
    latent = noise.shape[0]
    me = lax.axis_index(GENE)
    both = (BATCH, GENE)
    core = lax.axis_index(BATCH) % 2
    halves = 2 if lax.axis_size(BATCH) == 4 else 1
    order = (1 - core).astype(jnp.int32)[None]

    def hidden_part(vector):
        return lax.dynamic_slice_in_dim(vector, me * share, share, vector.ndim - 1)

    def hidden_placed(part):
        empty = jnp.zeros((part.shape[0], hidden), F32)
        return lax.dynamic_update_slice_in_dim(empty, part, me * share, 1)

    factor = (UMI_SCALE / umi_total.astype(F32))[None, :]
    mask = gene_mask.astype(F32)[None, :]
    w_enc_t = w_enc.T
    w_out_t = w_out.T
    b_lat_row = b_lat[None, :]
    noise_own = lax.dynamic_slice_in_dim(noise, me * own, own, 1)

    parts, rest, scaled, weights = scatter_encoded(
        counts_in, factor, mask, w_enc_t, (w_out_t, w_enc_t, w_lat, w_dec)
    )
    out_pair, turn_pair, enc_pair, lat_pair, tal_pair, dec_pair = weights
    affine1 = hidden_placed(jnp.stack([gain_enc, shift_enc]))
    pre_own, stats1 = own_moments(
        parts, rest, after=(affine1, noise_own, out_pair[0])
    )
    mean1, var1, affine1 = moments_all(stats1, own, both, affine1)
    vector1 = jnp.concatenate([mean1[None], var1[None], affine1])
    part_vector = hidden_part(vector1)
    z_own = latent_own(pre_own, vector1, lat_pair, b_lat_row, noise_own)

    z_mine, z_other, z_order = gather_blocks(z_own)
    zero = token((z_mine, z_other))
    pre_enc = lax.all_gather(pre_own + zero, GENE, axis=1, tiled=True)
    z, pre_dec, stats2 = decoder_hidden(z_order, dec_pair, z_mine, z_other)
    mean2, var2, _ = moments_all(stats2, here, (BATCH,))
    vector2 = jnp.stack([mean2, var2, gain_dec, shift_dec])
    recon, grad_high, grad_low, act_high, act_low, *terms, term_w_dec, sums2, grad_b_out = (
        decoder(
            cells, term_order(here), pre_dec, vector2, z, out_pair, turn_pair, counts_in,
            factor, mask, b_out[None, :], w_dec
        )
    )

    part, sums2 = scatter_sides(*terms, sums2)
    grad_w_out = weight_halves(
        order, halves, (act_high, act_low), (grad_high, grad_low), 1, 1024, after=(part,)
    )
    total = scatter_terms(part, (grad_w_out[0],))
    zero = token((total,))
    grad_w_out = add_cores([[grad_w_out[0] + zero, *grad_w_out[1:]]], 0.0)
    lat, slope1, gram_z, sum_z, term_w_dec = encode_again(
        pre_enc, vector1, lat_pair, b_lat_row, z, term_w_dec
    )
    term_mine, term_other, z_order = gather_blocks(total, (lat,))
    sums2 = gather_sums(term_mine, sums2)
    fix_z = fix_terms(cells, w_dec, vector2, sums2, b_lat_row)

    when = []
    if halves == 2:
        cuts = [0, 256, 512, counts_in.shape[0]]
        last = grad_w_out[0][:, cuts[2] :]
        grad_w_out = [
            swap_chips(grad_w_out[0][:, a:b], token((time,)))
            for a, b, time in zip(cuts, cuts[1:], [lat, term_mine])
        ]
        when = grad_w_out

    steps = list(reversed(bits(GENE)))
    term_w_dec = halve_blocks(term_w_dec.reshape(ranks, share, latent), steps[0])

    grad_in1, sums1, grad_lat, grad_b_lat = latent_back(
        cells, z_order, term_mine, term_other, z, fix_z, b_lat_row, lat, noise, tal_pair,
        slope1, pre_enc, vector1, [*when, term_w_dec]
    )
    received = []
    if halves == 2:
        received = [swap(last, BATCH, 2)]
        grad_w_out = [*grad_w_out, last + received[0]]
    sums1 = add_all(
        jnp.concatenate([sums1.reshape(-1), grad_b_lat[0], grad_b_out[0]]),
        (BATCH,),
    )
    grad_b_lat = sums1[2 * hidden : 2 * hidden + 2 * latent]
    grad_b_out = sums1[2 * hidden + 2 * latent :]
    sums1 = sums1[: 2 * hidden].reshape(2, hidden)
    vector6 = jnp.concatenate([vector1, sums1])
    term_w_dec = halve_blocks(term_w_dec, steps[1])
    high, low, *weight_part = encoder_weight(
        cells, order, halves, grad_in1, pre_enc, vector6, scaled[0], [term_w_dec, *received]
    )
    for bit in steps[2:]:
        term_w_dec = halve_blocks(term_w_dec, bit)
    term_w_dec = term_w_dec[0].T
    after = ()
    if halves == 2:
        weight_part = add_cores([weight_part], 0.0)
        after = weight_part
    grad_counts = counts_back(
        cells, enc_pair, (high, low), recon, counts_in, factor, mask, after=after
    )
    zero = token((grad_counts,))
    if halves == 2:
        weight_part = [swap_chips(weight_part[0], zero)]
    else:
        weight_part = [weight_part]
    grad_w_out = join_cores(order, grad_w_out, zero).T
    grad_w_enc = join_cores(order, weight_part, 0.0).T
    grad_w_lat = latent_weight(
        grad_lat, lax.dynamic_slice_in_dim(pre_enc, me * share, share, 0),
        part_vector, (grad_counts,)
    )
    small = jnp.concatenate(
        [
            term_w_dec + zero,
            grad_w_lat,
            rows_wide(gram_z.reshape(-1), share),
            rows_wide(sum_z[0], share),
        ]
    )
    small = add_all(small, (BATCH,)) + (token(weight_part[:1]) if halves == 2 else 0.0)
    term_w_dec = small[:latent]
    grad_w_lat = small[latent : 3 * latent]
    lines = -(-latent // share)
    gram_z = small[3 * latent : -lines].reshape(-1)[: latent * latent]
    gram_z = gram_z.reshape(latent, latent)
    sum_z = small[-lines:].reshape(-1)[:latent]
    grad_shift2 = hidden_part(sums2[0])
    grad_gain2 = hidden_part(sums2[1])
    rstd2 = hidden_part(lax.rsqrt(var2 + BN_EPS))
    cov_z = gram_z - sum_z[:, None] * (sum_z / cells)[None, :]
    pair_w_dec = rstd2[None, :] * jnp.dot(
        cov_z, hidden_part(w_dec), precision=lax.Precision.HIGHEST
    )
    sum_z = sum_z + cells * b_lat[:latent]
    grad_w_dec = (hidden_part(gain_dec) * rstd2)[None, :] * (
        term_w_dec
        - sum_z[:, None] * (grad_shift2 / cells)[None, :]
        - pair_w_dec * (grad_gain2 / cells)[None, :]
    )

    correct = cells / (cells - 1.0)
    new_mean_enc = (1.0 - MOMENTUM) * mean_enc + MOMENTUM * hidden_part(mean1)
    new_var_enc = (1.0 - MOMENTUM) * var_enc + MOMENTUM * hidden_part(var1) * correct
    new_mean_dec = (1.0 - MOMENTUM) * mean_dec + MOMENTUM * mean2
    new_var_dec = (1.0 - MOMENTUM) * var_dec + MOMENTUM * var2 * correct
    return (
        recon,
        grad_counts,
        grad_w_enc,
        hidden_part(sums1[1]),
        hidden_part(sums1[0]),
        grad_w_lat,
        grad_b_lat,
        grad_w_dec,
        grad_gain2,
        grad_shift2,
        grad_w_out,
        grad_b_out,
        new_mean_enc,
        new_var_enc,
        new_mean_dec,
        new_var_dec,
    )


def solution(mesh):
    return jax.shard_map(
        on_device,
        mesh=mesh,
        in_specs=(
            P(GENE, BATCH),
            P(BATCH),
            P(GENE),
            P(None, BATCH),
            P(GENE, None),
            P(GENE),
            P(GENE),
            P(),
            P(),
            P(),
            P(),
            P(),
            P(GENE, None),
            P(GENE),
            P(GENE),
            P(GENE),
            P(),
            P(),
        ),
        out_specs=(
            P(GENE, BATCH),
            P(GENE, BATCH),
            P(GENE, None),
            P(GENE),
            P(GENE),
            P(None, GENE),
            P(),
            P(None, GENE),
            P(GENE),
            P(GENE),
            P(GENE, None),
            P(GENE),
            P(GENE),
            P(GENE),
            P(),
            P(),
        ),
        check_vma=False,
    )
```

```python
import jax
import jax.numpy as jnp
from jax import lax
from jax.experimental import pallas as pl
from jax.experimental.pallas import tpu as pltpu
from jax.sharding import PartitionSpec as P

ALPHA = 0.002
BN_EPS = 1e-05
MOMENTUM = 0.1
UMI_SCALE = 10000.0
BATCH = "batch"
GENE = "gene"
TILE = 512
HALF = 256
ROWS = 16
VMEM_BYTES = 56 << 20
F32 = jnp.float32


BF16 = jnp.bfloat16
RATE = 600_000_000


def split(value):
    high = value.astype(BF16)
    return high, (value - high.astype(F32)).astype(BF16)


def whole(pair):
    return pair[0].astype(F32) + pair[1].astype(F32)


def dot(left, right, left_dim, right_dim):
    def one(a, b):
        return lax.dot_general(
            a,
            b,
            (((left_dim,), (right_dim,)), ((), ())),
            preferred_element_type=F32,
        )

    return one(left[0], right[0]) + (one(left[0], right[1]) + one(left[1], right[0]))


def kernel_call(
    body, grid, in_specs, out_specs, out_shape, micros, order=None, scratch=(), after=(),
    onto=(),
):
    leading = 0 if order is None else 1
    held = leading + len(in_specs)

    def run(*refs):
        body(*refs[:held], *refs[held + len(after) :])

    call = pl.pallas_call(
        run,
        grid_spec=pltpu.PrefetchScalarGridSpec(
            num_scalar_prefetch=leading,
            grid=grid,
            in_specs=list(in_specs) + [pl.BlockSpec(memory_space=pl.ANY)] * len(after),
            out_specs=out_specs,
            scratch_shapes=list(scratch),
        ),
        out_shape=out_shape,
        input_output_aliases={held + k: out for k, out in enumerate(onto)},
        compiler_params=pltpu.CompilerParams(vmem_limit_bytes=VMEM_BYTES),
        cost_estimate=pl.CostEstimate(
            flops=int(micros * RATE), bytes_accessed=1024, transcendentals=0
        ),
    )
    prefetch = () if order is None else (order,)
    return lambda *args: call(*prefetch, *args, *after)


def shape(*dims, dtype=F32):
    return jax.ShapeDtypeStruct(dims, dtype)


def full(*dims):
    return pl.BlockSpec(dims, lambda *_: (0,) * len(dims))


def tile(rows):
    return pl.BlockSpec((rows, TILE), lambda j, *_: (0, j))


def pair_of(spec):
    return [spec, spec]


def sigmoid(value):
    return 0.5 * jnp.tanh(0.5 * value) + 0.5


def silu_pair(value):
    sig = sigmoid(value)
    act = value * sig
    return act, sig + act * (1.0 - sig)


def start_or_add(ref, value, first):
    @pl.when(first)
    def _():
        ref[...] = value

    @pl.when(jnp.logical_not(first))
    def _():
        ref[...] += value


def fold(value):
    width = value.shape[1]
    if width % 128:
        return jnp.broadcast_to(
            jnp.sum(value, axis=1, keepdims=True) / 128.0, (value.shape[0], 128)
        )
    return sum(
        value[:, at : at + 128] for at in range(128, width, 128)
    ) + value[:, :128] if width > 128 else value


def rows_of(*folded):
    return jnp.concatenate(
        [jnp.sum(value, axis=1, keepdims=True) for value in folded], axis=1
    ).T


def moments(pre):
    mean = jnp.mean(pre, axis=1, keepdims=True)
    cent = pre - mean
    return jnp.concatenate(
        [mean, jnp.sum(cent * cent, axis=1, keepdims=True)], axis=1
    ).T


def wide(column):
    return jnp.concatenate([column] * (TILE // 128), axis=1)


def spread(column):
    return jnp.broadcast_to(column, (column.shape[0], 128))


def split_scaled(counts, factor, mask, high, low):
    column = mask[...].T
    scale = factor[...]
    for at in range(0, counts.shape[0], ROWS):
        rows = pl.ds(at, ROWS)
        high[rows, :], low[rows, :] = split(
            counts[rows, :] * scale * column[at : at + ROWS]
        )


def gene_cuts(genes):
    return [0, genes]


def turn_kernel(counts, factor, mask, *outs):
    turned = counts[...].T * factor[...].T * mask[...]
    cuts = gene_cuts(turned.shape[1])
    for place, (begin, end) in enumerate(zip(cuts, cuts[1:])):
        outs[2 * place][...], outs[2 * place + 1][...] = split(turned[:, begin:end])


def turn_counts(counts, factor, mask, after):
    genes, here = counts.shape
    cuts = gene_cuts(genes)
    widths = [end - begin for begin, end in zip(cuts, cuts[1:]) for _ in range(2)]
    out = kernel_call(
        turn_kernel,
        (here // TILE,),
        [tile(genes), tile(1), full(1, genes)],
        [pl.BlockSpec((TILE, width), lambda j: (j, 0)) for width in widths],
        [shape(here, width, dtype=BF16) for width in widths],
        5,
        after=after,
    )(counts, factor, mask)
    return [tuple(out[2 * k : 2 * k + 2]) for k in range(len(out) // 2)]


def encode_kernel(order, counts, factor, mask, w_enc_t, *refs):
    *outs, high, low, scaled_high, scaled_low = refs
    step = pl.program_id(0)

    @pl.when(step == 0)
    def _():
        for at in range(0, high.shape[0], ROWS):
            rows = pl.ds(at, ROWS)
            high[rows, :], low[rows, :] = split(w_enc_t[rows, :])

    split_scaled(counts, factor, mask, scaled_high, scaled_low)
    product = dot(
        (high[...], low[...]), (scaled_high[...], scaled_low[...]), 1, 0
    )
    side = order[0] == 0
    for place in range(len(outs) // 3):
        other, own, both = outs[3 * place : 3 * place + 3]
        rows = other.shape[0]

        @pl.when(step == place)
        def _():
            if rows < product.shape[0]:
                both[...] = product[rows:]

        @pl.when((step == place) & side)
        def _():
            other[...] = product[:rows, HALF:]
            own[...] = product[:rows, :HALF]

        @pl.when((step == place) & jnp.logical_not(side))
        def _():
            other[...] = product[:rows, :HALF]
            own[...] = product[:rows, HALF:]


def encode_products(side, order, counts, factor, mask, w_enc_t, rest, after=()):
    genes = counts.shape[0]
    hidden = w_enc_t.shape[0]
    blocks = order.shape[0]
    cells = lambda j, order: (0, order[j + 1])
    sizes = [(hidden - rest, HALF)] * 2 + [(max(rest, 8), TILE)]
    return kernel_call(
        encode_kernel,
        (blocks,),
        [
            pl.BlockSpec((genes, TILE), cells),
            pl.BlockSpec((1, TILE), cells),
            full(1, genes),
            full(hidden, genes),
        ],
        [full(*size) for size in sizes] * blocks,
        [shape(*size) for size in sizes] * blocks,
        4 * blocks,
        order=jnp.concatenate([side[None], order]).astype(jnp.int32),
        scratch=[pltpu.VMEM((hidden, genes), BF16)] * 2
        + [pltpu.VMEM((genes, TILE), BF16)] * 2,
        after=after,
    )(counts, factor, mask, w_enc_t)


def prepare_kernel(w_out_t, w_enc_t, w_lat, w_dec, out_high, out_low, turn_high, turn_low,
                   enc_high, enc_low, lat_high, lat_low, tal_high, tal_low,
                   dec_high, dec_low):
    out_high[...], out_low[...] = split(w_out_t[...])
    turn_high[...], turn_low[...] = split(w_out_t[...].T)
    enc_high[...], enc_low[...] = split(w_enc_t[...].T)
    lat_high[...], lat_low[...] = split(w_lat[...])
    tal_high[...], tal_low[...] = split(w_lat[...].T)
    dec_high[...], dec_low[...] = split(w_dec[...].T)


def prepare(w_out_t, w_enc_t, w_lat, w_dec, after):
    hidden, genes = w_out_t.shape
    latents, latent = w_lat.shape[0], w_dec.shape[0]
    sizes = [
        (hidden, genes),
        (genes, hidden),
        (genes, hidden),
        (latents, hidden),
        (hidden, latents),
        (hidden, latent),
    ]
    out = kernel_call(
        prepare_kernel,
        (),
        pair_of(full(hidden, genes)) + [full(latents, hidden), full(latent, hidden)],
        [full(*size) for size in sizes for _ in range(2)],
        [shape(*size, dtype=BF16) for size in sizes for _ in range(2)],
        6,
        after=after,
    )(w_out_t, w_enc_t, w_lat, w_dec)
    return [tuple(out[2 * k : 2 * k + 2]) for k in range(len(sizes))]


def own_kernel(main, *refs):
    *parts, pre_out, stats = refs
    rows = parts[0].shape[0]
    pre_out[:rows] = sum(part[...] for part in parts[1:main]) + parts[0][...]
    if main < len(parts):
        pre_out[rows:] = sum(part[...] for part in parts[main:])
    stats[...] = moments(pre_out[...])


def own_moments(parts, rest, after=()):
    rows, columns = parts[0].shape
    rows += rest[0].shape[0] if rest else 0
    return kernel_call(
        lambda *refs: own_kernel(len(parts), *refs),
        (),
        [full(*part.shape) for part in (*parts, *rest)],
        [full(rows, columns), full(2, rows)],
        [shape(rows, columns), shape(2, rows)],
        3,
        after=after,
    )(*parts, *rest)


def normalize(pre, vector):
    columns = vector.T
    norm = (pre - columns[:, 0:1]) * lax.rsqrt(columns[:, 1:2] + BN_EPS)
    return norm, norm * columns[:, 2:3] + columns[:, 3:4]


def latent_kernel(pre, vector, lat_high, lat_low, b_lat, noise, z_out):
    _, value = normalize(pre[...], vector[...])
    act, _ = silu_pair(value)
    lat = dot((lat_high[...], lat_low[...]), split(act), 1, 0) + b_lat[...].T
    latent = noise.shape[0]
    z_out[...] = lat[:latent] + jnp.exp(0.5 * lat[latent:]) * noise[...]


def latent_own(pre, vector, lat_pair, b_lat, noise):
    return kernel_call(
        latent_kernel,
        (),
        [full(*a.shape) for a in (pre, vector, *lat_pair, b_lat, noise)],
        full(*noise.shape),
        shape(*noise.shape),
        3,
    )(pre, vector, *lat_pair, b_lat, noise)


def sides(order, mine, other):
    left = order[0] == 0
    return jnp.concatenate(
        [jnp.where(left, mine, other), jnp.where(left, other, mine)], axis=1
    )


def hidden_kernel(order, dec_high, dec_low, mine, other, z_all, pre_out, stats,
                  sums):
    for step in range(mine.shape[0]):
        spot = order[step + 1]
        z = sides(order, mine[spot], other[spot])
        columns = pl.ds(step * TILE, TILE)
        z_all[:, columns] = z
        pre = dot((dec_high[...], dec_low[...]), split(z), 1, 0)
        pre_out[:, columns] = pre
        if step == 0:
            sums[...] = fold(pre)
        else:
            sums[...] += fold(pre)
    hidden, here = pre_out.shape
    mean = jnp.sum(sums[...], axis=1, keepdims=True) * (1.0 / here)
    sums[...] = spread(mean)
    squares = []
    for at in range(0, hidden, ROWS):
        rows = pl.ds(at, ROWS)
        total = jnp.zeros((ROWS, 128), F32)
        for step in range(mine.shape[0]):
            cent = pre_out[rows, pl.ds(step * TILE, TILE)] - wide(sums[rows, :])
            total = total + fold(cent * cent)
        squares.append(total)
    square = jnp.sum(jnp.concatenate(squares, axis=0), axis=1, keepdims=True)
    stats[...] = jnp.concatenate([mean, square], axis=1).T


def decoder_hidden(order, dec_pair, mine, other, after):
    hidden, latent = dec_pair[0].shape
    cells = 2 * mine.shape[0] * HALF
    return kernel_call(
        hidden_kernel,
        (1,),
        pair_of(full(hidden, latent)) + [full(*mine.shape), full(*other.shape)],
        [full(latent, cells), full(hidden, cells), full(2, hidden)],
        [shape(latent, cells), shape(hidden, cells), shape(2, hidden)],
        8,
        order=order,
        scratch=[pltpu.VMEM((hidden, 128), F32)],
        after=after,
    )(*dec_pair, mine, other)


def decoder_kernel(cells, order, pre, vector, z, out_high, out_low, turn_high, turn_low,
                   counts, factor, mask, b_out, w_dec,
                   recon_out, grad_high, grad_low, act_high, act_low, z_other, z_own,
                   weight_out, sums, bias_out,
                   sum_term, sum_gain, sum_grad, mean_w, scale_w, shift_w, mask_w, bias_w,
                   dec_high, dec_low, slope, product, term_high, term_low):
    step = pl.program_id(0)
    hidden, genes = out_high.shape

    @pl.when(step == 0)
    def _():
        columns = vector[...].T
        rstd = lax.rsqrt(columns[:, 1:2] + BN_EPS)
        mean_w[...] = spread(columns[:, 0:1])
        scale_w[...] = spread(rstd * columns[:, 2:3])
        shift_w[...] = spread(columns[:, 3:4])
        mask_w[...] = spread(mask[...].T * (1.0 / cells))
        bias_w[...] = spread(b_out[...].T)
        dec_high[...], dec_low[...] = split(
            w_dec[...] * (vector[2:3, :] * lax.rsqrt(vector[1:2, :] + BN_EPS))
        )
        for ref in (sum_term, sum_gain, sum_grad, weight_out):
            ref[...] = jnp.zeros_like(ref)

    for at in range(0, hidden, ROWS):
        rows = pl.ds(at, ROWS)
        cent = pre[rows, :] - wide(mean_w[rows, :])
        act, slope[rows, :] = silu_pair(
            cent * wide(scale_w[rows, :]) + wide(shift_w[rows, :])
        )
        act_high[rows, :], act_low[rows, :] = split(act)
    product[:genes, :] = dot(
        (turn_high[...], turn_low[...]), (act_high[...], act_low[...]), 1, 0
    )
    scale = factor[...]
    for at in range(0, genes, ROWS):
        rows = pl.ds(at, ROWS)
        out = product[rows, :] + wide(bias_w[rows, :])
        recon = jnp.maximum(out, 0.0) + jnp.log(1.0 + jnp.exp(-jnp.abs(out)))
        recon_out[rows, :] = recon
        grad = (recon - counts[rows, :] * scale) * (wide(mask_w[rows, :]) * sigmoid(out))
        sum_grad[rows, :] += fold(grad)
        grad_high[rows, :], grad_low[rows, :] = split(grad)
    product[:hidden, :] = dot(
        (out_high[...], out_low[...]), (grad_high[...], grad_low[...]), 1, 0
    )
    for at in range(0, hidden, ROWS):
        rows = pl.ds(at, ROWS)
        term = product[rows, :] * slope[rows, :]
        cent = pre[rows, :] - wide(mean_w[rows, :])
        sum_term[rows, :] += fold(term)
        sum_gain[rows, :] += fold(term * cent)
        term_high[rows, :], term_low[rows, :] = split(term)
    terms = term_high[...], term_low[...]
    back = dot((dec_high[...], dec_low[...]), terms, 1, 0)
    left = order[0] == 0
    z_other[...] = jnp.where(left, back[:, HALF:], back[:, :HALF])
    z_own[...] = jnp.where(left, back[:, :HALF], back[:, HALF:])
    weight_out[...] += dot(terms, split(z[...]), 1, 1)

    @pl.when(step == pl.num_programs(0) - 1)
    def _():
        rstd = lax.rsqrt(vector[1:2, :] + BN_EPS)
        both = rows_of(sum_term[...], sum_gain[...])
        sums[...] = jnp.concatenate([both[0:1], both[1:2] * rstd], axis=0)
        bias_out[...] = rows_of(sum_grad[...])


def decoder(cells, order, pre, vector, z, out_pair, turn_pair, counts, factor, mask, b_out,
            w_dec):
    hidden, genes = out_pair[0].shape
    here = counts.shape[1]
    latent = w_dec.shape[0]
    most = max(hidden, genes)
    placed = pl.BlockSpec((latent, HALF), lambda j, order: (0, order[j + 1]))
    return kernel_call(
        lambda *refs: decoder_kernel(cells, *refs),
        (here // TILE,),
        [tile(hidden), full(4, hidden), tile(latent)]
        + pair_of(full(hidden, genes))
        + pair_of(full(genes, hidden))
        + [
            tile(genes),
            tile(1),
            full(1, genes),
            full(1, genes),
            full(latent, hidden),
        ],
        [tile(genes)]
        + pair_of(tile(genes))
        + pair_of(tile(hidden))
        + pair_of(placed)
        + [full(hidden, latent), full(2, hidden), full(1, genes)],
        [shape(genes, here)]
        + [shape(genes, here, dtype=BF16)] * 2
        + [shape(hidden, here, dtype=BF16)] * 2
        + [shape(latent, here // 2)] * 2
        + [shape(hidden, latent), shape(2, hidden), shape(1, genes)],
        42,
        order=order,
        scratch=[pltpu.VMEM((hidden, 128), F32)] * 2
        + [pltpu.VMEM((genes, 128), F32)]
        + [pltpu.VMEM((hidden, 128), F32)] * 3
        + [pltpu.VMEM((genes, 128), F32)] * 2
        + [pltpu.VMEM((latent, hidden), BF16)] * 2
        + [pltpu.VMEM((hidden, TILE), F32), pltpu.VMEM((most, TILE), F32)]
        + [pltpu.VMEM((hidden, TILE), BF16)] * 2,
    )(pre, vector, z, *out_pair, *turn_pair, counts, factor, mask, b_out, w_dec)


def start_halves(order, product, outs, first):
    if len(outs) == 1:
        start_or_add(outs[0], product, first)
        return
    rows = product.shape[0] // 2
    upper = order[0] != 0

    @pl.when(upper)
    def _():
        start_or_add(outs[0], product[rows:], first)
        start_or_add(outs[1], product[:rows], first)

    @pl.when(jnp.logical_not(upper))
    def _():
        start_or_add(outs[0], product[:rows], first)
        start_or_add(outs[1], product[rows:], first)


def weight_kernel(right_dim, order, left_high, left_low, right_high, right_low, *outs):
    product = dot(
        (left_high[...], left_low[...]), (right_high[...], right_low[...]), 1, right_dim
    )
    start_halves(order, product, outs, pl.program_id(0) == 0)


def weight_halves(order, halves, left, right, right_dim, width, after=()):
    hidden, here = left[0].shape
    rows = hidden // halves
    genes = right[0].shape[1 - right_dim]
    if right_dim:
        cells = pl.BlockSpec((genes, width), lambda j, order: (0, j))
    else:
        cells = pl.BlockSpec((width, genes), lambda j, order: (j, 0))
    return kernel_call(
        lambda *refs: weight_kernel(right_dim, *refs),
        (here // width,),
        pair_of(pl.BlockSpec((hidden, width), lambda j, order: (0, j))) + pair_of(cells),
        [full(rows, genes)] * halves,
        [shape(rows, genes)] * halves,
        10,
        order=order,
        after=after,
    )(*left, *right)


def latent_weight_kernel(lat, part, vector, out):
    _, value = normalize(part[...], vector[...])
    act, _ = silu_pair(value)
    product = dot(split(lat[...]), split(act), 1, 1)
    start_or_add(out, product, pl.program_id(0) == 0)


def latent_weight(lat, part, vector, after):
    latents, here = lat.shape
    share = part.shape[0]
    return kernel_call(
        latent_weight_kernel,
        (here // 1024,),
        [
            pl.BlockSpec((latents, 1024), lambda j: (0, j)),
            pl.BlockSpec((share, 1024), lambda j: (0, j)),
            full(4, share),
        ],
        full(latents, share),
        shape(latents, share),
        4,
        after=after,
    )(lat, part, vector)


def again_kernel(pre_enc, vector, lat_high, lat_low, b_lat, z, later,
                 lat_out, slope_out, gram, sum_out, later_out, act_high, act_low):
    later_out[...] = later[...]
    first = pl.program_id(0) == 0
    moved = z[...] - b_lat[:, : z.shape[0]].T
    pair = split(moved)
    start_or_add(gram, dot(pair, pair, 1, 1), first)
    start_or_add(sum_out, rows_of(moved), first)
    columns = vector[...].T
    scale = lax.rsqrt(columns[:, 1:2] + BN_EPS) * columns[:, 2:3]
    for at in range(0, pre_enc.shape[0], ROWS):
        rows = pl.ds(at, ROWS)
        part = slice(at, at + ROWS)
        act, slope_out[rows, :] = silu_pair(
            (pre_enc[rows, :] - columns[part, 0:1]) * scale[part] + columns[part, 3:4]
        )
        act_high[rows, :], act_low[rows, :] = split(act)
    lat_out[...] = (
        dot((lat_high[...], lat_low[...]), (act_high[...], act_low[...]), 1, 0)
        + b_lat[...].T
    )


def encode_again(pre_enc, vector, lat_pair, b_lat, z, later, after=()):
    latent = z.shape[0]
    hidden, here = pre_enc.shape
    latents = lat_pair[0].shape[0]
    return kernel_call(
        again_kernel,
        (here // TILE,),
        [tile(hidden), full(4, hidden)]
        + pair_of(full(latents, hidden))
        + [full(1, latents), tile(latent), full(*later.shape)],
        [
            tile(latents),
            tile(hidden),
            full(latent, latent),
            full(1, latent),
            full(*later.shape),
        ],
        [
            shape(latents, here),
            shape(hidden, here),
            shape(latent, latent),
            shape(1, latent),
            shape(*later.shape),
        ],
        10,
        scratch=[pltpu.VMEM((hidden, TILE), BF16)] * 2,
        after=after,
    )(pre_enc, vector, *lat_pair, b_lat, z, later)


def fix_kernel(cells, w_dec, vector, sums, b_lat, matrix_out, column_out):
    weight = w_dec[...]
    rstd = lax.rsqrt(vector[1:2, :] + BN_EPS)
    scaled = weight * (vector[2:3, :] * rstd * (1.0 / cells))
    gained = scaled * (sums[1:2, :] * rstd)
    matrix_out[...] = dot(split(gained), split(weight), 1, 1)
    bias = b_lat[:, : weight.shape[0]].T
    mean = vector[0:1, :] - jnp.sum(weight * bias, axis=0, keepdims=True)
    column_out[...] = spread(
        jnp.sum(scaled * sums[0:1, :] - gained * mean, axis=1, keepdims=True)
    )


def fix_terms(cells, w_dec, vector, sums, b_lat):
    latent, hidden = w_dec.shape
    return kernel_call(
        lambda *refs: fix_kernel(cells, *refs),
        (),
        [full(latent, hidden), full(4, hidden), full(2, hidden), full(*b_lat.shape)],
        [full(latent, latent), full(latent, 128)],
        [shape(latent, latent), shape(latent, 128)],
        2,
    )(w_dec, vector, sums, b_lat)


def latent_back_kernel(cells, order, mine, other, z, matrix, column, b_lat, lat, noise,
                       tal_high, tal_low, slope, pre, vector, grad_out, sums, lat_out, bias_out,
                       sum_grad, sum_gain, sum_lat, product):
    step = pl.program_id(0)

    @pl.when(step == 0)
    def _():
        for ref in (sum_grad, sum_gain, sum_lat):
            ref[...] = jnp.zeros_like(ref)

    latent = noise.shape[0]
    moved = z[...] - b_lat[:, :latent].T
    fix = dot(split(matrix[...]), split(moved), 1, 0) + wide(column[...])
    grad_z = sides(order, mine[:latent, :], other[:latent, :]) - fix
    mu = lat[:latent, :]
    spread_z = jnp.exp(0.5 * lat[latent:, :])
    grad_mu = grad_z + (ALPHA / cells) * mu
    grad_logvar = 0.5 * grad_z * noise[...] * spread_z + (0.5 * ALPHA / cells) * (
        spread_z * spread_z - 1.0
    )
    grad_lat = jnp.concatenate([grad_mu, grad_logvar], axis=0)
    lat_out[...] = grad_lat
    sum_lat[...] += fold(grad_lat)
    product[...] = dot((tal_high[...], tal_low[...]), split(grad_lat), 1, 0)
    mean = vector[0:1, :].T
    for at in range(0, product.shape[0], ROWS):
        rows = pl.ds(at, ROWS)
        grad = product[rows, :] * slope[rows, :]
        grad_out[rows, :] = grad
        sum_grad[rows, :] += fold(grad)
        sum_gain[rows, :] += fold(grad * (pre[rows, :] - mean[at : at + ROWS]))

    @pl.when(step == pl.num_programs(0) - 1)
    def _():
        both = rows_of(sum_grad[...], sum_gain[...])
        sums[...] = jnp.concatenate(
            [both[0:1], both[1:2] * lax.rsqrt(vector[1:2, :] + BN_EPS)], axis=0
        )
        bias_out[...] = rows_of(sum_lat[...])


def latent_back(cells, order, mine, other, z, fix, b_lat, lat, noise, tal_pair, slope, pre,
                vector, after=()):
    hidden, here = pre.shape
    latents = lat.shape[0]
    latent = noise.shape[0]
    block = pl.BlockSpec(
        (None, mine.shape[1], HALF), lambda j, order: (order[j + 1], 0, 0)
    )
    return kernel_call(
        lambda *refs: latent_back_kernel(cells, *refs),
        (here // TILE,),
        [block, block, tile(latent), full(latent, latent), full(latent, 128)]
        + [full(1, latents), tile(latents), tile(latent)]
        + pair_of(full(hidden, latents))
        + [tile(hidden), tile(hidden), full(4, hidden)],
        [tile(hidden), full(2, hidden), tile(latents), full(1, latents)],
        [
            shape(hidden, here),
            shape(2, hidden),
            shape(latents, here),
            shape(1, latents),
        ],
        12,
        order=order,
        scratch=[
            pltpu.VMEM((hidden, 128), F32),
            pltpu.VMEM((hidden, 128), F32),
            pltpu.VMEM((latents, 128), F32),
            pltpu.VMEM((hidden, TILE), F32),
        ],
        after=after,
    )(mine, other, z, *fix, b_lat, lat, noise, *tal_pair, slope, pre, vector)


def encoder_weight_kernel(cells, order, grad_in, pre, vector, scaled_high, scaled_low,
                          high, low, *outs):
    columns = vector[...].T
    scale = lax.rsqrt(columns[:, 1:2] + BN_EPS)
    outer = columns[:, 2:3] * scale
    shift = columns[:, 4:5] * (1.0 / cells)
    gain = columns[:, 5:6] * (1.0 / cells) * scale
    for at in range(0, grad_in.shape[0], ROWS):
        rows = pl.ds(at, ROWS)
        part = slice(at, at + ROWS)
        grad = outer[part] * (
            grad_in[rows, :]
            - shift[part]
            - (pre[rows, :] - columns[part, 0:1]) * gain[part]
        )
        high[rows, :], low[rows, :] = split(grad)
    product = dot((high[...], low[...]), (scaled_high[...], scaled_low[...]), 1, 0)
    start_halves(order, product, outs, pl.program_id(0) == 0)


def encoder_weight(cells, order, halves, grad_in, pre, vector, scaled, after):
    hidden, here = pre.shape
    genes = scaled[0].shape[1]
    rows = hidden // halves
    return kernel_call(
        lambda *refs: encoder_weight_kernel(cells, *refs),
        (here // TILE,),
        [tile(hidden), tile(hidden), full(6, hidden)]
        + pair_of(pl.BlockSpec((TILE, genes), lambda j, order: (j, 0))),
        pair_of(tile(hidden)) + [full(rows, genes)] * halves,
        [shape(hidden, here, dtype=BF16)] * 2 + [shape(rows, genes)] * halves,
        12,
        order=order,
        after=after,
    )(grad_in, pre, vector, *scaled)


def counts_kernel(cells, enc_high, enc_low, high, low, recon, counts, factor, mask, out,
                  product):
    product[...] = dot((enc_high[...], enc_low[...]), (high[...], low[...]), 1, 0)
    mask_column = mask[...].T
    scale = factor[...]
    for at in range(0, out.shape[0], ROWS):
        rows = pl.ds(at, ROWS)
        column = mask_column[at : at + ROWS]
        diff = (recon[rows, :] - counts[rows, :] * scale) * (column * (1.0 / cells))
        out[rows, :] = (product[rows, :] - diff) * (scale * column)


def counts_back(cells, enc_pair, grads, recon, counts, factor, mask, after=()):
    genes, hidden = enc_pair[0].shape
    here = counts.shape[1]
    return kernel_call(
        lambda *refs: counts_kernel(cells, *refs),
        (here // TILE,),
        pair_of(full(genes, hidden))
        + pair_of(tile(hidden))
        + [tile(genes), tile(genes), tile(1), full(1, genes)],
        tile(genes),
        shape(genes, here),
        16,
        scratch=[pltpu.VMEM((genes, TILE), F32)],
        after=after,
    )(*enc_pair, *grads, recon, counts, factor, mask)


def token_kernel(out):
    out[...] = jnp.zeros_like(out)


def token(after):
    return kernel_call(
        token_kernel, (), [], full(1, 1), shape(1, 1), 0, after=after
    )()[0, 0]


def swap(value, axis, bit):
    size = lax.axis_size(axis)
    return lax.ppermute(value, axis, [(i, i ^ bit) for i in range(size)])


def bits(axis):
    size, bit, out = lax.axis_size(axis), 1, []
    while bit < size:
        out.append(bit)
        bit *= 2
    return out


def add_all(value, axes):
    for axis in axes:
        for bit in bits(axis):
            value = value + swap(value, axis, bit)
    return value


def moments_all(both, count, axes, others=None):
    for axis in axes:
        if axis == GENE and others is not None:
            both = jnp.concatenate([both, others])
        for bit in bits(axis):
            other = swap(both, axis, bit)
            gap = both[0] - other[0]
            rows = [
                0.5 * (both[0] + other[0]),
                both[1] + other[1] + gap * gap * (0.5 * count),
            ]
            both = jnp.concatenate([jnp.stack(rows), both[2:] + other[2:]])
            count = 2 * count
    return both[0], both[1] / count, both[2:]


def rows_wide(vector, share):
    size = vector.shape[0]
    lines = -(-size // share)
    return jnp.pad(vector, (0, lines * share - size)).reshape(lines, share)


def halve_blocks(value, bit):
    half = value.shape[0] // 2
    upper = (lax.axis_index(GENE) & bit) != 0
    sent = jnp.where(upper, value[:half], value[half:])
    kept = jnp.where(upper, value[half:], value[:half])
    return kept + swap(sent, GENE, bit)


def gene_pairs(links):
    return [(2 * a + y, 2 * b + y) for a, b in links for y in (0, 1)]


OUTER = gene_pairs([(0, 1), (3, 2)])
MIDDLE = gene_pairs([(1, 2), (2, 1)])
SIDES = gene_pairs([(0, 1), (1, 0), (2, 3), (3, 2)])


def line_order(z):
    low = z < 2
    return [
        jnp.where(low, z + 3, z + 1) % 4,
        (z + 2) % 4,
        jnp.where(low, z + 1, z + 3) % 4,
        z,
    ]


def by_line(here):
    return lax.axis_size(GENE) == 8 and here == 8 * HALF


def scatter_encoded(counts, factor, mask, w_enc_t, others):
    here = counts.shape[1]
    hidden = w_enc_t.shape[0]
    me = lax.axis_index(GENE)
    if not by_line(here):
        side = 0 * me
        order = jnp.arange(here // TILE, dtype=jnp.int32)
        blocks = encode_products(side, order, counts, factor, mask, w_enc_t, 0)
        pre = [blocks[3 * k + i] for k in range(len(blocks) // 3) for i in (1, 0)]
        pre = lax.psum_scatter(
            jnp.concatenate(pre, axis=1), GENE, scatter_dimension=1, tiled=True
        )
        scaled = turn_counts(counts, factor, mask, (blocks[0],))
        return [pre], [], scaled, prepare(*others, scaled[0])
    z, y = me // 2, me % 2
    rest = hidden // 6 // 16 * 16
    order = jnp.stack(line_order(z)).astype(jnp.int32)

    def products(first, last, after=()):
        return encode_products(
            y, order[first:last], counts, factor, mask, w_enc_t, rest, after
        )

    middle = (z == 1) | (z == 2)
    blocks = products(0, 1)
    step1 = lax.ppermute(blocks[2], GENE, OUTER)
    blocks += products(1, 2, (step1,))
    blocks += products(2, 3, blocks[3:4])
    blocks += products(3, 4, blocks[6:7])
    part = [blocks[3 * k + 1] + swap(blocks[3 * k], GENE, 1) for k in range(4)]
    tail = blocks[2::3]
    step2 = lax.ppermute(tail[1], GENE, OUTER)
    across = lax.ppermute(tail[1] + step1, GENE, MIDDLE)
    scaled = turn_counts(counts, factor, mask, (step2, across, blocks[6]))
    side = lax.ppermute(jnp.where(middle, tail[0] + across, tail[2]), GENE, SIDES)
    inner = lax.ppermute(tail[2] + step2, GENE, MIDDLE)
    weights = prepare(*others, (side, inner, scaled[0][0]))
    tail = tail[3] + side + inner
    left, right = tail[:, :HALF], tail[:, HALF:]
    mine = jnp.where(y == 0, left, right)
    step1 = lax.ppermute(part[0], GENE, OUTER)
    step2 = lax.ppermute(part[1], GENE, OUTER)
    across = lax.ppermute(part[1] + step1, GENE, MIDDLE)
    side = lax.ppermute(jnp.where(middle, part[0] + across, part[2]), GENE, SIDES)
    inner = lax.ppermute(part[2] + step2, GENE, MIDDLE)
    back = swap(jnp.where(y == 0, right, left), GENE, 1)
    return [part[3], side, inner], [mine, back], scaled, weights


def gather_blocks(value, before=None):
    rows, own = value.shape
    if not by_line(own * lax.axis_size(GENE)):
        value = lax.all_gather(value, GENE, axis=1, tiled=True)
        blocks = value.shape[1] // TILE
        stack = jnp.moveaxis(value.reshape(rows, blocks, 2, HALF), 0, 2)
        order = jnp.concatenate([jnp.zeros(1), jnp.arange(blocks)])
        return stack[:, 0], stack[:, 1], order.astype(jnp.int32)
    me = lax.axis_index(GENE)
    mine = jnp.stack([value] + [swap(value, GENE, bit) for bit in (2, 4, 6)])
    if before is not None:
        mine = mine + token(before)
    other = swap(mine, GENE, 1)
    order = jnp.concatenate([(me % 2)[None], (me // 2) ^ jnp.arange(4)])
    return mine, other, order.astype(jnp.int32)


def term_order(here):
    blocks = jnp.arange(here // TILE)
    if not by_line(here):
        return jnp.concatenate([jnp.zeros(1), blocks]).astype(jnp.int32)
    me = lax.axis_index(GENE)
    return jnp.concatenate([(me % 2)[None], ((me // 2 ^ blocks) + 3) % 4]).astype(
        jnp.int32
    )


def scatter_sides(other, own, sums):
    rows, half = own.shape
    if not by_line(2 * half):
        value = jnp.stack(
            [own.reshape(rows, -1, HALF), other.reshape(rows, -1, HALF)], axis=2
        ).reshape(rows, 2 * half)
        return value, add_all(sums, (BATCH, GENE))
    z = lax.axis_index(GENE) // 2
    sums = add_all(sums, (BATCH,))
    sums = sums + swap(sums, GENE, 1)
    quarter = sums.shape[1] // 4
    quarters = [
        jnp.pad(
            lax.dynamic_slice_in_dim(sums, (z ^ k) * quarter, quarter, 1),
            ((0, 0), (0, HALF - quarter)),
        )
        for k in (1, 2, 3, 0)
    ]
    return jnp.concatenate(
        [own + swap(other, GENE, 1), jnp.concatenate(quarters, axis=1)], axis=0
    ), sums


def scatter_terms(part, before):
    if not by_line(2 * part.shape[1]):
        return lax.psum_scatter(part, GENE, scatter_dimension=1, tiled=True)
    total = part[:, 3 * HALF :] + token(before)
    for k in (1, 2, 3):
        total = total + swap(part[:, (k - 1) * HALF : k * HALF], GENE, 2 * k)
    return total


def gather_sums(stack, sums):
    if stack.shape[0] != 4 or not by_line(8 * stack.shape[2]):
        return sums
    z = lax.axis_index(GENE) // 2
    quarter = sums.shape[1] // 4
    quarters = stack[:, -sums.shape[0] :, :quarter]
    return jnp.concatenate(
        [
            lax.dynamic_index_in_dim(quarters, z ^ place, 0, keepdims=False)
            for place in range(4)
        ],
        axis=1,
    )


def add_cores(chunks, zero):
    if len(chunks[0]) == 1:
        return chunks
    return [own + swap(other, BATCH, 1) + zero for other, own in chunks]


def swap_chips(part, zero=0.0):
    if lax.axis_size(BATCH) != 4:
        return part
    return part + swap(part, BATCH, 2) + zero


def join_cores(order, chunks, zero):
    if lax.axis_size(BATCH) != 4:
        return lax.psum(jnp.concatenate([chunk[0] for chunk in chunks], axis=1), BATCH)
    low = order[0] != 0
    other = [swap(part + zero, BATCH, 1) for part in chunks]
    return jnp.concatenate(
        [
            jnp.concatenate([jnp.where(low, a, b), jnp.where(low, b, a)], axis=0)
            for a, b in zip(chunks, other)
        ],
        axis=1,
    )


def on_device(
    counts_in,
    umi_total,
    gene_mask,
    noise,
    w_enc,
    gain_enc,
    shift_enc,
    w_lat,
    b_lat,
    w_dec,
    gain_dec,
    shift_dec,
    w_out,
    b_out,
    mean_enc,
    var_enc,
    mean_dec,
    var_dec,
):
    here = counts_in.shape[1]
    cells = here * lax.axis_size(BATCH)
    hidden = w_enc.shape[1]
    ranks = lax.axis_size(GENE)
    share = hidden // ranks
    own = here // ranks
    latent = noise.shape[0]
    me = lax.axis_index(GENE)
    both = (BATCH, GENE)
    core = lax.axis_index(BATCH) % 2
    halves = 2 if lax.axis_size(BATCH) == 4 else 1
    order = (1 - core).astype(jnp.int32)[None]

    def hidden_part(vector):
        return lax.dynamic_slice_in_dim(vector, me * share, share, vector.ndim - 1)

    def hidden_placed(part):
        empty = jnp.zeros((part.shape[0], hidden), F32)
        return lax.dynamic_update_slice_in_dim(empty, part, me * share, 1)

    factor = (UMI_SCALE / umi_total.astype(F32))[None, :]
    mask = gene_mask.astype(F32)[None, :]
    w_enc_t = w_enc.T
    w_out_t = w_out.T
    b_lat_row = b_lat[None, :]
    noise_own = lax.dynamic_slice_in_dim(noise, me * own, own, 1)

    parts, rest, scaled, weights = scatter_encoded(
        counts_in, factor, mask, w_enc_t, (w_out_t, w_enc_t, w_lat, w_dec)
    )
    out_pair, turn_pair, enc_pair, lat_pair, tal_pair, dec_pair = weights
    affine1 = hidden_placed(jnp.stack([gain_enc, shift_enc]))
    pre_own, stats1 = own_moments(
        parts, rest, after=(affine1, noise_own, out_pair[0])
    )
    mean1, var1, affine1 = moments_all(stats1, own, both, affine1)
    vector1 = jnp.concatenate([mean1[None], var1[None], affine1])
    part_vector = hidden_part(vector1)
    z_own = latent_own(pre_own, vector1, lat_pair, b_lat_row, noise_own)

    z_mine, z_other, z_order = gather_blocks(z_own)
    zero = token((z_mine, z_other))
    pre_enc = lax.all_gather(pre_own + zero, GENE, axis=1, tiled=True)
    z, pre_dec, stats2 = decoder_hidden(
        z_order, dec_pair, z_mine, z_other, (part_vector,)
    )
    mean2, var2, _ = moments_all(stats2, here, (BATCH,))
    vector2 = jnp.stack([mean2, var2, gain_dec, shift_dec])
    recon, grad_high, grad_low, act_high, act_low, *terms, term_w_dec, sums2, grad_b_out = (
        decoder(
            cells, term_order(here), pre_dec, vector2, z, out_pair, turn_pair, counts_in,
            factor, mask, b_out[None, :], w_dec
        )
    )

    part, sums2 = scatter_sides(*terms, sums2)
    grad_w_out = weight_halves(
        order, halves, (act_high, act_low), (grad_high, grad_low), 1, 1024, after=(part,)
    )
    total = scatter_terms(part, (grad_w_out[0],))
    zero = token((total,))
    lat, slope1, gram_z, sum_z, term_w_dec = encode_again(
        pre_enc, vector1, lat_pair, b_lat_row, z, term_w_dec
    )
    grad_w_out = add_cores([[grad_w_out[0] + zero, *grad_w_out[1:]]], token((lat,)))
    term_mine, term_other, z_order = gather_blocks(total, (lat,))
    sums2 = gather_sums(term_mine, sums2)
    fix_z = fix_terms(cells, w_dec, vector2, sums2, b_lat_row)

    received = []
    if halves == 2:
        cuts = [0, 256, 512, counts_in.shape[0]]
        grad_w_out = [grad_w_out[0][:, a:b] for a, b in zip(cuts, cuts[1:])]
        received = [swap(piece, BATCH, 2) for piece in grad_w_out]
    steps = list(reversed(bits(GENE)))
    term_w_dec = halve_blocks(term_w_dec.reshape(ranks, share, latent), steps[0])

    pre_part = lax.dynamic_slice_in_dim(pre_enc, me * share, share, 0)
    grad_in1, sums1, grad_lat, grad_b_lat = latent_back(
        cells, z_order, term_mine, term_other, z, fix_z, b_lat_row, lat, noise, tal_pair,
        slope1, pre_enc, vector1, [*received[:1], term_w_dec, pre_part]
    )
    sums1 = add_all(
        jnp.concatenate([sums1.reshape(-1), grad_b_lat[0], grad_b_out[0]]),
        (BATCH,),
    )
    grad_b_lat = sums1[2 * hidden : 2 * hidden + 2 * latent]
    grad_b_out = sums1[2 * hidden + 2 * latent :]
    sums1 = sums1[: 2 * hidden].reshape(2, hidden)
    vector6 = jnp.concatenate([vector1, sums1])
    term_w_dec = halve_blocks(term_w_dec, steps[1])
    high, low, *weight_part = encoder_weight(
        cells, order, halves, grad_in1, pre_enc, vector6, scaled[0], [term_w_dec, *received[1:]]
    )
    for bit in steps[2:]:
        term_w_dec = halve_blocks(term_w_dec, bit)
    term_w_dec = term_w_dec[0].T
    after = ()
    if halves == 2:
        weight_part = add_cores([weight_part], 0.0)
        after = weight_part
    grad_counts = counts_back(
        cells, enc_pair, (high, low), recon, counts_in, factor, mask, after=after
    )
    zero = token((grad_counts,))
    if halves == 2:
        weight_part = [swap_chips(weight_part[0], zero)]
    else:
        weight_part = [weight_part]
    if halves == 2:
        grad_w_out = [a + b for a, b in zip(grad_w_out, received)]
    grad_w_out = join_cores(order, grad_w_out, zero).T
    grad_w_enc = join_cores(order, weight_part, 0.0).T
    grad_w_lat = latent_weight(
        grad_lat, pre_part, part_vector, (grad_counts,)
    )
    small = jnp.concatenate(
        [
            term_w_dec + zero,
            grad_w_lat,
            rows_wide(gram_z.reshape(-1), share),
            rows_wide(sum_z[0], share),
        ]
    )
    small = add_all(small, (BATCH,)) + (token(weight_part[:1]) if halves == 2 else 0.0)
    term_w_dec = small[:latent]
    grad_w_lat = small[latent : 3 * latent]
    lines = -(-latent // share)
    gram_z = small[3 * latent : -lines].reshape(-1)[: latent * latent]
    gram_z = gram_z.reshape(latent, latent)
    sum_z = small[-lines:].reshape(-1)[:latent]
    grad_shift2 = hidden_part(sums2[0])
    grad_gain2 = hidden_part(sums2[1])
    rstd2 = hidden_part(lax.rsqrt(var2 + BN_EPS))
    cov_z = gram_z - sum_z[:, None] * (sum_z / cells)[None, :]
    pair_w_dec = rstd2[None, :] * jnp.dot(
        cov_z, hidden_part(w_dec), precision=lax.Precision.HIGHEST
    )
    sum_z = sum_z + cells * b_lat[:latent]
    grad_w_dec = (hidden_part(gain_dec) * rstd2)[None, :] * (
        term_w_dec
        - sum_z[:, None] * (grad_shift2 / cells)[None, :]
        - pair_w_dec * (grad_gain2 / cells)[None, :]
    )

    correct = cells / (cells - 1.0)
    new_mean_enc = (1.0 - MOMENTUM) * mean_enc + MOMENTUM * hidden_part(mean1)
    new_var_enc = (1.0 - MOMENTUM) * var_enc + MOMENTUM * hidden_part(var1) * correct
    new_mean_dec = (1.0 - MOMENTUM) * mean_dec + MOMENTUM * mean2
    new_var_dec = (1.0 - MOMENTUM) * var_dec + MOMENTUM * var2 * correct
    return (
        recon,
        grad_counts,
        grad_w_enc,
        hidden_part(sums1[1]),
        hidden_part(sums1[0]),
        grad_w_lat,
        grad_b_lat,
        grad_w_dec,
        grad_gain2,
        grad_shift2,
        grad_w_out,
        grad_b_out,
        new_mean_enc,
        new_var_enc,
        new_mean_dec,
        new_var_dec,
    )


def solution(mesh):
    return jax.shard_map(
        on_device,
        mesh=mesh,
        in_specs=(
            P(GENE, BATCH),
            P(BATCH),
            P(GENE),
            P(None, BATCH),
            P(GENE, None),
            P(GENE),
            P(GENE),
            P(),
            P(),
            P(),
            P(),
            P(),
            P(GENE, None),
            P(GENE),
            P(GENE),
            P(GENE),
            P(),
            P(),
        ),
        out_specs=(
            P(GENE, BATCH),
            P(GENE, BATCH),
            P(GENE, None),
            P(GENE),
            P(GENE),
            P(None, GENE),
            P(),
            P(None, GENE),
            P(GENE),
            P(GENE),
            P(GENE, None),
            P(GENE),
            P(GENE),
            P(GENE),
            P(),
            P(),
        ),
        check_vma=False,
    )
```

```python
import jax
import jax.numpy as jnp
from jax import lax
from jax.experimental import pallas as pl
from jax.experimental.pallas import tpu as pltpu
from jax.sharding import PartitionSpec as P

ALPHA = 0.002
BN_EPS = 1e-05
MOMENTUM = 0.1
UMI_SCALE = 10000.0
BATCH = "batch"
GENE = "gene"
TILE = 512
HALF = 256
ROWS = 16
VMEM_BYTES = 56 << 20
F32 = jnp.float32


BF16 = jnp.bfloat16
RATE = 600_000_000


def split(value):
    high = value.astype(BF16)
    return high, (value - high.astype(F32)).astype(BF16)


def whole(pair):
    return pair[0].astype(F32) + pair[1].astype(F32)


def dot(left, right, left_dim, right_dim):
    def one(a, b):
        return lax.dot_general(
            a,
            b,
            (((left_dim,), (right_dim,)), ((), ())),
            preferred_element_type=F32,
        )

    return one(left[0], right[0]) + (one(left[0], right[1]) + one(left[1], right[0]))


def kernel_call(
    body, grid, in_specs, out_specs, out_shape, micros, order=None, scratch=(), after=(),
    onto=(),
):
    leading = 0 if order is None else 1
    held = leading + len(in_specs)

    def run(*refs):
        body(*refs[:held], *refs[held + len(after) :])

    call = pl.pallas_call(
        run,
        grid_spec=pltpu.PrefetchScalarGridSpec(
            num_scalar_prefetch=leading,
            grid=grid,
            in_specs=list(in_specs) + [pl.BlockSpec(memory_space=pl.ANY)] * len(after),
            out_specs=out_specs,
            scratch_shapes=list(scratch),
        ),
        out_shape=out_shape,
        input_output_aliases={held + k: out for k, out in enumerate(onto)},
        compiler_params=pltpu.CompilerParams(vmem_limit_bytes=VMEM_BYTES),
        cost_estimate=pl.CostEstimate(
            flops=int(micros * RATE), bytes_accessed=1024, transcendentals=0
        ),
    )
    prefetch = () if order is None else (order,)
    return lambda *args: call(*prefetch, *args, *after)


def shape(*dims, dtype=F32):
    return jax.ShapeDtypeStruct(dims, dtype)


def full(*dims):
    return pl.BlockSpec(dims, lambda *_: (0,) * len(dims))


def tile(rows):
    return pl.BlockSpec((rows, TILE), lambda j, *_: (0, j))


def pair_of(spec):
    return [spec, spec]


def sigmoid(value):
    return 0.5 * jnp.tanh(0.5 * value) + 0.5


def silu_pair(value):
    sig = sigmoid(value)
    act = value * sig
    return act, sig + act * (1.0 - sig)


def start_or_add(ref, value, first):
    @pl.when(first)
    def _():
        ref[...] = value

    @pl.when(jnp.logical_not(first))
    def _():
        ref[...] += value


def fold(value):
    width = value.shape[1]
    if width % 128:
        return jnp.broadcast_to(
            jnp.sum(value, axis=1, keepdims=True) / 128.0, (value.shape[0], 128)
        )
    return sum(
        value[:, at : at + 128] for at in range(128, width, 128)
    ) + value[:, :128] if width > 128 else value


def rows_of(*folded):
    return jnp.concatenate(
        [jnp.sum(value, axis=1, keepdims=True) for value in folded], axis=1
    ).T


def moments(pre):
    mean = jnp.mean(pre, axis=1, keepdims=True)
    cent = pre - mean
    return jnp.concatenate(
        [mean, jnp.sum(cent * cent, axis=1, keepdims=True)], axis=1
    ).T


def wide(column):
    return jnp.concatenate([column] * (TILE // 128), axis=1)


def spread(column):
    return jnp.broadcast_to(column, (column.shape[0], 128))


def split_scaled(counts, factor, mask, high, low):
    column = mask[...].T
    scale = factor[...]
    for at in range(0, counts.shape[0], ROWS):
        rows = pl.ds(at, ROWS)
        high[rows, :], low[rows, :] = split(
            counts[rows, :] * scale * column[at : at + ROWS]
        )


def gene_cuts(genes):
    return [0, genes]


def turn_kernel(counts, factor, mask, *outs):
    turned = counts[...].T * factor[...].T * mask[...]
    cuts = gene_cuts(turned.shape[1])
    for place, (begin, end) in enumerate(zip(cuts, cuts[1:])):
        outs[2 * place][...], outs[2 * place + 1][...] = split(turned[:, begin:end])


def turn_counts(counts, factor, mask, after):
    genes, here = counts.shape
    cuts = gene_cuts(genes)
    widths = [end - begin for begin, end in zip(cuts, cuts[1:]) for _ in range(2)]
    out = kernel_call(
        turn_kernel,
        (here // TILE,),
        [tile(genes), tile(1), full(1, genes)],
        [pl.BlockSpec((TILE, width), lambda j: (j, 0)) for width in widths],
        [shape(here, width, dtype=BF16) for width in widths],
        5,
        after=after,
    )(counts, factor, mask)
    return [tuple(out[2 * k : 2 * k + 2]) for k in range(len(out) // 2)]


def encode_kernel(order, counts, factor, mask, w_enc_t, *refs):
    *outs, high, low, scaled_high, scaled_low = refs
    step = pl.program_id(0)

    @pl.when(step == 0)
    def _():
        for at in range(0, high.shape[0], ROWS):
            rows = pl.ds(at, ROWS)
            high[rows, :], low[rows, :] = split(w_enc_t[rows, :])

    split_scaled(counts, factor, mask, scaled_high, scaled_low)
    product = dot(
        (high[...], low[...]), (scaled_high[...], scaled_low[...]), 1, 0
    )
    side = order[0] == 0
    for place in range(len(outs) // 3):
        other, own, both = outs[3 * place : 3 * place + 3]
        rows = other.shape[0]

        @pl.when(step == place)
        def _():
            if rows < product.shape[0]:
                both[...] = product[rows:]

        @pl.when((step == place) & side)
        def _():
            other[...] = product[:rows, HALF:]
            own[...] = product[:rows, :HALF]

        @pl.when((step == place) & jnp.logical_not(side))
        def _():
            other[...] = product[:rows, :HALF]
            own[...] = product[:rows, HALF:]


def encode_products(side, order, counts, factor, mask, w_enc_t, rest, after=()):
    genes = counts.shape[0]
    hidden = w_enc_t.shape[0]
    blocks = order.shape[0]
    cells = lambda j, order: (0, order[j + 1])
    sizes = [(hidden - rest, HALF)] * 2 + [(max(rest, 8), TILE)]
    return kernel_call(
        encode_kernel,
        (blocks,),
        [
            pl.BlockSpec((genes, TILE), cells),
            pl.BlockSpec((1, TILE), cells),
            full(1, genes),
            full(hidden, genes),
        ],
        [full(*size) for size in sizes] * blocks,
        [shape(*size) for size in sizes] * blocks,
        4 * blocks,
        order=jnp.concatenate([side[None], order]).astype(jnp.int32),
        scratch=[pltpu.VMEM((hidden, genes), BF16)] * 2
        + [pltpu.VMEM((genes, TILE), BF16)] * 2,
        after=after,
    )(counts, factor, mask, w_enc_t)


def prepare_kernel(w_out_t, w_enc_t, w_lat, w_dec, out_high, out_low, turn_high, turn_low,
                   enc_high, enc_low, lat_high, lat_low, tal_high, tal_low,
                   dec_high, dec_low):
    out_high[...], out_low[...] = split(w_out_t[...])
    turn_high[...], turn_low[...] = split(w_out_t[...].T)
    enc_high[...], enc_low[...] = split(w_enc_t[...].T)
    lat_high[...], lat_low[...] = split(w_lat[...])
    tal_high[...], tal_low[...] = split(w_lat[...].T)
    dec_high[...], dec_low[...] = split(w_dec[...].T)


def prepare(w_out_t, w_enc_t, w_lat, w_dec, after):
    hidden, genes = w_out_t.shape
    latents, latent = w_lat.shape[0], w_dec.shape[0]
    sizes = [
        (hidden, genes),
        (genes, hidden),
        (genes, hidden),
        (latents, hidden),
        (hidden, latents),
        (hidden, latent),
    ]
    out = kernel_call(
        prepare_kernel,
        (),
        pair_of(full(hidden, genes)) + [full(latents, hidden), full(latent, hidden)],
        [full(*size) for size in sizes for _ in range(2)],
        [shape(*size, dtype=BF16) for size in sizes for _ in range(2)],
        6,
        after=after,
    )(w_out_t, w_enc_t, w_lat, w_dec)
    return [tuple(out[2 * k : 2 * k + 2]) for k in range(len(sizes))]


def own_kernel(main, *refs):
    *parts, pre_out, stats = refs
    rows = parts[0].shape[0]
    pre_out[:rows] = sum(part[...] for part in parts[1:main]) + parts[0][...]
    if main < len(parts):
        pre_out[rows:] = sum(part[...] for part in parts[main:])
    stats[...] = moments(pre_out[...])


def own_moments(parts, rest, after=()):
    rows, columns = parts[0].shape
    rows += rest[0].shape[0] if rest else 0
    return kernel_call(
        lambda *refs: own_kernel(len(parts), *refs),
        (),
        [full(*part.shape) for part in (*parts, *rest)],
        [full(rows, columns), full(2, rows)],
        [shape(rows, columns), shape(2, rows)],
        3,
        after=after,
    )(*parts, *rest)


def normalize(pre, vector):
    columns = vector.T
    norm = (pre - columns[:, 0:1]) * lax.rsqrt(columns[:, 1:2] + BN_EPS)
    return norm, norm * columns[:, 2:3] + columns[:, 3:4]


def latent_kernel(pre, vector, lat_high, lat_low, b_lat, noise, z_out):
    _, value = normalize(pre[...], vector[...])
    act, _ = silu_pair(value)
    lat = dot((lat_high[...], lat_low[...]), split(act), 1, 0) + b_lat[...].T
    latent = noise.shape[0]
    z_out[...] = lat[:latent] + jnp.exp(0.5 * lat[latent:]) * noise[...]


def latent_own(pre, vector, lat_pair, b_lat, noise):
    return kernel_call(
        latent_kernel,
        (),
        [full(*a.shape) for a in (pre, vector, *lat_pair, b_lat, noise)],
        full(*noise.shape),
        shape(*noise.shape),
        3,
    )(pre, vector, *lat_pair, b_lat, noise)


def sides(order, mine, other):
    left = order[0] == 0
    return jnp.concatenate(
        [jnp.where(left, mine, other), jnp.where(left, other, mine)], axis=1
    )


def hidden_kernel(order, dec_high, dec_low, mine, other, z_all, pre_out, stats,
                  sums):
    for step in range(mine.shape[0]):
        spot = order[step + 1]
        z = sides(order, mine[spot], other[spot])
        columns = pl.ds(step * TILE, TILE)
        z_all[:, columns] = z
        pre = dot((dec_high[...], dec_low[...]), split(z), 1, 0)
        pre_out[:, columns] = pre
        if step == 0:
            sums[...] = fold(pre)
        else:
            sums[...] += fold(pre)
    hidden, here = pre_out.shape
    mean = jnp.sum(sums[...], axis=1, keepdims=True) * (1.0 / here)
    sums[...] = spread(mean)
    squares = []
    for at in range(0, hidden, ROWS):
        rows = pl.ds(at, ROWS)
        total = jnp.zeros((ROWS, 128), F32)
        for step in range(mine.shape[0]):
            cent = pre_out[rows, pl.ds(step * TILE, TILE)] - wide(sums[rows, :])
            total = total + fold(cent * cent)
        squares.append(total)
    square = jnp.sum(jnp.concatenate(squares, axis=0), axis=1, keepdims=True)
    stats[...] = jnp.concatenate([mean, square], axis=1).T


def decoder_hidden(order, dec_pair, mine, other, after):
    hidden, latent = dec_pair[0].shape
    cells = 2 * mine.shape[0] * HALF
    return kernel_call(
        hidden_kernel,
        (1,),
        pair_of(full(hidden, latent)) + [full(*mine.shape), full(*other.shape)],
        [full(latent, cells), full(hidden, cells), full(2, hidden)],
        [shape(latent, cells), shape(hidden, cells), shape(2, hidden)],
        8,
        order=order,
        scratch=[pltpu.VMEM((hidden, 128), F32)],
        after=after,
    )(*dec_pair, mine, other)


def decoder_kernel(cells, order, pre, vector, z, out_high, out_low, turn_high, turn_low,
                   counts, factor, mask, b_out, w_dec,
                   recon_out, grad_high, grad_low, act_high, act_low, z_other, z_own,
                   weight_out, sums, bias_out,
                   sum_term, sum_gain, sum_grad, mean_w, scale_w, shift_w, mask_w, bias_w,
                   dec_high, dec_low, slope, product, term_high, term_low):
    step = pl.program_id(0)
    hidden, genes = out_high.shape

    @pl.when(step == 0)
    def _():
        columns = vector[...].T
        rstd = lax.rsqrt(columns[:, 1:2] + BN_EPS)
        mean_w[...] = spread(columns[:, 0:1])
        scale_w[...] = spread(rstd * columns[:, 2:3])
        shift_w[...] = spread(columns[:, 3:4])
        mask_w[...] = spread(mask[...].T * (1.0 / cells))
        bias_w[...] = spread(b_out[...].T)
        dec_high[...], dec_low[...] = split(
            w_dec[...] * (vector[2:3, :] * lax.rsqrt(vector[1:2, :] + BN_EPS))
        )
        for ref in (sum_term, sum_gain, sum_grad, weight_out):
            ref[...] = jnp.zeros_like(ref)

    for at in range(0, hidden, ROWS):
        rows = pl.ds(at, ROWS)
        cent = pre[rows, :] - wide(mean_w[rows, :])
        act, slope[rows, :] = silu_pair(
            cent * wide(scale_w[rows, :]) + wide(shift_w[rows, :])
        )
        act_high[rows, :], act_low[rows, :] = split(act)
    product[:genes, :] = dot(
        (turn_high[...], turn_low[...]), (act_high[...], act_low[...]), 1, 0
    )
    scale = factor[...]
    for at in range(0, genes, ROWS):
        rows = pl.ds(at, ROWS)
        out = product[rows, :] + wide(bias_w[rows, :])
        recon = jnp.maximum(out, 0.0) + jnp.log(1.0 + jnp.exp(-jnp.abs(out)))
        recon_out[rows, :] = recon
        grad = (recon - counts[rows, :] * scale) * (wide(mask_w[rows, :]) * sigmoid(out))
        sum_grad[rows, :] += fold(grad)
        grad_high[rows, :], grad_low[rows, :] = split(grad)
    product[:hidden, :] = dot(
        (out_high[...], out_low[...]), (grad_high[...], grad_low[...]), 1, 0
    )
    for at in range(0, hidden, ROWS):
        rows = pl.ds(at, ROWS)
        term = product[rows, :] * slope[rows, :]
        cent = pre[rows, :] - wide(mean_w[rows, :])
        sum_term[rows, :] += fold(term)
        sum_gain[rows, :] += fold(term * cent)
        term_high[rows, :], term_low[rows, :] = split(term)
    terms = term_high[...], term_low[...]
    back = dot((dec_high[...], dec_low[...]), terms, 1, 0)
    left = order[0] == 0
    z_other[...] = jnp.where(left, back[:, HALF:], back[:, :HALF])
    z_own[...] = jnp.where(left, back[:, :HALF], back[:, HALF:])
    weight_out[...] += dot(terms, split(z[...]), 1, 1)

    @pl.when(step == pl.num_programs(0) - 1)
    def _():
        rstd = lax.rsqrt(vector[1:2, :] + BN_EPS)
        both = rows_of(sum_term[...], sum_gain[...])
        sums[...] = jnp.concatenate([both[0:1], both[1:2] * rstd], axis=0)
        bias_out[...] = rows_of(sum_grad[...])


def decoder(cells, order, pre, vector, z, out_pair, turn_pair, counts, factor, mask, b_out,
            w_dec):
    hidden, genes = out_pair[0].shape
    here = counts.shape[1]
    latent = w_dec.shape[0]
    most = max(hidden, genes)
    placed = pl.BlockSpec((latent, HALF), lambda j, order: (0, order[j + 1]))
    return kernel_call(
        lambda *refs: decoder_kernel(cells, *refs),
        (here // TILE,),
        [tile(hidden), full(4, hidden), tile(latent)]
        + pair_of(full(hidden, genes))
        + pair_of(full(genes, hidden))
        + [
            tile(genes),
            tile(1),
            full(1, genes),
            full(1, genes),
            full(latent, hidden),
        ],
        [tile(genes)]
        + pair_of(tile(genes))
        + pair_of(tile(hidden))
        + pair_of(placed)
        + [full(hidden, latent), full(2, hidden), full(1, genes)],
        [shape(genes, here)]
        + [shape(genes, here, dtype=BF16)] * 2
        + [shape(hidden, here, dtype=BF16)] * 2
        + [shape(latent, here // 2)] * 2
        + [shape(hidden, latent), shape(2, hidden), shape(1, genes)],
        42,
        order=order,
        scratch=[pltpu.VMEM((hidden, 128), F32)] * 2
        + [pltpu.VMEM((genes, 128), F32)]
        + [pltpu.VMEM((hidden, 128), F32)] * 3
        + [pltpu.VMEM((genes, 128), F32)] * 2
        + [pltpu.VMEM((latent, hidden), BF16)] * 2
        + [pltpu.VMEM((hidden, TILE), F32), pltpu.VMEM((most, TILE), F32)]
        + [pltpu.VMEM((hidden, TILE), BF16)] * 2,
    )(pre, vector, z, *out_pair, *turn_pair, counts, factor, mask, b_out, w_dec)


def start_halves(order, product, outs, first):
    if len(outs) == 1:
        start_or_add(outs[0], product, first)
        return
    rows = product.shape[0] // 2
    upper = order[0] != 0

    @pl.when(upper)
    def _():
        start_or_add(outs[0], product[rows:], first)
        start_or_add(outs[1], product[:rows], first)

    @pl.when(jnp.logical_not(upper))
    def _():
        start_or_add(outs[0], product[:rows], first)
        start_or_add(outs[1], product[rows:], first)


def weight_kernel(right_dim, order, left_high, left_low, right_high, right_low, *outs):
    product = dot(
        (left_high[...], left_low[...]), (right_high[...], right_low[...]), 1, right_dim
    )
    start_halves(order, product, outs, pl.program_id(0) == 0)


def weight_halves(order, halves, left, right, right_dim, width, after=()):
    hidden, here = left[0].shape
    rows = hidden // halves
    genes = right[0].shape[1 - right_dim]
    if right_dim:
        cells = pl.BlockSpec((genes, width), lambda j, order: (0, j))
    else:
        cells = pl.BlockSpec((width, genes), lambda j, order: (j, 0))
    return kernel_call(
        lambda *refs: weight_kernel(right_dim, *refs),
        (here // width,),
        pair_of(pl.BlockSpec((hidden, width), lambda j, order: (0, j))) + pair_of(cells),
        [full(rows, genes)] * halves,
        [shape(rows, genes)] * halves,
        10,
        order=order,
        after=after,
    )(*left, *right)


def latent_weight_kernel(lat, part, vector, out):
    _, value = normalize(part[...], vector[...])
    act, _ = silu_pair(value)
    product = dot(split(lat[...]), split(act), 1, 1)
    start_or_add(out, product, pl.program_id(0) == 0)


def latent_weight(lat, part, vector, after):
    latents, here = lat.shape
    share = part.shape[0]
    return kernel_call(
        latent_weight_kernel,
        (here // 1024,),
        [
            pl.BlockSpec((latents, 1024), lambda j: (0, j)),
            pl.BlockSpec((share, 1024), lambda j: (0, j)),
            full(4, share),
        ],
        full(latents, share),
        shape(latents, share),
        4,
        after=after,
    )(lat, part, vector)


def again_kernel(pre_enc, vector, lat_high, lat_low, b_lat, z, later,
                 lat_out, slope_out, gram, sum_out, later_out, act_high, act_low):
    later_out[...] = later[...]
    first = pl.program_id(0) == 0
    moved = z[...] - b_lat[:, : z.shape[0]].T
    pair = split(moved)
    start_or_add(gram, dot(pair, pair, 1, 1), first)
    start_or_add(sum_out, rows_of(moved), first)
    columns = vector[...].T
    scale = lax.rsqrt(columns[:, 1:2] + BN_EPS) * columns[:, 2:3]
    for at in range(0, pre_enc.shape[0], ROWS):
        rows = pl.ds(at, ROWS)
        part = slice(at, at + ROWS)
        act, slope_out[rows, :] = silu_pair(
            (pre_enc[rows, :] - columns[part, 0:1]) * scale[part] + columns[part, 3:4]
        )
        act_high[rows, :], act_low[rows, :] = split(act)
    lat_out[...] = (
        dot((lat_high[...], lat_low[...]), (act_high[...], act_low[...]), 1, 0)
        + b_lat[...].T
    )


def encode_again(pre_enc, vector, lat_pair, b_lat, z, later, after=()):
    latent = z.shape[0]
    hidden, here = pre_enc.shape
    latents = lat_pair[0].shape[0]
    return kernel_call(
        again_kernel,
        (here // TILE,),
        [tile(hidden), full(4, hidden)]
        + pair_of(full(latents, hidden))
        + [full(1, latents), tile(latent), full(*later.shape)],
        [
            tile(latents),
            tile(hidden),
            full(latent, latent),
            full(1, latent),
            full(*later.shape),
        ],
        [
            shape(latents, here),
            shape(hidden, here),
            shape(latent, latent),
            shape(1, latent),
            shape(*later.shape),
        ],
        10,
        scratch=[pltpu.VMEM((hidden, TILE), BF16)] * 2,
        after=after,
    )(pre_enc, vector, *lat_pair, b_lat, z, later)


def fix_kernel(cells, w_dec, vector, sums, b_lat, matrix_out, column_out):
    weight = w_dec[...]
    rstd = lax.rsqrt(vector[1:2, :] + BN_EPS)
    scaled = weight * (vector[2:3, :] * rstd * (1.0 / cells))
    gained = scaled * (sums[1:2, :] * rstd)
    matrix_out[...] = dot(split(gained), split(weight), 1, 1)
    bias = b_lat[:, : weight.shape[0]].T
    mean = vector[0:1, :] - jnp.sum(weight * bias, axis=0, keepdims=True)
    column_out[...] = spread(
        jnp.sum(scaled * sums[0:1, :] - gained * mean, axis=1, keepdims=True)
    )


def fix_terms(cells, w_dec, vector, sums, b_lat):
    latent, hidden = w_dec.shape
    return kernel_call(
        lambda *refs: fix_kernel(cells, *refs),
        (),
        [full(latent, hidden), full(4, hidden), full(2, hidden), full(*b_lat.shape)],
        [full(latent, latent), full(latent, 128)],
        [shape(latent, latent), shape(latent, 128)],
        2,
    )(w_dec, vector, sums, b_lat)


def latent_back_kernel(cells, order, mine, other, z, matrix, column, b_lat, lat, noise,
                       tal_high, tal_low, slope, pre, vector, grad_out, sums, lat_out, bias_out,
                       sum_grad, sum_gain, sum_lat, product):
    step = pl.program_id(0)

    @pl.when(step == 0)
    def _():
        for ref in (sum_grad, sum_gain, sum_lat):
            ref[...] = jnp.zeros_like(ref)

    latent = noise.shape[0]
    moved = z[...] - b_lat[:, :latent].T
    fix = dot(split(matrix[...]), split(moved), 1, 0) + wide(column[...])
    grad_z = sides(order, mine[:latent, :], other[:latent, :]) - fix
    mu = lat[:latent, :]
    spread_z = jnp.exp(0.5 * lat[latent:, :])
    grad_mu = grad_z + (ALPHA / cells) * mu
    grad_logvar = 0.5 * grad_z * noise[...] * spread_z + (0.5 * ALPHA / cells) * (
        spread_z * spread_z - 1.0
    )
    grad_lat = jnp.concatenate([grad_mu, grad_logvar], axis=0)
    lat_out[...] = grad_lat
    sum_lat[...] += fold(grad_lat)
    product[...] = dot((tal_high[...], tal_low[...]), split(grad_lat), 1, 0)
    mean = vector[0:1, :].T
    for at in range(0, product.shape[0], ROWS):
        rows = pl.ds(at, ROWS)
        grad = product[rows, :] * slope[rows, :]
        grad_out[rows, :] = grad
        sum_grad[rows, :] += fold(grad)
        sum_gain[rows, :] += fold(grad * (pre[rows, :] - mean[at : at + ROWS]))

    @pl.when(step == pl.num_programs(0) - 1)
    def _():
        both = rows_of(sum_grad[...], sum_gain[...])
        sums[...] = jnp.concatenate(
            [both[0:1], both[1:2] * lax.rsqrt(vector[1:2, :] + BN_EPS)], axis=0
        )
        bias_out[...] = rows_of(sum_lat[...])


def latent_back(cells, order, mine, other, z, fix, b_lat, lat, noise, tal_pair, slope, pre,
                vector, after=()):
    hidden, here = pre.shape
    latents = lat.shape[0]
    latent = noise.shape[0]
    block = pl.BlockSpec(
        (None, mine.shape[1], HALF), lambda j, order: (order[j + 1], 0, 0)
    )
    return kernel_call(
        lambda *refs: latent_back_kernel(cells, *refs),
        (here // TILE,),
        [block, block, tile(latent), full(latent, latent), full(latent, 128)]
        + [full(1, latents), tile(latents), tile(latent)]
        + pair_of(full(hidden, latents))
        + [tile(hidden), tile(hidden), full(4, hidden)],
        [tile(hidden), full(2, hidden), tile(latents), full(1, latents)],
        [
            shape(hidden, here),
            shape(2, hidden),
            shape(latents, here),
            shape(1, latents),
        ],
        12,
        order=order,
        scratch=[
            pltpu.VMEM((hidden, 128), F32),
            pltpu.VMEM((hidden, 128), F32),
            pltpu.VMEM((latents, 128), F32),
            pltpu.VMEM((hidden, TILE), F32),
        ],
        after=after,
    )(mine, other, z, *fix, b_lat, lat, noise, *tal_pair, slope, pre, vector)


def encoder_weight_kernel(cells, order, grad_in, pre, vector, scaled_high, scaled_low,
                          high, low, *outs):
    columns = vector[...].T
    scale = lax.rsqrt(columns[:, 1:2] + BN_EPS)
    outer = columns[:, 2:3] * scale
    shift = columns[:, 4:5] * (1.0 / cells)
    gain = columns[:, 5:6] * (1.0 / cells) * scale
    for at in range(0, grad_in.shape[0], ROWS):
        rows = pl.ds(at, ROWS)
        part = slice(at, at + ROWS)
        grad = outer[part] * (
            grad_in[rows, :]
            - shift[part]
            - (pre[rows, :] - columns[part, 0:1]) * gain[part]
        )
        high[rows, :], low[rows, :] = split(grad)
    product = dot((high[...], low[...]), (scaled_high[...], scaled_low[...]), 1, 0)
    start_halves(order, product, outs, pl.program_id(0) == 0)


def encoder_weight(cells, order, halves, grad_in, pre, vector, scaled, after):
    hidden, here = pre.shape
    genes = scaled[0].shape[1]
    rows = hidden // halves
    return kernel_call(
        lambda *refs: encoder_weight_kernel(cells, *refs),
        (here // TILE,),
        [tile(hidden), tile(hidden), full(6, hidden)]
        + pair_of(pl.BlockSpec((TILE, genes), lambda j, order: (j, 0))),
        pair_of(tile(hidden)) + [full(rows, genes)] * halves,
        [shape(hidden, here, dtype=BF16)] * 2 + [shape(rows, genes)] * halves,
        12,
        order=order,
        after=after,
    )(grad_in, pre, vector, *scaled)


def counts_kernel(cells, enc_high, enc_low, high, low, recon, counts, factor, mask, out,
                  product):
    product[...] = dot((enc_high[...], enc_low[...]), (high[...], low[...]), 1, 0)
    mask_column = mask[...].T
    scale = factor[...]
    for at in range(0, out.shape[0], ROWS):
        rows = pl.ds(at, ROWS)
        column = mask_column[at : at + ROWS]
        diff = (recon[rows, :] - counts[rows, :] * scale) * (column * (1.0 / cells))
        out[rows, :] = (product[rows, :] - diff) * (scale * column)


def counts_back(cells, enc_pair, grads, recon, counts, factor, mask, after=()):
    genes, hidden = enc_pair[0].shape
    here = counts.shape[1]
    return kernel_call(
        lambda *refs: counts_kernel(cells, *refs),
        (here // TILE,),
        pair_of(full(genes, hidden))
        + pair_of(tile(hidden))
        + [tile(genes), tile(genes), tile(1), full(1, genes)],
        tile(genes),
        shape(genes, here),
        16,
        scratch=[pltpu.VMEM((genes, TILE), F32)],
        after=after,
    )(*enc_pair, *grads, recon, counts, factor, mask)


def token_kernel(out):
    out[...] = jnp.zeros_like(out)


def token(after):
    return kernel_call(
        token_kernel, (), [], full(1, 1), shape(1, 1), 0, after=after
    )()[0, 0]


def swap(value, axis, bit):
    size = lax.axis_size(axis)
    return lax.ppermute(value, axis, [(i, i ^ bit) for i in range(size)])


def bits(axis):
    size, bit, out = lax.axis_size(axis), 1, []
    while bit < size:
        out.append(bit)
        bit *= 2
    return out


def add_all(value, axes):
    for axis in axes:
        for bit in bits(axis):
            value = value + swap(value, axis, bit)
    return value


def moments_all(both, count, axes, others=None):
    for axis in axes:
        if axis == GENE and others is not None:
            both = jnp.concatenate([both, others])
        for bit in bits(axis):
            other = swap(both, axis, bit)
            gap = both[0] - other[0]
            rows = [
                0.5 * (both[0] + other[0]),
                both[1] + other[1] + gap * gap * (0.5 * count),
            ]
            both = jnp.concatenate([jnp.stack(rows), both[2:] + other[2:]])
            count = 2 * count
    return both[0], both[1] / count, both[2:]


def rows_wide(vector, share):
    size = vector.shape[0]
    lines = -(-size // share)
    return jnp.pad(vector, (0, lines * share - size)).reshape(lines, share)


def halve_blocks(value, bit):
    half = value.shape[0] // 2
    upper = (lax.axis_index(GENE) & bit) != 0
    sent = jnp.where(upper, value[:half], value[half:])
    kept = jnp.where(upper, value[half:], value[:half])
    return kept + swap(sent, GENE, bit)


def gene_pairs(links):
    return [(2 * a + y, 2 * b + y) for a, b in links for y in (0, 1)]


OUTER = gene_pairs([(0, 1), (3, 2)])
MIDDLE = gene_pairs([(1, 2), (2, 1)])
SIDES = gene_pairs([(0, 1), (1, 0), (2, 3), (3, 2)])


def line_order(z):
    low = z < 2
    return [
        jnp.where(low, z + 3, z + 1) % 4,
        (z + 2) % 4,
        jnp.where(low, z + 1, z + 3) % 4,
        z,
    ]


def by_line(here):
    return lax.axis_size(GENE) == 8 and here == 8 * HALF


def scatter_encoded(counts, factor, mask, w_enc_t, others):
    here = counts.shape[1]
    hidden = w_enc_t.shape[0]
    me = lax.axis_index(GENE)
    if not by_line(here):
        side = 0 * me
        order = jnp.arange(here // TILE, dtype=jnp.int32)
        blocks = encode_products(side, order, counts, factor, mask, w_enc_t, 0)
        pre = [blocks[3 * k + i] for k in range(len(blocks) // 3) for i in (1, 0)]
        pre = lax.psum_scatter(
            jnp.concatenate(pre, axis=1), GENE, scatter_dimension=1, tiled=True
        )
        scaled = turn_counts(counts, factor, mask, (blocks[0],))
        return [pre], [], scaled, prepare(*others, scaled[0])
    z, y = me // 2, me % 2
    rest = hidden // 6 // 16 * 16
    order = jnp.stack(line_order(z)).astype(jnp.int32)

    def products(first, last, after=()):
        return encode_products(
            y, order[first:last], counts, factor, mask, w_enc_t, rest, after
        )

    middle = (z == 1) | (z == 2)
    blocks = products(0, 1)
    step1 = lax.ppermute(blocks[2], GENE, OUTER)
    blocks += products(1, 2, (step1,))
    blocks += products(2, 3, blocks[3:4])
    blocks += products(3, 4, blocks[6:7])
    part = [blocks[3 * k + 1] + swap(blocks[3 * k], GENE, 1) for k in range(4)]
    tail = blocks[2::3]
    step2 = lax.ppermute(tail[1], GENE, OUTER)
    across = lax.ppermute(tail[1] + step1, GENE, MIDDLE)
    scaled = turn_counts(counts, factor, mask, (step2, across, blocks[6]))
    side = lax.ppermute(jnp.where(middle, tail[0] + across, tail[2]), GENE, SIDES)
    inner = lax.ppermute(tail[2] + step2, GENE, MIDDLE)
    weights = prepare(*others, (side, inner, scaled[0][0]))
    tail = tail[3] + side + inner
    left, right = tail[:, :HALF], tail[:, HALF:]
    mine = jnp.where(y == 0, left, right)
    step1 = lax.ppermute(part[0], GENE, OUTER)
    step2 = lax.ppermute(part[1], GENE, OUTER)
    across = lax.ppermute(part[1] + step1, GENE, MIDDLE)
    side = lax.ppermute(jnp.where(middle, part[0] + across, part[2]), GENE, SIDES)
    inner = lax.ppermute(part[2] + step2, GENE, MIDDLE)
    back = swap(jnp.where(y == 0, right, left), GENE, 1)
    return [part[3], side, inner], [mine, back], scaled, weights


def gather_blocks(value, before=None):
    rows, own = value.shape
    if not by_line(own * lax.axis_size(GENE)):
        value = lax.all_gather(value, GENE, axis=1, tiled=True)
        blocks = value.shape[1] // TILE
        stack = jnp.moveaxis(value.reshape(rows, blocks, 2, HALF), 0, 2)
        order = jnp.concatenate([jnp.zeros(1), jnp.arange(blocks)])
        return stack[:, 0], stack[:, 1], order.astype(jnp.int32)
    me = lax.axis_index(GENE)
    mine = jnp.stack([value] + [swap(value, GENE, bit) for bit in (2, 4, 6)])
    if before is not None:
        mine = mine + token(before)
    other = swap(mine, GENE, 1)
    order = jnp.concatenate([(me % 2)[None], (me // 2) ^ jnp.arange(4)])
    return mine, other, order.astype(jnp.int32)


def term_order(here):
    blocks = jnp.arange(here // TILE)
    if not by_line(here):
        return jnp.concatenate([jnp.zeros(1), blocks]).astype(jnp.int32)
    me = lax.axis_index(GENE)
    return jnp.concatenate([(me % 2)[None], ((me // 2 ^ blocks) + 3) % 4]).astype(
        jnp.int32
    )


def scatter_sides(other, own, sums):
    rows, half = own.shape
    if not by_line(2 * half):
        value = jnp.stack(
            [own.reshape(rows, -1, HALF), other.reshape(rows, -1, HALF)], axis=2
        ).reshape(rows, 2 * half)
        return value, add_all(sums, (BATCH, GENE))
    z = lax.axis_index(GENE) // 2
    sums = add_all(sums, (BATCH,))
    sums = sums + swap(sums, GENE, 1)
    quarter = sums.shape[1] // 4
    quarters = [
        jnp.pad(
            lax.dynamic_slice_in_dim(sums, (z ^ k) * quarter, quarter, 1),
            ((0, 0), (0, HALF - quarter)),
        )
        for k in (1, 2, 3, 0)
    ]
    return jnp.concatenate(
        [own + swap(other, GENE, 1), jnp.concatenate(quarters, axis=1)], axis=0
    ), sums


def scatter_terms(part, before):
    if not by_line(2 * part.shape[1]):
        return lax.psum_scatter(part, GENE, scatter_dimension=1, tiled=True)
    total = part[:, 3 * HALF :] + token(before)
    for k in (1, 2, 3):
        total = total + swap(part[:, (k - 1) * HALF : k * HALF], GENE, 2 * k)
    return total


def gather_sums(stack, sums):
    if stack.shape[0] != 4 or not by_line(8 * stack.shape[2]):
        return sums
    z = lax.axis_index(GENE) // 2
    quarter = sums.shape[1] // 4
    quarters = stack[:, -sums.shape[0] :, :quarter]
    return jnp.concatenate(
        [
            lax.dynamic_index_in_dim(quarters, z ^ place, 0, keepdims=False)
            for place in range(4)
        ],
        axis=1,
    )


def add_cores(chunks, zero):
    if len(chunks[0]) == 1:
        return chunks
    return [own + swap(other, BATCH, 1) + zero for other, own in chunks]


def swap_chips(part, zero=0.0):
    if lax.axis_size(BATCH) != 4:
        return part
    return part + swap(part, BATCH, 2) + zero


def join_cores(order, chunks, zero):
    if lax.axis_size(BATCH) != 4:
        return lax.psum(jnp.concatenate([chunk[0] for chunk in chunks], axis=1), BATCH)
    low = order[0] != 0
    other = [swap(part + zero, BATCH, 1) for part in chunks]
    return jnp.concatenate(
        [
            jnp.concatenate([jnp.where(low, a, b), jnp.where(low, b, a)], axis=0)
            for a, b in zip(chunks, other)
        ],
        axis=1,
    )


def on_device(
    counts_in,
    umi_total,
    gene_mask,
    noise,
    w_enc,
    gain_enc,
    shift_enc,
    w_lat,
    b_lat,
    w_dec,
    gain_dec,
    shift_dec,
    w_out,
    b_out,
    mean_enc,
    var_enc,
    mean_dec,
    var_dec,
):
    here = counts_in.shape[1]
    cells = here * lax.axis_size(BATCH)
    hidden = w_enc.shape[1]
    ranks = lax.axis_size(GENE)
    share = hidden // ranks
    own = here // ranks
    latent = noise.shape[0]
    me = lax.axis_index(GENE)
    both = (BATCH, GENE)
    core = lax.axis_index(BATCH) % 2
    halves = 2 if lax.axis_size(BATCH) == 4 else 1
    order = (1 - core).astype(jnp.int32)[None]

    def hidden_part(vector):
        return lax.dynamic_slice_in_dim(vector, me * share, share, vector.ndim - 1)

    def hidden_placed(part):
        empty = jnp.zeros((part.shape[0], hidden), F32)
        return lax.dynamic_update_slice_in_dim(empty, part, me * share, 1)

    factor = (UMI_SCALE / umi_total.astype(F32))[None, :]
    mask = gene_mask.astype(F32)[None, :]
    w_enc_t = w_enc.T
    w_out_t = w_out.T
    b_lat_row = b_lat[None, :]
    noise_own = lax.dynamic_slice_in_dim(noise, me * own, own, 1)

    parts, rest, scaled, weights = scatter_encoded(
        counts_in, factor, mask, w_enc_t, (w_out_t, w_enc_t, w_lat, w_dec)
    )
    out_pair, turn_pair, enc_pair, lat_pair, tal_pair, dec_pair = weights
    affine1 = hidden_placed(jnp.stack([gain_enc, shift_enc]))
    pre_own, stats1 = own_moments(
        parts, rest, after=(affine1, noise_own, out_pair[0])
    )
    mean1, var1, affine1 = moments_all(stats1, own, both, affine1)
    vector1 = jnp.concatenate([mean1[None], var1[None], affine1])
    part_vector = hidden_part(vector1)
    z_own = latent_own(pre_own, vector1, lat_pair, b_lat_row, noise_own)

    z_mine, z_other, z_order = gather_blocks(z_own)
    zero = token((z_own,))
    pre_enc = lax.all_gather(pre_own + zero, GENE, axis=1, tiled=True)
    z, pre_dec, stats2 = decoder_hidden(
        z_order, dec_pair, z_mine, z_other, (part_vector,)
    )
    mean2, var2, _ = moments_all(stats2, here, (BATCH,))
    vector2 = jnp.stack([mean2, var2, gain_dec, shift_dec])
    recon, grad_high, grad_low, act_high, act_low, *terms, term_w_dec, sums2, grad_b_out = (
        decoder(
            cells, term_order(here), pre_dec, vector2, z, out_pair, turn_pair, counts_in,
            factor, mask, b_out[None, :], w_dec
        )
    )

    part, sums2 = scatter_sides(*terms, sums2)
    grad_w_out = weight_halves(
        order, halves, (act_high, act_low), (grad_high, grad_low), 1, 1024, after=(part,)
    )
    total = scatter_terms(part, (grad_w_out[0],))
    zero = token((total,))
    lat, slope1, gram_z, sum_z, term_w_dec = encode_again(
        pre_enc, vector1, lat_pair, b_lat_row, z, term_w_dec
    )
    grad_w_out = add_cores([[grad_w_out[0] + zero, *grad_w_out[1:]]], token((lat,)))
    term_mine, term_other, z_order = gather_blocks(total, (lat,))
    sums2 = gather_sums(term_mine, sums2)
    fix_z = fix_terms(cells, w_dec, vector2, sums2, b_lat_row)

    received = []
    if halves == 2:
        cuts = [0, 256, 512, counts_in.shape[0]]
        grad_w_out = [grad_w_out[0][:, a:b] for a, b in zip(cuts, cuts[1:])]
        received = [swap(piece, BATCH, 2) for piece in grad_w_out]
    steps = list(reversed(bits(GENE)))
    term_w_dec = halve_blocks(term_w_dec.reshape(ranks, share, latent), steps[0])

    pre_part = lax.dynamic_slice_in_dim(pre_enc, me * share, share, 0)
    grad_in1, sums1, grad_lat, grad_b_lat = latent_back(
        cells, z_order, term_mine, term_other, z, fix_z, b_lat_row, lat, noise, tal_pair,
        slope1, pre_enc, vector1, [*received[:1], term_w_dec, pre_part]
    )
    sums1 = add_all(
        jnp.concatenate([sums1.reshape(-1), grad_b_lat[0], grad_b_out[0]]),
        (BATCH,),
    )
    grad_b_lat = sums1[2 * hidden : 2 * hidden + 2 * latent]
    grad_b_out = sums1[2 * hidden + 2 * latent :]
    sums1 = sums1[: 2 * hidden].reshape(2, hidden)
    vector6 = jnp.concatenate([vector1, sums1])
    term_w_dec = halve_blocks(term_w_dec, steps[1])
    high, low, *weight_part = encoder_weight(
        cells, order, halves, grad_in1, pre_enc, vector6, scaled[0], [term_w_dec, *received[1:]]
    )
    for bit in steps[2:]:
        term_w_dec = halve_blocks(term_w_dec, bit)
    term_w_dec = term_w_dec[0].T
    after = ()
    if halves == 2:
        weight_part = add_cores([weight_part], 0.0)
        after = weight_part
    grad_counts = counts_back(
        cells, enc_pair, (high, low), recon, counts_in, factor, mask, after=after
    )
    zero = token((grad_counts,))
    if halves == 2:
        weight_part = [swap_chips(weight_part[0], zero)]
    else:
        weight_part = [weight_part]
    if halves == 2:
        grad_w_out = [a + b for a, b in zip(grad_w_out, received)]
    grad_w_out = join_cores(order, grad_w_out, zero).T
    grad_w_enc = join_cores(order, weight_part, 0.0).T
    grad_w_lat = latent_weight(
        grad_lat, pre_part, part_vector, (grad_counts,)
    )
    small = jnp.concatenate(
        [
            term_w_dec + zero,
            grad_w_lat,
            rows_wide(gram_z.reshape(-1), share),
            rows_wide(sum_z[0], share),
        ]
    )
    small = add_all(small, (BATCH,)) + (token(weight_part[:1]) if halves == 2 else 0.0)
    term_w_dec = small[:latent]
    grad_w_lat = small[latent : 3 * latent]
    lines = -(-latent // share)
    gram_z = small[3 * latent : -lines].reshape(-1)[: latent * latent]
    gram_z = gram_z.reshape(latent, latent)
    sum_z = small[-lines:].reshape(-1)[:latent]
    grad_shift2 = hidden_part(sums2[0])
    grad_gain2 = hidden_part(sums2[1])
    rstd2 = hidden_part(lax.rsqrt(var2 + BN_EPS))
    cov_z = gram_z - sum_z[:, None] * (sum_z / cells)[None, :]
    pair_w_dec = rstd2[None, :] * jnp.dot(
        cov_z, hidden_part(w_dec), precision=lax.Precision.HIGHEST
    )
    sum_z = sum_z + cells * b_lat[:latent]
    grad_w_dec = (hidden_part(gain_dec) * rstd2)[None, :] * (
        term_w_dec
        - sum_z[:, None] * (grad_shift2 / cells)[None, :]
        - pair_w_dec * (grad_gain2 / cells)[None, :]
    )

    correct = cells / (cells - 1.0)
    new_mean_enc = (1.0 - MOMENTUM) * mean_enc + MOMENTUM * hidden_part(mean1)
    new_var_enc = (1.0 - MOMENTUM) * var_enc + MOMENTUM * hidden_part(var1) * correct
    new_mean_dec = (1.0 - MOMENTUM) * mean_dec + MOMENTUM * mean2
    new_var_dec = (1.0 - MOMENTUM) * var_dec + MOMENTUM * var2 * correct
    return (
        recon,
        grad_counts,
        grad_w_enc,
        hidden_part(sums1[1]),
        hidden_part(sums1[0]),
        grad_w_lat,
        grad_b_lat,
        grad_w_dec,
        grad_gain2,
        grad_shift2,
        grad_w_out,
        grad_b_out,
        new_mean_enc,
        new_var_enc,
        new_mean_dec,
        new_var_dec,
    )


def solution(mesh):
    return jax.shard_map(
        on_device,
        mesh=mesh,
        in_specs=(
            P(GENE, BATCH),
            P(BATCH),
            P(GENE),
            P(None, BATCH),
            P(GENE, None),
            P(GENE),
            P(GENE),
            P(),
            P(),
            P(),
            P(),
            P(),
            P(GENE, None),
            P(GENE),
            P(GENE),
            P(GENE),
            P(),
            P(),
        ),
        out_specs=(
            P(GENE, BATCH),
            P(GENE, BATCH),
            P(GENE, None),
            P(GENE),
            P(GENE),
            P(None, GENE),
            P(),
            P(None, GENE),
            P(GENE),
            P(GENE),
            P(GENE, None),
            P(GENE),
            P(GENE),
            P(GENE),
            P(),
            P(),
        ),
        check_vma=False,
    )
```

```python
import jax
import jax.numpy as jnp
from jax import lax
from jax.experimental import pallas as pl
from jax.experimental.pallas import tpu as pltpu
from jax.sharding import PartitionSpec as P

ALPHA = 0.002
BN_EPS = 1e-05
MOMENTUM = 0.1
UMI_SCALE = 10000.0
BATCH = "batch"
GENE = "gene"
TILE = 512
HALF = 256
ROWS = 16
VMEM_BYTES = 56 << 20
F32 = jnp.float32


BF16 = jnp.bfloat16
RATE = 600_000_000


def split(value):
    high = value.astype(BF16)
    return high, (value - high.astype(F32)).astype(BF16)


def whole(pair):
    return pair[0].astype(F32) + pair[1].astype(F32)


def dot(left, right, left_dim, right_dim):
    def one(a, b):
        return lax.dot_general(
            a,
            b,
            (((left_dim,), (right_dim,)), ((), ())),
            preferred_element_type=F32,
        )

    return one(left[0], right[0]) + (one(left[0], right[1]) + one(left[1], right[0]))


def kernel_call(
    body, grid, in_specs, out_specs, out_shape, micros, order=None, scratch=(), after=(),
    onto=(),
):
    leading = 0 if order is None else 1
    held = leading + len(in_specs)

    def run(*refs):
        body(*refs[:held], *refs[held + len(after) :])

    call = pl.pallas_call(
        run,
        grid_spec=pltpu.PrefetchScalarGridSpec(
            num_scalar_prefetch=leading,
            grid=grid,
            in_specs=list(in_specs) + [pl.BlockSpec(memory_space=pl.ANY)] * len(after),
            out_specs=out_specs,
            scratch_shapes=list(scratch),
        ),
        out_shape=out_shape,
        input_output_aliases={held + k: out for k, out in enumerate(onto)},
        compiler_params=pltpu.CompilerParams(vmem_limit_bytes=VMEM_BYTES),
        cost_estimate=pl.CostEstimate(
            flops=int(micros * RATE), bytes_accessed=1024, transcendentals=0
        ),
    )
    prefetch = () if order is None else (order,)
    return lambda *args: call(*prefetch, *args, *after)


def shape(*dims, dtype=F32):
    return jax.ShapeDtypeStruct(dims, dtype)


def full(*dims):
    return pl.BlockSpec(dims, lambda *_: (0,) * len(dims))


def tile(rows):
    return pl.BlockSpec((rows, TILE), lambda j, *_: (0, j))


def pair_of(spec):
    return [spec, spec]


def sigmoid(value):
    return 0.5 * jnp.tanh(0.5 * value) + 0.5


def silu_pair(value):
    sig = sigmoid(value)
    act = value * sig
    return act, sig + act * (1.0 - sig)


def start_or_add(ref, value, first):
    @pl.when(first)
    def _():
        ref[...] = value

    @pl.when(jnp.logical_not(first))
    def _():
        ref[...] += value


def fold(value):
    width = value.shape[1]
    if width % 128:
        return jnp.broadcast_to(
            jnp.sum(value, axis=1, keepdims=True) / 128.0, (value.shape[0], 128)
        )
    return sum(
        value[:, at : at + 128] for at in range(128, width, 128)
    ) + value[:, :128] if width > 128 else value


def rows_of(*folded):
    return jnp.concatenate(
        [jnp.sum(value, axis=1, keepdims=True) for value in folded], axis=1
    ).T


def moments(pre):
    mean = jnp.mean(pre, axis=1, keepdims=True)
    cent = pre - mean
    return jnp.concatenate(
        [mean, jnp.sum(cent * cent, axis=1, keepdims=True)], axis=1
    ).T


def wide(column):
    return jnp.concatenate([column] * (TILE // 128), axis=1)


def spread(column):
    return jnp.broadcast_to(column, (column.shape[0], 128))


def split_scaled(counts, factor, mask, high, low):
    column = mask[...].T
    scale = factor[...]
    for at in range(0, counts.shape[0], ROWS):
        rows = pl.ds(at, ROWS)
        high[rows, :], low[rows, :] = split(
            counts[rows, :] * scale * column[at : at + ROWS]
        )


def gene_cuts(genes):
    return [0, genes]


def turn_kernel(counts, factor, mask, *outs):
    turned = counts[...].T * factor[...].T * mask[...]
    cuts = gene_cuts(turned.shape[1])
    for place, (begin, end) in enumerate(zip(cuts, cuts[1:])):
        outs[2 * place][...], outs[2 * place + 1][...] = split(turned[:, begin:end])


def turn_counts(counts, factor, mask, after):
    genes, here = counts.shape
    cuts = gene_cuts(genes)
    widths = [end - begin for begin, end in zip(cuts, cuts[1:]) for _ in range(2)]
    out = kernel_call(
        turn_kernel,
        (here // TILE,),
        [tile(genes), tile(1), full(1, genes)],
        [pl.BlockSpec((TILE, width), lambda j: (j, 0)) for width in widths],
        [shape(here, width, dtype=BF16) for width in widths],
        5,
        after=after,
    )(counts, factor, mask)
    return [tuple(out[2 * k : 2 * k + 2]) for k in range(len(out) // 2)]


def encode_kernel(order, counts, factor, mask, w_enc_t, *refs):
    *outs, high, low, scaled_high, scaled_low = refs
    step = pl.program_id(0)

    @pl.when(step == 0)
    def _():
        for at in range(0, high.shape[0], ROWS):
            rows = pl.ds(at, ROWS)
            high[rows, :], low[rows, :] = split(w_enc_t[rows, :])

    split_scaled(counts, factor, mask, scaled_high, scaled_low)
    product = dot(
        (high[...], low[...]), (scaled_high[...], scaled_low[...]), 1, 0
    )
    side = order[0] == 0
    for place in range(len(outs) // 3):
        other, own, both = outs[3 * place : 3 * place + 3]
        rows = other.shape[0]

        @pl.when(step == place)
        def _():
            if rows < product.shape[0]:
                both[...] = product[rows:]

        @pl.when((step == place) & side)
        def _():
            other[...] = product[:rows, HALF:]
            own[...] = product[:rows, :HALF]

        @pl.when((step == place) & jnp.logical_not(side))
        def _():
            other[...] = product[:rows, :HALF]
            own[...] = product[:rows, HALF:]


def encode_products(side, order, counts, factor, mask, w_enc_t, rest, after=()):
    genes = counts.shape[0]
    hidden = w_enc_t.shape[0]
    blocks = order.shape[0]
    cells = lambda j, order: (0, order[j + 1])
    sizes = [(hidden - rest, HALF)] * 2 + [(max(rest, 8), TILE)]
    return kernel_call(
        encode_kernel,
        (blocks,),
        [
            pl.BlockSpec((genes, TILE), cells),
            pl.BlockSpec((1, TILE), cells),
            full(1, genes),
            full(hidden, genes),
        ],
        [full(*size) for size in sizes] * blocks,
        [shape(*size) for size in sizes] * blocks,
        4 * blocks,
        order=jnp.concatenate([side[None], order]).astype(jnp.int32),
        scratch=[pltpu.VMEM((hidden, genes), BF16)] * 2
        + [pltpu.VMEM((genes, TILE), BF16)] * 2,
        after=after,
    )(counts, factor, mask, w_enc_t)


def prepare_kernel(w_out_t, w_enc_t, w_lat, w_dec, out_high, out_low, turn_high, turn_low,
                   enc_high, enc_low, lat_high, lat_low, tal_high, tal_low,
                   dec_high, dec_low):
    out_high[...], out_low[...] = split(w_out_t[...])
    turn_high[...], turn_low[...] = split(w_out_t[...].T)
    enc_high[...], enc_low[...] = split(w_enc_t[...].T)
    lat_high[...], lat_low[...] = split(w_lat[...])
    tal_high[...], tal_low[...] = split(w_lat[...].T)
    dec_high[...], dec_low[...] = split(w_dec[...].T)


def prepare(w_out_t, w_enc_t, w_lat, w_dec, after):
    hidden, genes = w_out_t.shape
    latents, latent = w_lat.shape[0], w_dec.shape[0]
    sizes = [
        (hidden, genes),
        (genes, hidden),
        (genes, hidden),
        (latents, hidden),
        (hidden, latents),
        (hidden, latent),
    ]
    out = kernel_call(
        prepare_kernel,
        (),
        pair_of(full(hidden, genes)) + [full(latents, hidden), full(latent, hidden)],
        [full(*size) for size in sizes for _ in range(2)],
        [shape(*size, dtype=BF16) for size in sizes for _ in range(2)],
        6,
        after=after,
    )(w_out_t, w_enc_t, w_lat, w_dec)
    return [tuple(out[2 * k : 2 * k + 2]) for k in range(len(sizes))]


def own_kernel(main, *refs):
    *parts, pre_out, stats = refs
    rows = parts[0].shape[0]
    pre_out[:rows] = sum(part[...] for part in parts[1:main]) + parts[0][...]
    if main < len(parts):
        pre_out[rows:] = sum(part[...] for part in parts[main:])
    stats[...] = moments(pre_out[...])


def own_moments(parts, rest, after=()):
    rows, columns = parts[0].shape
    rows += rest[0].shape[0] if rest else 0
    return kernel_call(
        lambda *refs: own_kernel(len(parts), *refs),
        (),
        [full(*part.shape) for part in (*parts, *rest)],
        [full(rows, columns), full(2, rows)],
        [shape(rows, columns), shape(2, rows)],
        3,
        after=after,
    )(*parts, *rest)


def normalize(pre, vector):
    columns = vector.T
    norm = (pre - columns[:, 0:1]) * lax.rsqrt(columns[:, 1:2] + BN_EPS)
    return norm, norm * columns[:, 2:3] + columns[:, 3:4]


def latent_kernel(pre, vector, lat_high, lat_low, b_lat, noise, z_out):
    _, value = normalize(pre[...], vector[...])
    act, _ = silu_pair(value)
    lat = dot((lat_high[...], lat_low[...]), split(act), 1, 0) + b_lat[...].T
    latent = noise.shape[0]
    z_out[...] = lat[:latent] + jnp.exp(0.5 * lat[latent:]) * noise[...]


def latent_own(pre, vector, lat_pair, b_lat, noise):
    return kernel_call(
        latent_kernel,
        (),
        [full(*a.shape) for a in (pre, vector, *lat_pair, b_lat, noise)],
        full(*noise.shape),
        shape(*noise.shape),
        3,
    )(pre, vector, *lat_pair, b_lat, noise)


def sides(order, mine, other):
    left = order[0] == 0
    return jnp.concatenate(
        [jnp.where(left, mine, other), jnp.where(left, other, mine)], axis=1
    )


def hidden_kernel(order, dec_high, dec_low, mine, other, z_all, pre_out, stats,
                  sums):
    for step in range(mine.shape[0]):
        spot = order[step + 1]
        z = sides(order, mine[spot], other[spot])
        columns = pl.ds(step * TILE, TILE)
        z_all[:, columns] = z
        pre = dot((dec_high[...], dec_low[...]), split(z), 1, 0)
        pre_out[:, columns] = pre
        if step == 0:
            sums[...] = fold(pre)
        else:
            sums[...] += fold(pre)
    hidden, here = pre_out.shape
    mean = jnp.sum(sums[...], axis=1, keepdims=True) * (1.0 / here)
    sums[...] = spread(mean)
    squares = []
    for at in range(0, hidden, ROWS):
        rows = pl.ds(at, ROWS)
        total = jnp.zeros((ROWS, 128), F32)
        for step in range(mine.shape[0]):
            cent = pre_out[rows, pl.ds(step * TILE, TILE)] - wide(sums[rows, :])
            total = total + fold(cent * cent)
        squares.append(total)
    square = jnp.sum(jnp.concatenate(squares, axis=0), axis=1, keepdims=True)
    stats[...] = jnp.concatenate([mean, square], axis=1).T


def decoder_hidden(order, dec_pair, mine, other, after):
    hidden, latent = dec_pair[0].shape
    cells = 2 * mine.shape[0] * HALF
    return kernel_call(
        hidden_kernel,
        (1,),
        pair_of(full(hidden, latent)) + [full(*mine.shape), full(*other.shape)],
        [full(latent, cells), full(hidden, cells), full(2, hidden)],
        [shape(latent, cells), shape(hidden, cells), shape(2, hidden)],
        8,
        order=order,
        scratch=[pltpu.VMEM((hidden, 128), F32)],
        after=after,
    )(*dec_pair, mine, other)


def decoder_kernel(cells, order, pre, vector, z, out_high, out_low, turn_high, turn_low,
                   counts, factor, mask, b_out, w_dec,
                   recon_out, grad_high, grad_low, act_high, act_low, z_other, z_own,
                   weight_out, sums, bias_out,
                   sum_term, sum_gain, sum_grad, mean_w, scale_w, shift_w, mask_w, bias_w,
                   dec_high, dec_low, slope, product, term_high, term_low):
    step = pl.program_id(0)
    hidden, genes = out_high.shape

    @pl.when(step == 0)
    def _():
        columns = vector[...].T
        rstd = lax.rsqrt(columns[:, 1:2] + BN_EPS)
        mean_w[...] = spread(columns[:, 0:1])
        scale_w[...] = spread(rstd * columns[:, 2:3])
        shift_w[...] = spread(columns[:, 3:4])
        mask_w[...] = spread(mask[...].T * (1.0 / cells))
        bias_w[...] = spread(b_out[...].T)
        dec_high[...], dec_low[...] = split(
            w_dec[...] * (vector[2:3, :] * lax.rsqrt(vector[1:2, :] + BN_EPS))
        )
        for ref in (sum_term, sum_gain, sum_grad, weight_out):
            ref[...] = jnp.zeros_like(ref)

    for at in range(0, hidden, ROWS):
        rows = pl.ds(at, ROWS)
        cent = pre[rows, :] - wide(mean_w[rows, :])
        act, slope[rows, :] = silu_pair(
            cent * wide(scale_w[rows, :]) + wide(shift_w[rows, :])
        )
        act_high[rows, :], act_low[rows, :] = split(act)
    product[:genes, :] = dot(
        (turn_high[...], turn_low[...]), (act_high[...], act_low[...]), 1, 0
    )
    scale = factor[...]
    for at in range(0, genes, ROWS):
        rows = pl.ds(at, ROWS)
        out = product[rows, :] + wide(bias_w[rows, :])
        recon = jnp.maximum(out, 0.0) + jnp.log(1.0 + jnp.exp(-jnp.abs(out)))
        recon_out[rows, :] = recon
        grad = (recon - counts[rows, :] * scale) * (wide(mask_w[rows, :]) * sigmoid(out))
        sum_grad[rows, :] += fold(grad)
        grad_high[rows, :], grad_low[rows, :] = split(grad)
    product[:hidden, :] = dot(
        (out_high[...], out_low[...]), (grad_high[...], grad_low[...]), 1, 0
    )
    for at in range(0, hidden, ROWS):
        rows = pl.ds(at, ROWS)
        term = product[rows, :] * slope[rows, :]
        cent = pre[rows, :] - wide(mean_w[rows, :])
        sum_term[rows, :] += fold(term)
        sum_gain[rows, :] += fold(term * cent)
        term_high[rows, :], term_low[rows, :] = split(term)
    terms = term_high[...], term_low[...]
    back = dot((dec_high[...], dec_low[...]), terms, 1, 0)
    left = order[0] == 0
    z_other[...] = jnp.where(left, back[:, HALF:], back[:, :HALF])
    z_own[...] = jnp.where(left, back[:, :HALF], back[:, HALF:])
    weight_out[...] += dot(terms, split(z[...]), 1, 1)

    @pl.when(step == pl.num_programs(0) - 1)
    def _():
        rstd = lax.rsqrt(vector[1:2, :] + BN_EPS)
        both = rows_of(sum_term[...], sum_gain[...])
        sums[...] = jnp.concatenate([both[0:1], both[1:2] * rstd], axis=0)
        bias_out[...] = rows_of(sum_grad[...])


def decoder(cells, order, pre, vector, z, out_pair, turn_pair, counts, factor, mask, b_out,
            w_dec):
    hidden, genes = out_pair[0].shape
    here = counts.shape[1]
    latent = w_dec.shape[0]
    most = max(hidden, genes)
    placed = pl.BlockSpec((latent, HALF), lambda j, order: (0, order[j + 1]))
    return kernel_call(
        lambda *refs: decoder_kernel(cells, *refs),
        (here // TILE,),
        [tile(hidden), full(4, hidden), tile(latent)]
        + pair_of(full(hidden, genes))
        + pair_of(full(genes, hidden))
        + [
            tile(genes),
            tile(1),
            full(1, genes),
            full(1, genes),
            full(latent, hidden),
        ],
        [tile(genes)]
        + pair_of(tile(genes))
        + pair_of(tile(hidden))
        + pair_of(placed)
        + [full(hidden, latent), full(2, hidden), full(1, genes)],
        [shape(genes, here)]
        + [shape(genes, here, dtype=BF16)] * 2
        + [shape(hidden, here, dtype=BF16)] * 2
        + [shape(latent, here // 2)] * 2
        + [shape(hidden, latent), shape(2, hidden), shape(1, genes)],
        42,
        order=order,
        scratch=[pltpu.VMEM((hidden, 128), F32)] * 2
        + [pltpu.VMEM((genes, 128), F32)]
        + [pltpu.VMEM((hidden, 128), F32)] * 3
        + [pltpu.VMEM((genes, 128), F32)] * 2
        + [pltpu.VMEM((latent, hidden), BF16)] * 2
        + [pltpu.VMEM((hidden, TILE), F32), pltpu.VMEM((most, TILE), F32)]
        + [pltpu.VMEM((hidden, TILE), BF16)] * 2,
    )(pre, vector, z, *out_pair, *turn_pair, counts, factor, mask, b_out, w_dec)


def start_halves(order, product, outs, first):
    if len(outs) == 1:
        start_or_add(outs[0], product, first)
        return
    rows = product.shape[0] // 2
    upper = order[0] != 0

    @pl.when(upper)
    def _():
        start_or_add(outs[0], product[rows:], first)
        start_or_add(outs[1], product[:rows], first)

    @pl.when(jnp.logical_not(upper))
    def _():
        start_or_add(outs[0], product[:rows], first)
        start_or_add(outs[1], product[rows:], first)


def weight_kernel(right_dim, order, left_high, left_low, right_high, right_low, *outs):
    product = dot(
        (left_high[...], left_low[...]), (right_high[...], right_low[...]), 1, right_dim
    )
    start_halves(order, product, outs, pl.program_id(0) == 0)


def weight_halves(order, halves, left, right, right_dim, width, after=()):
    hidden, here = left[0].shape
    rows = hidden // halves
    genes = right[0].shape[1 - right_dim]
    if right_dim:
        cells = pl.BlockSpec((genes, width), lambda j, order: (0, j))
    else:
        cells = pl.BlockSpec((width, genes), lambda j, order: (j, 0))
    return kernel_call(
        lambda *refs: weight_kernel(right_dim, *refs),
        (here // width,),
        pair_of(pl.BlockSpec((hidden, width), lambda j, order: (0, j))) + pair_of(cells),
        [full(rows, genes)] * halves,
        [shape(rows, genes)] * halves,
        10,
        order=order,
        after=after,
    )(*left, *right)


def latent_weight_kernel(lat, part, vector, out):
    _, value = normalize(part[...], vector[...])
    act, _ = silu_pair(value)
    product = dot(split(lat[...]), split(act), 1, 1)
    start_or_add(out, product, pl.program_id(0) == 0)


def latent_weight(lat, part, vector, after):
    latents, here = lat.shape
    share = part.shape[0]
    return kernel_call(
        latent_weight_kernel,
        (here // 1024,),
        [
            pl.BlockSpec((latents, 1024), lambda j: (0, j)),
            pl.BlockSpec((share, 1024), lambda j: (0, j)),
            full(4, share),
        ],
        full(latents, share),
        shape(latents, share),
        4,
        after=after,
    )(lat, part, vector)


def again_kernel(pre_enc, vector, lat_high, lat_low, b_lat, z, later,
                 lat_out, slope_out, gram, sum_out, later_out, act_high, act_low):
    later_out[...] = later[...]
    first = pl.program_id(0) == 0
    moved = z[...] - b_lat[:, : z.shape[0]].T
    pair = split(moved)
    start_or_add(gram, dot(pair, pair, 1, 1), first)
    start_or_add(sum_out, rows_of(moved), first)
    columns = vector[...].T
    scale = lax.rsqrt(columns[:, 1:2] + BN_EPS) * columns[:, 2:3]
    for at in range(0, pre_enc.shape[0], ROWS):
        rows = pl.ds(at, ROWS)
        part = slice(at, at + ROWS)
        act, slope_out[rows, :] = silu_pair(
            (pre_enc[rows, :] - columns[part, 0:1]) * scale[part] + columns[part, 3:4]
        )
        act_high[rows, :], act_low[rows, :] = split(act)
    lat_out[...] = (
        dot((lat_high[...], lat_low[...]), (act_high[...], act_low[...]), 1, 0)
        + b_lat[...].T
    )


def encode_again(pre_enc, vector, lat_pair, b_lat, z, later, after=()):
    latent = z.shape[0]
    hidden, here = pre_enc.shape
    latents = lat_pair[0].shape[0]
    return kernel_call(
        again_kernel,
        (here // TILE,),
        [tile(hidden), full(4, hidden)]
        + pair_of(full(latents, hidden))
        + [full(1, latents), tile(latent), full(*later.shape)],
        [
            tile(latents),
            tile(hidden),
            full(latent, latent),
            full(1, latent),
            full(*later.shape),
        ],
        [
            shape(latents, here),
            shape(hidden, here),
            shape(latent, latent),
            shape(1, latent),
            shape(*later.shape),
        ],
        10,
        scratch=[pltpu.VMEM((hidden, TILE), BF16)] * 2,
        after=after,
    )(pre_enc, vector, *lat_pair, b_lat, z, later)


def fix_kernel(cells, w_dec, vector, sums, b_lat, matrix_out, column_out):
    weight = w_dec[...]
    rstd = lax.rsqrt(vector[1:2, :] + BN_EPS)
    scaled = weight * (vector[2:3, :] * rstd * (1.0 / cells))
    gained = scaled * (sums[1:2, :] * rstd)
    matrix_out[...] = dot(split(gained), split(weight), 1, 1)
    bias = b_lat[:, : weight.shape[0]].T
    mean = vector[0:1, :] - jnp.sum(weight * bias, axis=0, keepdims=True)
    column_out[...] = spread(
        jnp.sum(scaled * sums[0:1, :] - gained * mean, axis=1, keepdims=True)
    )


def fix_terms(cells, w_dec, vector, sums, b_lat):
    latent, hidden = w_dec.shape
    return kernel_call(
        lambda *refs: fix_kernel(cells, *refs),
        (),
        [full(latent, hidden), full(4, hidden), full(2, hidden), full(*b_lat.shape)],
        [full(latent, latent), full(latent, 128)],
        [shape(latent, latent), shape(latent, 128)],
        2,
    )(w_dec, vector, sums, b_lat)


def latent_back_kernel(cells, order, mine, other, z, matrix, column, b_lat, lat, noise,
                       tal_high, tal_low, slope, pre, vector, grad_out, sums, lat_out, bias_out,
                       sum_grad, sum_gain, sum_lat, product):
    step = pl.program_id(0)

    @pl.when(step == 0)
    def _():
        for ref in (sum_grad, sum_gain, sum_lat):
            ref[...] = jnp.zeros_like(ref)

    latent = noise.shape[0]
    moved = z[...] - b_lat[:, :latent].T
    fix = dot(split(matrix[...]), split(moved), 1, 0) + wide(column[...])
    grad_z = sides(order, mine[:latent, :], other[:latent, :]) - fix
    mu = lat[:latent, :]
    spread_z = jnp.exp(0.5 * lat[latent:, :])
    grad_mu = grad_z + (ALPHA / cells) * mu
    grad_logvar = 0.5 * grad_z * noise[...] * spread_z + (0.5 * ALPHA / cells) * (
        spread_z * spread_z - 1.0
    )
    grad_lat = jnp.concatenate([grad_mu, grad_logvar], axis=0)
    lat_out[...] = grad_lat
    sum_lat[...] += fold(grad_lat)
    product[...] = dot((tal_high[...], tal_low[...]), split(grad_lat), 1, 0)
    mean = vector[0:1, :].T
    for at in range(0, product.shape[0], ROWS):
        rows = pl.ds(at, ROWS)
        grad = product[rows, :] * slope[rows, :]
        grad_out[rows, :] = grad
        sum_grad[rows, :] += fold(grad)
        sum_gain[rows, :] += fold(grad * (pre[rows, :] - mean[at : at + ROWS]))

    @pl.when(step == pl.num_programs(0) - 1)
    def _():
        both = rows_of(sum_grad[...], sum_gain[...])
        sums[...] = jnp.concatenate(
            [both[0:1], both[1:2] * lax.rsqrt(vector[1:2, :] + BN_EPS)], axis=0
        )
        bias_out[...] = rows_of(sum_lat[...])


def latent_back(cells, order, mine, other, z, fix, b_lat, lat, noise, tal_pair, slope, pre,
                vector, after=()):
    hidden, here = pre.shape
    latents = lat.shape[0]
    latent = noise.shape[0]
    block = pl.BlockSpec(
        (None, mine.shape[1], HALF), lambda j, order: (order[j + 1], 0, 0)
    )
    return kernel_call(
        lambda *refs: latent_back_kernel(cells, *refs),
        (here // TILE,),
        [block, block, tile(latent), full(latent, latent), full(latent, 128)]
        + [full(1, latents), tile(latents), tile(latent)]
        + pair_of(full(hidden, latents))
        + [tile(hidden), tile(hidden), full(4, hidden)],
        [tile(hidden), full(2, hidden), tile(latents), full(1, latents)],
        [
            shape(hidden, here),
            shape(2, hidden),
            shape(latents, here),
            shape(1, latents),
        ],
        12,
        order=order,
        scratch=[
            pltpu.VMEM((hidden, 128), F32),
            pltpu.VMEM((hidden, 128), F32),
            pltpu.VMEM((latents, 128), F32),
            pltpu.VMEM((hidden, TILE), F32),
        ],
        after=after,
    )(mine, other, z, *fix, b_lat, lat, noise, *tal_pair, slope, pre, vector)


def encoder_weight_kernel(cells, order, grad_in, pre, vector, scaled_high, scaled_low,
                          high, low, *outs):
    columns = vector[...].T
    scale = lax.rsqrt(columns[:, 1:2] + BN_EPS)
    outer = columns[:, 2:3] * scale
    shift = columns[:, 4:5] * (1.0 / cells)
    gain = columns[:, 5:6] * (1.0 / cells) * scale
    for at in range(0, grad_in.shape[0], ROWS):
        rows = pl.ds(at, ROWS)
        part = slice(at, at + ROWS)
        grad = outer[part] * (
            grad_in[rows, :]
            - shift[part]
            - (pre[rows, :] - columns[part, 0:1]) * gain[part]
        )
        high[rows, :], low[rows, :] = split(grad)
    product = dot((high[...], low[...]), (scaled_high[...], scaled_low[...]), 1, 0)
    start_halves(order, product, outs, pl.program_id(0) == 0)


def encoder_weight(cells, order, halves, grad_in, pre, vector, scaled, after):
    hidden, here = pre.shape
    genes = scaled[0].shape[1]
    rows = hidden // halves
    return kernel_call(
        lambda *refs: encoder_weight_kernel(cells, *refs),
        (here // TILE,),
        [tile(hidden), tile(hidden), full(6, hidden)]
        + pair_of(pl.BlockSpec((TILE, genes), lambda j, order: (j, 0))),
        pair_of(tile(hidden)) + [full(rows, genes)] * halves,
        [shape(hidden, here, dtype=BF16)] * 2 + [shape(rows, genes)] * halves,
        12,
        order=order,
        after=after,
    )(grad_in, pre, vector, *scaled)


def counts_kernel(cells, enc_high, enc_low, high, low, recon, counts, factor, mask, out,
                  product):
    product[...] = dot((enc_high[...], enc_low[...]), (high[...], low[...]), 1, 0)
    mask_column = mask[...].T
    scale = factor[...]
    for at in range(0, out.shape[0], ROWS):
        rows = pl.ds(at, ROWS)
        column = mask_column[at : at + ROWS]
        diff = (recon[rows, :] - counts[rows, :] * scale) * (column * (1.0 / cells))
        out[rows, :] = (product[rows, :] - diff) * (scale * column)


def counts_back(cells, enc_pair, grads, recon, counts, factor, mask, after=()):
    genes, hidden = enc_pair[0].shape
    here = counts.shape[1]
    return kernel_call(
        lambda *refs: counts_kernel(cells, *refs),
        (here // TILE,),
        pair_of(full(genes, hidden))
        + pair_of(tile(hidden))
        + [tile(genes), tile(genes), tile(1), full(1, genes)],
        tile(genes),
        shape(genes, here),
        16,
        scratch=[pltpu.VMEM((genes, TILE), F32)],
        after=after,
    )(*enc_pair, *grads, recon, counts, factor, mask)


def token_kernel(out):
    out[...] = jnp.zeros_like(out)


def token(after):
    return kernel_call(
        token_kernel, (), [], full(1, 1), shape(1, 1), 0, after=after
    )()[0, 0]


def swap(value, axis, bit):
    size = lax.axis_size(axis)
    return lax.ppermute(value, axis, [(i, i ^ bit) for i in range(size)])


def bits(axis):
    size, bit, out = lax.axis_size(axis), 1, []
    while bit < size:
        out.append(bit)
        bit *= 2
    return out


def add_all(value, axes):
    for axis in axes:
        for bit in bits(axis):
            value = value + swap(value, axis, bit)
    return value


def moments_all(both, count, axes, others=None):
    for axis in axes:
        if axis == GENE and others is not None:
            both = jnp.concatenate([both, others])
        for bit in bits(axis):
            other = swap(both, axis, bit)
            gap = both[0] - other[0]
            rows = [
                0.5 * (both[0] + other[0]),
                both[1] + other[1] + gap * gap * (0.5 * count),
            ]
            both = jnp.concatenate([jnp.stack(rows), both[2:] + other[2:]])
            count = 2 * count
    return both[0], both[1] / count, both[2:]


def rows_wide(vector, share):
    size = vector.shape[0]
    lines = -(-size // share)
    return jnp.pad(vector, (0, lines * share - size)).reshape(lines, share)


def halve_blocks(value, bit):
    half = value.shape[0] // 2
    upper = (lax.axis_index(GENE) & bit) != 0
    sent = jnp.where(upper, value[:half], value[half:])
    kept = jnp.where(upper, value[half:], value[:half])
    return kept + swap(sent, GENE, bit)


def gene_pairs(links):
    return [(2 * a + y, 2 * b + y) for a, b in links for y in (0, 1)]


OUTER = gene_pairs([(0, 1), (3, 2)])
MIDDLE = gene_pairs([(1, 2), (2, 1)])
SIDES = gene_pairs([(0, 1), (1, 0), (2, 3), (3, 2)])


def line_order(z):
    low = z < 2
    return [
        jnp.where(low, z + 3, z + 1) % 4,
        (z + 2) % 4,
        jnp.where(low, z + 1, z + 3) % 4,
        z,
    ]


def by_line(here):
    return lax.axis_size(GENE) == 8 and here == 8 * HALF


def scatter_encoded(counts, factor, mask, w_enc_t, others):
    here = counts.shape[1]
    hidden = w_enc_t.shape[0]
    me = lax.axis_index(GENE)
    if not by_line(here):
        side = 0 * me
        order = jnp.arange(here // TILE, dtype=jnp.int32)
        blocks = encode_products(side, order, counts, factor, mask, w_enc_t, 0)
        pre = [blocks[3 * k + i] for k in range(len(blocks) // 3) for i in (1, 0)]
        pre = lax.psum_scatter(
            jnp.concatenate(pre, axis=1), GENE, scatter_dimension=1, tiled=True
        )
        scaled = turn_counts(counts, factor, mask, (blocks[0],))
        return [pre], [], scaled, prepare(*others, scaled[0])
    z, y = me // 2, me % 2
    rest = hidden // 6 // 16 * 16
    order = jnp.stack(line_order(z)).astype(jnp.int32)

    def products(first, last, after=()):
        return encode_products(
            y, order[first:last], counts, factor, mask, w_enc_t, rest, after
        )

    middle = (z == 1) | (z == 2)
    blocks = products(0, 1)
    step1 = lax.ppermute(blocks[2], GENE, OUTER)
    blocks += products(1, 2, (step1,))
    blocks += products(2, 3, blocks[3:4])
    blocks += products(3, 4, blocks[6:7])
    part = [blocks[3 * k + 1] + swap(blocks[3 * k], GENE, 1) for k in range(4)]
    tail = blocks[2::3]
    step2 = lax.ppermute(tail[1], GENE, OUTER)
    across = lax.ppermute(tail[1] + step1, GENE, MIDDLE)
    scaled = turn_counts(counts, factor, mask, (step2, across, blocks[6]))
    side = lax.ppermute(jnp.where(middle, tail[0] + across, tail[2]), GENE, SIDES)
    inner = lax.ppermute(tail[2] + step2, GENE, MIDDLE)
    weights = prepare(*others, (side, inner, scaled[0][0]))
    tail = tail[3] + side + inner
    left, right = tail[:, :HALF], tail[:, HALF:]
    mine = jnp.where(y == 0, left, right)
    step1 = lax.ppermute(part[0], GENE, OUTER)
    step2 = lax.ppermute(part[1], GENE, OUTER)
    across = lax.ppermute(part[1] + step1, GENE, MIDDLE)
    side = lax.ppermute(jnp.where(middle, part[0] + across, part[2]), GENE, SIDES)
    inner = lax.ppermute(part[2] + step2, GENE, MIDDLE)
    back = swap(jnp.where(y == 0, right, left), GENE, 1)
    return [part[3], side, inner], [mine, back], scaled, weights


def gather_blocks(value, before=None):
    rows, own = value.shape
    if not by_line(own * lax.axis_size(GENE)):
        value = lax.all_gather(value, GENE, axis=1, tiled=True)
        blocks = value.shape[1] // TILE
        stack = jnp.moveaxis(value.reshape(rows, blocks, 2, HALF), 0, 2)
        order = jnp.concatenate([jnp.zeros(1), jnp.arange(blocks)])
        return stack[:, 0], stack[:, 1], order.astype(jnp.int32)
    me = lax.axis_index(GENE)
    mine = jnp.stack([value] + [swap(value, GENE, bit) for bit in (2, 4, 6)])
    if before is not None:
        mine = mine + token(before)
    other = swap(mine, GENE, 1)
    order = jnp.concatenate([(me % 2)[None], (me // 2) ^ jnp.arange(4)])
    return mine, other, order.astype(jnp.int32)


def term_order(here):
    blocks = jnp.arange(here // TILE)
    if not by_line(here):
        return jnp.concatenate([jnp.zeros(1), blocks]).astype(jnp.int32)
    me = lax.axis_index(GENE)
    return jnp.concatenate([(me % 2)[None], ((me // 2 ^ blocks) + 3) % 4]).astype(
        jnp.int32
    )


def scatter_sides(other, own, sums):
    rows, half = own.shape
    if not by_line(2 * half):
        value = jnp.stack(
            [own.reshape(rows, -1, HALF), other.reshape(rows, -1, HALF)], axis=2
        ).reshape(rows, 2 * half)
        return value, add_all(sums, (BATCH, GENE))
    z = lax.axis_index(GENE) // 2
    sums = add_all(sums, (BATCH,))
    sums = sums + swap(sums, GENE, 1)
    quarter = sums.shape[1] // 4
    quarters = [
        jnp.pad(
            lax.dynamic_slice_in_dim(sums, (z ^ k) * quarter, quarter, 1),
            ((0, 0), (0, HALF - quarter)),
        )
        for k in (1, 2, 3, 0)
    ]
    return jnp.concatenate(
        [own + swap(other, GENE, 1), jnp.concatenate(quarters, axis=1)], axis=0
    ), sums


def scatter_terms(part, before):
    if not by_line(2 * part.shape[1]):
        return lax.psum_scatter(part, GENE, scatter_dimension=1, tiled=True)
    total = part[:, 3 * HALF :] + token(before)
    for k in (1, 2, 3):
        total = total + swap(part[:, (k - 1) * HALF : k * HALF], GENE, 2 * k)
    return total


def gather_sums(stack, sums):
    if stack.shape[0] != 4 or not by_line(8 * stack.shape[2]):
        return sums
    z = lax.axis_index(GENE) // 2
    quarter = sums.shape[1] // 4
    quarters = stack[:, -sums.shape[0] :, :quarter]
    return jnp.concatenate(
        [
            lax.dynamic_index_in_dim(quarters, z ^ place, 0, keepdims=False)
            for place in range(4)
        ],
        axis=1,
    )


def add_cores(chunks, zero):
    if len(chunks[0]) == 1:
        return chunks
    return [own + swap(other, BATCH, 1) + zero for other, own in chunks]


def swap_chips(part, zero=0.0):
    if lax.axis_size(BATCH) != 4:
        return part
    return part + swap(part, BATCH, 2) + zero


def join_cores(order, chunks, zero):
    if lax.axis_size(BATCH) != 4:
        return lax.psum(jnp.concatenate([chunk[0] for chunk in chunks], axis=1), BATCH)
    low = order[0] != 0
    other = [swap(part + zero, BATCH, 1) for part in chunks]
    return jnp.concatenate(
        [
            jnp.concatenate([jnp.where(low, a, b), jnp.where(low, b, a)], axis=0)
            for a, b in zip(chunks, other)
        ],
        axis=1,
    )


def on_device(
    counts_in,
    umi_total,
    gene_mask,
    noise,
    w_enc,
    gain_enc,
    shift_enc,
    w_lat,
    b_lat,
    w_dec,
    gain_dec,
    shift_dec,
    w_out,
    b_out,
    mean_enc,
    var_enc,
    mean_dec,
    var_dec,
):
    here = counts_in.shape[1]
    cells = here * lax.axis_size(BATCH)
    hidden = w_enc.shape[1]
    ranks = lax.axis_size(GENE)
    share = hidden // ranks
    own = here // ranks
    latent = noise.shape[0]
    me = lax.axis_index(GENE)
    both = (BATCH, GENE)
    core = lax.axis_index(BATCH) % 2
    halves = 2 if lax.axis_size(BATCH) == 4 else 1
    order = (1 - core).astype(jnp.int32)[None]

    def hidden_part(vector):
        return lax.dynamic_slice_in_dim(vector, me * share, share, vector.ndim - 1)

    def hidden_placed(part):
        empty = jnp.zeros((part.shape[0], hidden), F32)
        return lax.dynamic_update_slice_in_dim(empty, part, me * share, 1)

    factor = (UMI_SCALE / umi_total.astype(F32))[None, :]
    mask = gene_mask.astype(F32)[None, :]
    w_enc_t = w_enc.T
    w_out_t = w_out.T
    b_lat_row = b_lat[None, :]
    noise_own = lax.dynamic_slice_in_dim(noise, me * own, own, 1)

    parts, rest, scaled, weights = scatter_encoded(
        counts_in, factor, mask, w_enc_t, (w_out_t, w_enc_t, w_lat, w_dec)
    )
    out_pair, turn_pair, enc_pair, lat_pair, tal_pair, dec_pair = weights
    affine1 = hidden_placed(jnp.stack([gain_enc, shift_enc]))
    pre_own, stats1 = own_moments(
        parts, rest, after=(affine1, noise_own, out_pair[0])
    )
    mean1, var1, affine1 = moments_all(stats1, own, both, affine1)
    vector1 = jnp.concatenate([mean1[None], var1[None], affine1])
    part_vector = hidden_part(vector1)
    z_own = latent_own(pre_own, vector1, lat_pair, b_lat_row, noise_own)

    z_mine, z_other, z_order = gather_blocks(z_own)
    zero = token((z_own,))
    pre_enc = lax.all_gather(pre_own + zero, GENE, axis=1, tiled=True)
    z, pre_dec, stats2 = decoder_hidden(
        z_order, dec_pair, z_mine, z_other, (part_vector,)
    )
    mean2, var2, _ = moments_all(stats2, here, (BATCH,))
    vector2 = jnp.stack([mean2, var2, gain_dec, shift_dec])
    recon, grad_high, grad_low, act_high, act_low, *terms, term_w_dec, sums2, grad_b_out = (
        decoder(
            cells, term_order(here), pre_dec, vector2, z, out_pair, turn_pair, counts_in,
            factor, mask, b_out[None, :], w_dec
        )
    )

    part, sums2 = scatter_sides(*terms, sums2)
    grad_w_out = weight_halves(
        order, halves, (act_high, act_low), (grad_high, grad_low), 1, 1024, after=(part,)
    )
    total = scatter_terms(part, (grad_w_out[0],))
    zero = token((total,))
    lat, slope1, gram_z, sum_z, term_w_dec = encode_again(
        pre_enc, vector1, lat_pair, b_lat_row, z, term_w_dec
    )
    grad_w_out = add_cores([[grad_w_out[0] + zero, *grad_w_out[1:]]], token((lat,)))
    term_mine, term_other, z_order = gather_blocks(total, (lat,))
    sums2 = gather_sums(term_mine, sums2)
    fix_z = fix_terms(cells, w_dec, vector2, sums2, b_lat_row)

    received = []
    if halves == 2:
        cuts = [0, 256, 512, counts_in.shape[0]]
        grad_w_out = [grad_w_out[0][:, a:b] for a, b in zip(cuts, cuts[1:])]
        received = [swap(piece, BATCH, 2) for piece in grad_w_out]
    steps = list(reversed(bits(GENE)))
    term_w_dec = halve_blocks(term_w_dec.reshape(ranks, share, latent), steps[0])

    pre_part = lax.dynamic_slice_in_dim(pre_enc, me * share, share, 0)
    grad_in1, sums1, grad_lat, grad_b_lat = latent_back(
        cells, z_order, term_mine, term_other, z, fix_z, b_lat_row, lat, noise, tal_pair,
        slope1, pre_enc, vector1, [*received[:1], term_w_dec, pre_part]
    )
    sums1 = add_all(
        jnp.concatenate([sums1.reshape(-1), grad_b_lat[0], grad_b_out[0]]),
        (BATCH,),
    )
    grad_b_lat = sums1[2 * hidden : 2 * hidden + 2 * latent]
    grad_b_out = sums1[2 * hidden + 2 * latent :]
    sums1 = sums1[: 2 * hidden].reshape(2, hidden)
    vector6 = jnp.concatenate([vector1, sums1])
    term_w_dec = halve_blocks(term_w_dec, steps[1])
    high, low, *weight_part = encoder_weight(
        cells, order, halves, grad_in1, pre_enc, vector6, scaled[0], [term_w_dec, *received[1:]]
    )
    for bit in steps[2:]:
        term_w_dec = halve_blocks(term_w_dec, bit)
    term_w_dec = term_w_dec[0].T
    after = ()
    if halves == 2:
        weight_part = add_cores([weight_part], 0.0)
        after = weight_part
    grad_counts = counts_back(
        cells, enc_pair, (high, low), recon, counts_in, factor, mask, after=after
    )
    zero = token((grad_counts,))
    if halves == 2:
        weight_part = [swap_chips(weight_part[0], zero)]
    else:
        weight_part = [weight_part]
    if halves == 2:
        grad_w_out = [a + b for a, b in zip(grad_w_out, received)]
    grad_w_out = join_cores(order, grad_w_out, zero).T
    grad_w_enc = join_cores(order, weight_part, 0.0).T
    grad_w_lat = latent_weight(
        grad_lat, pre_part, part_vector, (grad_counts,)
    )
    small = jnp.concatenate(
        [
            term_w_dec + zero,
            grad_w_lat,
            rows_wide(gram_z.reshape(-1), share),
            rows_wide(sum_z[0], share),
        ]
    )
    small = add_all(small, (BATCH,))
    term_w_dec = small[:latent]
    grad_w_lat = small[latent : 3 * latent]
    lines = -(-latent // share)
    gram_z = small[3 * latent : -lines].reshape(-1)[: latent * latent]
    gram_z = gram_z.reshape(latent, latent)
    sum_z = small[-lines:].reshape(-1)[:latent]
    grad_shift2 = hidden_part(sums2[0])
    grad_gain2 = hidden_part(sums2[1])
    rstd2 = hidden_part(lax.rsqrt(var2 + BN_EPS))
    cov_z = gram_z - sum_z[:, None] * (sum_z / cells)[None, :]
    pair_w_dec = rstd2[None, :] * jnp.dot(
        cov_z, hidden_part(w_dec), precision=lax.Precision.HIGHEST
    )
    sum_z = sum_z + cells * b_lat[:latent]
    grad_w_dec = (hidden_part(gain_dec) * rstd2)[None, :] * (
        term_w_dec
        - sum_z[:, None] * (grad_shift2 / cells)[None, :]
        - pair_w_dec * (grad_gain2 / cells)[None, :]
    )

    correct = cells / (cells - 1.0)
    new_mean_enc = (1.0 - MOMENTUM) * mean_enc + MOMENTUM * hidden_part(mean1)
    new_var_enc = (1.0 - MOMENTUM) * var_enc + MOMENTUM * hidden_part(var1) * correct
    new_mean_dec = (1.0 - MOMENTUM) * mean_dec + MOMENTUM * mean2
    new_var_dec = (1.0 - MOMENTUM) * var_dec + MOMENTUM * var2 * correct
    return (
        recon,
        grad_counts,
        grad_w_enc,
        hidden_part(sums1[1]),
        hidden_part(sums1[0]),
        grad_w_lat,
        grad_b_lat,
        grad_w_dec,
        grad_gain2,
        grad_shift2,
        grad_w_out,
        grad_b_out,
        new_mean_enc,
        new_var_enc,
        new_mean_dec,
        new_var_dec,
    )


def solution(mesh):
    return jax.shard_map(
        on_device,
        mesh=mesh,
        in_specs=(
            P(GENE, BATCH),
            P(BATCH),
            P(GENE),
            P(None, BATCH),
            P(GENE, None),
            P(GENE),
            P(GENE),
            P(),
            P(),
            P(),
            P(),
            P(),
            P(GENE, None),
            P(GENE),
            P(GENE),
            P(GENE),
            P(),
            P(),
        ),
        out_specs=(
            P(GENE, BATCH),
            P(GENE, BATCH),
            P(GENE, None),
            P(GENE),
            P(GENE),
            P(None, GENE),
            P(),
            P(None, GENE),
            P(GENE),
            P(GENE),
            P(GENE, None),
            P(GENE),
            P(GENE),
            P(GENE),
            P(),
            P(),
        ),
        check_vma=False,
    )
```
